256 devices in a mesh: cuts: 16 (over z, core), row: 16 (over y, x).
Axes of the slice: x: 4, y: 4, z: 8, core: 2. Of those that a mesh axis runs over, the one named last changes fastest.
Arguments:
- diagonal_blocks: bfloat16 [32, 2, 1024, 1024], P('cuts', None, 'row'), as said below
- diagonal_inverses: bfloat16 [32, 2, 1024, 1024], P('cuts', None, 'row'), as said below
- lower_blocks: bfloat16 [32, 2, 1024, 1024], P('cuts', None, 'row'), may hold values from -0.140625 to 0.140625
- upper_blocks: bfloat16 [32, 2, 1024, 1024], P('cuts', None, 'row'), may hold values from -0.140625 to 0.140625
- injection: bfloat16 [32, 2, 1024, 128], P('cuts', None, 'row'), may hold values from -6 to 6
- orbitals: int32 [32], replicated, may hold values from 512 to 1024, as said below
Outputs:
- reduced_diagonal: bfloat16 [16, 2, 1024, 1024], P('cuts', None, 'row')
- reduced_lower: bfloat16 [16, 2, 1024, 1024], P('cuts', None, 'row')
- reduced_upper: bfloat16 [16, 2, 1024, 1024], P('cuts', None, 'row')
- reduced_rhs: float32 [16, 2, 1024, 128], P('cuts', None, 'row')
- block_solutions: float32 [16, 2, 1024, 128], P('cuts', None, 'row')
The draws below stay inside these ranges and needn't reach their ends.
Inputs may be any that keep to these rules, and one draw needn't show every extreme that they name: Active orbitals of each slice, at least half of 1024; block rows and columns at or beyond the count are inactive; some slice has all 1024. `diagonal_blocks`: diagonal blocks, a varying diagonal plus a dense part. `diagonal_inverses`: approximate inverses of the diagonal blocks.
All inputs are finite; a program needn't handle non-finite values.
Results may differ from the reference program's by a relative error of at most 0.014.
Values may be sent and summed in bfloat16 or wider, within the bound.
No kernel may reach another device: no remote copies, remote signals or barrier semaphores. Data moves between devices by JAX's collectives and lax.ppermute only.
A program may use at most 64 MiB of HBM per device.

```python
import math
import jax
import jax.numpy as jnp
from jax import lax

ORB = 1024
NRHS = 128
REFINE = 2
SLICES = 32


def paired_blocks(key, diag_low, diag_high, scale):
    key_diag, key_gauss = jax.random.split(key, 2)
    diagonal = jax.random.uniform(key_diag, (SLICES, ORB), jnp.float32, diag_low, diag_high)
    gauss = jax.random.normal(key_gauss, (SLICES, 2, ORB, ORB), jnp.float32)
    offdiag = gauss * (scale / math.sqrt(ORB))
    identity = jnp.eye(ORB, dtype=jnp.float32)
    blocks = jnp.stack([offdiag[:, 0] + identity[None] * diagonal[:, :, None], offdiag[:, 1]], axis=1)
    outer = diagonal[:, :, None] * diagonal[:, None, :]
    inverses = jnp.stack([identity[None] / diagonal[:, :, None] - offdiag[:, 0] / outer, -offdiag[:, 1] / outer], axis=1)
    return (blocks, inverses)


def draw_diagonal_blocks(key, part):
    blocks, inverses = paired_blocks(key, 1.2, 2.4, 0.6)
    return blocks.astype(jnp.bfloat16)


def draw_diagonal_inverses(key, part):
    blocks, inverses = paired_blocks(key, 1.2, 2.4, 0.6)
    return inverses.astype(jnp.bfloat16)


def draw_orbitals(key, part):
    key = jax.random.fold_in(key, 7)
    key_counts, key_full = jax.random.split(key)
    counts = jax.random.randint(key_counts, (SLICES,), ORB // 2, ORB + 1, jnp.int32)
    fullest = jax.random.randint(key_full, (), 0, SLICES, jnp.int32)
    return jnp.where(jnp.arange(SLICES, dtype=jnp.int32) == fullest, ORB, counts).astype(jnp.int32)


def levels(key, extent, shards, smallest, high):
    gain, own = 1.0, jax.random.fold_in(key, 6)
    for dim, blocks in shards:
        heights = jnp.exp(jax.random.uniform(jax.random.fold_in(own, dim), (blocks,), jnp.float32, smallest / len(shards), high / len(shards)))
        gain = gain * jnp.repeat(heights, extent[dim] // blocks).reshape([-1 if axis == dim else 1 for axis in range(len(extent))])
    return gain


def bell_draw(own_key, extent, spread, reach, cuts=(), held_as=jnp.bfloat16):
    drawn = jax.random.normal(own_key, extent, jnp.float32) * spread
    if len(cuts) > 0:
        drawn = levels(own_key, extent, cuts, -0.22, 0.18) * drawn
    return jnp.clip(drawn, min=-reach, max=reach).astype(held_as)


def setup_inputs(seed: int = 0) -> dict:
    splits = jax.random.split(jax.random.key(seed), 7)
    return {
        "diagonal_blocks": draw_diagonal_blocks(jax.random.fold_in(splits[6], 71), 0),
        "diagonal_inverses": draw_diagonal_inverses(jax.random.fold_in(splits[6], 71), 0),
        "lower_blocks": bell_draw(splits[2], (SLICES, 2, ORB, ORB), (0.75 / ORB ** 0.5), 0.140625, ((0, 16), (2, 16))),
        "upper_blocks": bell_draw(splits[3], (SLICES, 2, ORB, ORB), (0.75 / ORB ** 0.5), 0.140625, ((0, 16), (2, 16))),
        "injection": bell_draw(splits[4], (SLICES, 2, ORB, NRHS), 1.0, 6.0, ((0, 16), (2, 16))),
        "orbitals": draw_orbitals(jax.random.fold_in(splits[6], 71), 0),
    }


def complex_product(left_block, right_block):
    real_part = jnp.dot(left_block[0], right_block[0], preferred_element_type=jnp.float32) - jnp.dot(left_block[1], right_block[1], preferred_element_type=jnp.float32)
    imag_part = jnp.dot(left_block[0], right_block[1], preferred_element_type=jnp.float32) + jnp.dot(left_block[1], right_block[0], preferred_element_type=jnp.float32)
    return jnp.stack([real_part, imag_part])


def odd_terms(slice_item):
    inverse, upper_block, lower_block, source = slice_item
    return (complex_product(inverse, upper_block).astype(jnp.bfloat16),
            complex_product(inverse, lower_block).astype(jnp.bfloat16),
            complex_product(inverse, source).astype(jnp.bfloat16))


def even_terms(slice_item):
    diagonal, lower_block, upper_block, source, p_prev, q_prev, y_prev, p_next, q_next, y_next = slice_item
    lower_p = complex_product(lower_block, p_prev)
    lower_q = complex_product(lower_block, q_prev)
    lower_y = complex_product(lower_block, y_prev)
    upper_p = complex_product(upper_block, p_next)
    upper_q = complex_product(upper_block, q_next)
    upper_y = complex_product(upper_block, y_next)
    new_diagonal = (diagonal.astype(jnp.float32) - lower_p - upper_q).astype(jnp.bfloat16)
    new_lower = (-lower_q).astype(jnp.bfloat16)
    new_upper = (-upper_p).astype(jnp.bfloat16)
    new_source = (source.astype(jnp.float32) - lower_y - upper_y).astype(jnp.bfloat16)
    return new_diagonal, new_lower, new_upper, new_source


def refine_solve(slice_item):
    diagonal, inverse, source = slice_item
    iterate = complex_product(inverse, source).astype(jnp.bfloat16)
    for refine_turn in range(REFINE):
        residue = (source.astype(jnp.float32) - complex_product(diagonal, iterate)).astype(jnp.bfloat16)
        iterate = (iterate.astype(jnp.float32) + complex_product(inverse, residue)).astype(jnp.bfloat16)
    return iterate


def combine_terms(slice_item):
    lower_block, upper_block, source, from_below, from_above = slice_item
    return source.astype(jnp.float32) - complex_product(lower_block, from_below) - complex_product(upper_block, from_above)


def reference(diagonal_blocks, diagonal_inverses, lower_blocks, upper_blocks, injection, orbitals):
    empty_count = jnp.zeros((1,), jnp.int32)
    padded = jnp.concatenate([empty_count, orbitals.astype(jnp.int32), empty_count])
    own_count = padded[1:-1]
    before_count = padded[:-2]
    after_count = padded[2:]
    places = jnp.arange(ORB, dtype=jnp.int32)
    row_on = places[None, :] < own_count[:, None]
    lower_on = row_on[:, :, None] & (places[None, None, :] < before_count[:, None, None])
    upper_on = row_on[:, :, None] & (places[None, None, :] < after_count[:, None, None])
    lower_masked = lower_blocks * lower_on[:, None].astype(jnp.bfloat16)
    upper_masked = upper_blocks * upper_on[:, None].astype(jnp.bfloat16)
    source = injection * row_on[:, None, :, None].astype(jnp.bfloat16)
    p_next, q_next, y_next = lax.map(odd_terms, (diagonal_inverses[1::2], upper_masked[1::2], lower_masked[1::2], source[1::2]))
    p_prev = jnp.concatenate([jnp.zeros_like(p_next[:1]), p_next[:-1]])
    q_prev = jnp.concatenate([jnp.zeros_like(q_next[:1]), q_next[:-1]])
    y_prev = jnp.concatenate([jnp.zeros_like(y_next[:1]), y_next[:-1]])
    new_diagonal, new_lower, new_upper, new_source = lax.map(even_terms, (diagonal_blocks[0::2], lower_masked[0::2], upper_masked[0::2], source[0::2], p_prev, q_prev, y_prev, p_next, q_next, y_next))
    solved = lax.map(refine_solve, (new_diagonal, diagonal_inverses[0::2], new_source))
    zero_slice = jnp.zeros_like(solved[:1])
    from_below = jnp.concatenate([zero_slice, solved[:-1]])
    from_above = jnp.concatenate([solved[1:], zero_slice])
    combined = lax.map(combine_terms, (new_lower, new_upper, new_source, from_below, from_above))
    return new_diagonal, new_lower, new_upper, combined, solved.astype(jnp.float32)
```

```python
import functools

import jax
import jax.numpy as jnp
from jax import lax
from jax.experimental import pallas as pl
from jax.experimental.pallas import tpu as pltpu
from jax.sharding import PartitionSpec as P

REFINE = 2
BF = jnp.bfloat16
F32 = jnp.float32
VMEM = pl.BlockSpec(memory_space=pltpu.VMEM)
SMEM = pl.BlockSpec(memory_space=pltpu.SMEM)


def call(kernel, out_shapes, flops, *args):
    moved = sum(a.size * a.dtype.itemsize for a in args) + sum(
        s.size * s.dtype.itemsize for s in out_shapes
    )
    return pl.pallas_call(
        kernel,
        out_shape=tuple(out_shapes),
        in_specs=[SMEM] + [VMEM] * (len(args) - 1),
        out_specs=tuple([VMEM] * len(out_shapes)),
        compiler_params=pltpu.CompilerParams(vmem_limit_bytes=40 * 1024 * 1024),
        cost_estimate=pl.CostEstimate(flops=flops, bytes_accessed=moved, transcendentals=0),
    )(*args)


def shape(dims, dtype=BF):
    return jax.ShapeDtypeStruct(dims, dtype)


def mod4(v):
    return lax.rem(v + 8, 4)


def lanes_of(rows):
    return lax.broadcasted_iota(jnp.int32, (rows, 128), 1)


def combine_small(real_rows, imag_rows):
    lane = lanes_of(real_rows.shape[0])
    turned = jnp.where(lane < 32, -pltpu.roll(imag_rows, 96, 1), pltpu.roll(imag_rows, 32, 1))
    return jnp.where(lane < 64, real_rows + turned, 0.0)


def prepare_kernel(s_ref, d_ref, g_ref, a_ref, c_ref, b_ref,
                   piece0, piece1, piece2, piece3, g_odd, g_even, a_even, c_even):
    y, x = s_ref[0], s_ref[1]
    first_row = (y * 4 + x) * 64
    before, own, odd, after = s_ref[2], s_ref[3], s_ref[4], s_ref[5]
    row = first_row + lax.broadcasted_iota(jnp.int32, (64, 256), 0)
    col = lax.broadcasted_iota(jnp.int32, (64, 256), 1)
    row_b = first_row + lax.broadcasted_iota(jnp.int32, (64, 128), 0)
    lane = lanes_of(64)

    def masked(block, rows_on, chunk, cols_on):
        on = (row < rows_on) & (col + chunk * 256 < cols_on)
        return jnp.where(on, block.astype(F32), 0.0).astype(BF)

    for shift, piece in enumerate((piece0, piece1, piece2, piece3)):
        chunk = mod4(x + shift)
        cols = pl.ds(pl.multiple_of(chunk * 256, 256), 256)
        for part in range(2):
            piece[:, pl.ds(part * 256, 256)] = masked(c_ref[1, part, :, cols], odd, chunk, after)
            piece[:, pl.ds(512 + part * 256, 256)] = masked(a_ref[1, part, :, cols], odd, chunk, own)
            piece[:, pl.ds(1152 + part * 256, 256)] = d_ref[0, part, :, cols]
        tile = jnp.zeros((64, 128), F32)
        for place, (which, part, rows_on) in enumerate(
            ((1, 0, odd), (1, 1, odd), (0, 0, own), (0, 1, own))
        ):
            block = jnp.where(row_b < rows_on, b_ref[which, part].astype(F32), 0.0)
            turned = pltpu.roll(block, mod4(place - chunk) * 32, 1)
            tile = jnp.where((lane >= place * 32) & (lane < place * 32 + 32), turned, tile)
        piece[:, pl.ds(1024, 128)] = tile.astype(BF)
    for place in range(4):
        chunk = mod4(y + place)
        cols = pl.ds(pl.multiple_of(chunk * 256, 256), 256)
        out = pl.ds(place * 256, 256)
        for part in range(2):
            g_odd[part, :, out] = g_ref[1, part, :, cols]
            g_even[part, :, out] = g_ref[0, part, :, cols]
            a_even[part, :, out] = masked(a_ref[0, part, :, cols], own, chunk, before)
            c_even[part, :, out] = masked(c_ref[0, part, :, cols], own, chunk, odd)


def assemble_kernel(s_ref, piece0, piece1, piece2, piece3, panel, diagonal):
    x = s_ref[1]
    for shift, piece in enumerate((piece0, piece1, piece2, piece3)):
        rows = pl.ds(pl.multiple_of(mod4(x - shift) * 64, 64), 64)
        panel[rows, :] = piece[:, pl.ds(0, 1152)]
        diagonal[rows, :] = piece[:, pl.ds(1152, 512)]


def wide_dot(left, panels, start, width):
    total = None
    for place, panel in enumerate(panels):
        term = jnp.dot(
            left[:, place * 256 : place * 256 + 256],
            panel[:, pl.ds(start, width)],
            preferred_element_type=F32,
        )
        total = term if total is None else total + term
    return total


def split_rows(stacked):
    width = stacked.shape[1]
    parts = stacked.reshape(4, 2, 64, width)
    return parts[:, 0].reshape(256, width), parts[:, 1].reshape(256, width)


def wide_product(left, panels, start):
    real_rows, imag_rows = split_rows(wide_dot(left, panels, start, 512))
    real = real_rows[:, :256] - imag_rows[:, 256:]
    imag = real_rows[:, 256:] + imag_rows[:, :256]
    return real, imag


def small_product(left, panels, start):
    return combine_small(*split_rows(wide_dot(left, panels, start, 128)))


def odd_kernel(s_ref, g_ref, panel0, panel1, panel2, panel3, out):
    left = g_ref[...].reshape(512, 1024)
    panels = (panel0, panel1, panel2, panel3)
    for start in (0, 512):
        real, imag = wide_product(left, panels, start)
        out[:, pl.ds(start, 256)] = real.astype(BF)
        out[:, pl.ds(start + 256, 256)] = imag.astype(BF)
    out[:, pl.ds(1024, 128)] = small_product(left, panels, 1024).astype(BF)


def even_kernel(s_ref, a_ref, c_ref, panel0, panel1, panel2, panel3, diagonal, source,
                ship, ship_lower, upper_new, diagonal_part, source_part):
    panels = (panel0, panel1, panel2, panel3)
    left = a_ref[...].reshape(512, 1024)
    ship[:, pl.ds(512, 128)] = small_product(left, panels, 1024).astype(BF)
    real, imag = wide_product(left, panels, 0)
    ship[:, pl.ds(0, 256)] = real.astype(BF)
    ship[:, pl.ds(256, 256)] = imag.astype(BF)
    real, imag = wide_product(left, panels, 512)
    ship_lower[:, pl.ds(0, 256)] = (-real).astype(BF)
    ship_lower[:, pl.ds(256, 256)] = (-imag).astype(BF)
    left = c_ref[...].reshape(512, 1024)
    own = pltpu.roll(source[:, pl.ds(1024, 128)].astype(F32), 64, 1)
    own = jnp.where(lanes_of(256) < 64, own, 0.0)
    source_part[...] = own - small_product(left, panels, 1024)
    real, imag = wide_product(left, panels, 512)
    diagonal_part[:, pl.ds(0, 256)] = diagonal[:, pl.ds(0, 256)].astype(F32) - real
    diagonal_part[:, pl.ds(256, 256)] = diagonal[:, pl.ds(256, 256)].astype(F32) - imag
    real, imag = wide_product(left, panels, 0)
    upper_new[:, pl.ds(0, 256)] = (-real).astype(BF)
    upper_new[:, pl.ds(256, 256)] = (-imag).astype(BF)


def finish_kernel(s_ref, diagonal_part, source_part, shipped, diagonal_new, source_new):
    diagonal_new[...] = (diagonal_part[...] - shipped[:, pl.ds(0, 512)].astype(F32)).astype(BF)
    source_new[...] = (source_part[...] - shipped[:, pl.ds(512, 128)].astype(F32)).astype(BF)


def pair_kernel(s_ref, lower, upper, out):
    out[:, pl.ds(0, 512)] = lower[...]
    out[:, pl.ds(512, 512)] = upper[...]


def inverse_kernel(s_ref, g_ref, base, piece0, piece1, piece2, piece3, out, add):
    left = g_ref[...].reshape(512, 1024)
    value = small_product(left, (piece0, piece1, piece2, piece3), 0)
    if add:
        value = base[...].astype(F32) + value
    out[...] = value.astype(BF)


def panel_product(block_of, pieces):
    real_rows = imag_rows = None
    for place, piece in enumerate(pieces):
        block = block_of(place)
        right = piece[...]
        real = jnp.dot(block[:, :256], right, preferred_element_type=F32)
        imag = jnp.dot(block[:, 256:512], right, preferred_element_type=F32)
        real_rows = real if real_rows is None else real_rows + real
        imag_rows = imag if imag_rows is None else imag_rows + imag
    return combine_small(real_rows, imag_rows)


def residue_kernel(s_ref, blocks, source, piece0, piece1, piece2, piece3, out):
    y = s_ref[0]
    pieces = (piece0, piece1, piece2, piece3)
    value = panel_product(lambda place: blocks[mod4(y + place)], pieces)
    out[...] = (source[...].astype(F32) - value).astype(BF)


def gather_diagonal_kernel(s_ref, block0, block1, block2, block3, out, rows_out):
    x = s_ref[1]
    rows = pl.ds(pl.multiple_of(x * 64, 64), 64)
    for shift, block in enumerate((block0, block1, block2, block3)):
        chunk = mod4(x - shift)
        out[chunk] = block[...]
        cols = pl.ds(pl.multiple_of(chunk * 256, 256), 256)
        rows_out[0, :, cols] = block[rows, pl.ds(0, 256)]
        rows_out[1, :, cols] = block[rows, pl.ds(256, 256)]


def coupling_rows_kernel(s_ref, pairs, lower_out, upper_out):
    rows = pl.ds(pl.multiple_of(s_ref[1] * 64, 64), 64)
    for chunk in range(4):
        cols = pl.ds(chunk * 256, 256)
        lower_out[0, :, cols] = pairs[chunk, rows, pl.ds(0, 256)]
        lower_out[1, :, cols] = pairs[chunk, rows, pl.ds(256, 256)]
        upper_out[0, :, cols] = pairs[chunk, rows, pl.ds(512, 256)]
        upper_out[1, :, cols] = pairs[chunk, rows, pl.ds(768, 256)]


def couple_kernel(s_ref, pairs, source, solved, piece0, piece1, piece2, piece3,
                  out0, out1, out2, out3, held):
    y, x = s_ref[0], s_ref[1]
    pieces = (piece0, piece1, piece2, piece3)
    lower = panel_product(
        lambda place: pairs[mod4(y + place), :, pl.ds(0, 512)], [p.at[0] for p in pieces]
    )
    upper = panel_product(
        lambda place: pairs[mod4(y + place), :, pl.ds(512, 512)], [p.at[1] for p in pieces]
    )
    combined = source[...].astype(F32) - lower - upper
    moved = pltpu.roll(solved[...].astype(F32), 64, 1)
    held[...] = jnp.where(lanes_of(256) < 64, combined, moved)
    for shift, out in enumerate((out0, out1, out2, out3)):
        out[...] = held[pl.ds(pl.multiple_of(mod4(x + shift) * 64, 64), 64), :]


def spread_kernel(s_ref, piece0, piece1, piece2, piece3, combined, solved):
    x = s_ref[1]
    lane = lanes_of(64)
    totals = [jnp.zeros((64, 128), F32) for _ in range(4)]
    for shift, piece in enumerate((piece0, piece1, piece2, piece3)):
        chunk = mod4(x - shift)
        value = piece[...]
        on = (lane >= chunk * 32) & (lane < chunk * 32 + 32)
        for place in range(4):
            turned = pltpu.roll(value, mod4(chunk - place) * 32, 1)
            totals[place] = jnp.where(on, turned, totals[place])
    combined[0] = totals[0]
    combined[1] = totals[1]
    solved[0] = totals[2]
    solved[1] = totals[3]


def moved_x(block, by):
    pairs = [(y * 4 + x, y * 4 + (x + by) % 4) for y in range(4) for x in range(4)]
    return lax.ppermute(block, "row", pairs)


def moved_y(block, by):
    pairs = [(y * 4 + x, ((y + by) % 4) * 4 + x) for y in range(4) for x in range(4)]
    return lax.ppermute(block, "row", pairs)


def gathered_y(block):
    return (block, moved_y(block, 3), moved_y(block, 2), moved_y(block, 1))


def gathered_x(block):
    groups = [[y * 4 + x for x in range(4)] for y in range(4)]
    return lax.all_gather(block, "row", axis_index_groups=groups)


def along_cuts(block, by):
    count = lax.axis_size("cuts")
    pairs = [(i, i + by) for i in range(count) if 0 <= i + by < count]
    return lax.ppermute(block, "cuts", pairs)


def body(diagonal_blocks, diagonal_inverses, lower_blocks, upper_blocks, injection, orbitals):
    cut = lax.axis_index("cuts")
    place = lax.axis_index("row")
    zero = jnp.zeros((1,), jnp.int32)
    window = lax.dynamic_slice_in_dim(jnp.concatenate([zero, orbitals, zero]), 2 * cut, 4)
    scalars = jnp.concatenate([jnp.stack([place // 4, place % 4]).astype(jnp.int32), window])
    pieces_and = call(
        prepare_kernel,
        [shape((64, 1664))] * 4 + [shape((2, 64, 1024))] * 4,
        0,
        scalars, diagonal_blocks, diagonal_inverses, lower_blocks, upper_blocks, injection,
    )
    pieces, (g_odd, g_even, a_even, c_even) = pieces_and[:4], pieces_and[4:]
    a_next = along_cuts(a_even, -1)
    g_odd_rows = gathered_x(g_odd)
    c_rows = gathered_x(c_even)
    a_rows = gathered_x(a_next)
    g_even_rows = gathered_x(g_even)
    pieces = [pieces[0]] + [moved_x(pieces[by], by) for by in (1, 2, 3)]
    panel, diagonal = call(
        assemble_kernel, [shape((256, 1152)), shape((256, 512))], 0, scalars, *pieces
    )
    panels = gathered_y(panel)
    (odd_panel,) = call(
        odd_kernel, [shape((256, 1152))], 2 * 512 * 1024 * 1152, scalars, g_odd_rows, *panels
    )
    odd_panels = gathered_y(odd_panel)
    ship, ship_lower, upper_new, diagonal_part, source_part = call(
        even_kernel,
        [shape((256, 640)), shape((256, 512)), shape((256, 512)), shape((256, 512), F32),
         shape((256, 128), F32)],
        4 * 512 * 1024 * 1152,
        scalars, a_rows, c_rows, *odd_panels, diagonal, panel,
    )
    shipped = along_cuts(ship, 1)
    lower_new = along_cuts(ship_lower, 1)
    diagonal_new, source = call(
        finish_kernel,
        [shape((256, 512)), shape((256, 128))],
        0, scalars, diagonal_part, source_part, shipped,
    )
    (pair,) = call(pair_kernel, [shape((256, 1024))], 0, scalars, lower_new, upper_new)
    pairs = gathered_x(pair)
    sources = gathered_y(source)
    diagonals = (diagonal_new,) + tuple(moved_x(diagonal_new, by) for by in (1, 2, 3))
    diagonal_panel, diagonal_rows = call(
        gather_diagonal_kernel,
        [shape((4, 256, 512)), shape((2, 64, 1024))],
        0, scalars, *diagonals,
    )
    solve_flops = 2 * 512 * 1024 * 128
    (iterate,) = call(
        functools.partial(inverse_kernel, add=False),
        [shape((256, 128))], solve_flops, scalars, g_even_rows, source, *sources,
    )
    for _ in range(REFINE):
        (residue,) = call(
            residue_kernel,
            [shape((256, 128))], solve_flops,
            scalars, diagonal_panel, source, *gathered_y(iterate),
        )
        (iterate,) = call(
            functools.partial(inverse_kernel, add=True),
            [shape((256, 128))], solve_flops,
            scalars, g_even_rows, iterate, *gathered_y(residue),
        )
    neighbours = jnp.stack([along_cuts(iterate, 1), along_cuts(iterate, -1)])
    ends = pl.pallas_call(
        couple_kernel,
        out_shape=tuple([shape((64, 128), F32)] * 4),
        in_specs=[SMEM] + [VMEM] * 7,
        out_specs=tuple([VMEM] * 4),
        scratch_shapes=[pltpu.VMEM((256, 128), F32)],
        compiler_params=pltpu.CompilerParams(vmem_limit_bytes=40 * 1024 * 1024),
    )(scalars, pairs, source, iterate, *gathered_y(neighbours))
    ends = [ends[0]] + [moved_x(ends[by], by) for by in (1, 2, 3)]
    combined, solved = call(
        spread_kernel, [shape((2, 64, 128), F32)] * 2, 0, scalars, *ends
    )
    lower_rows, upper_rows = call(
        coupling_rows_kernel, [shape((2, 64, 1024))] * 2, 0, scalars, pairs
    )
    return (
        diagonal_rows[None],
        lower_rows[None],
        upper_rows[None],
        combined[None],
        solved[None],
    )


def solution(mesh):
    split = P("cuts", None, "row", None)
    return jax.shard_map(
        body,
        mesh=mesh,
        in_specs=(split, split, split, split, split, P()),
        out_specs=(split,) * 5,
        check_vma=False,
    )
```

```python
import functools

import jax
import jax.numpy as jnp
from jax import lax
from jax.experimental import pallas as pl
from jax.experimental.pallas import tpu as pltpu
from jax.sharding import PartitionSpec as P

REFINE = 2
BF = jnp.bfloat16
F32 = jnp.float32
VMEM = pl.BlockSpec(memory_space=pltpu.VMEM)
SMEM = pl.BlockSpec(memory_space=pltpu.SMEM)


def call(kernel, out_shapes, flops, *args, scratch=(), hbm=0):
    moved = sum(a.size * a.dtype.itemsize for a in args) + sum(
        s.size * s.dtype.itemsize for s in out_shapes
    )
    anywhere = pl.BlockSpec(memory_space=pl.ANY)
    return pl.pallas_call(
        kernel,
        out_shape=tuple(out_shapes),
        in_specs=[SMEM] + [anywhere] * hbm + [VMEM] * (len(args) - 1 - hbm),
        out_specs=tuple([VMEM] * len(out_shapes)),
        scratch_shapes=list(scratch),
        compiler_params=pltpu.CompilerParams(vmem_limit_bytes=32 * 1024 * 1024),
        cost_estimate=pl.CostEstimate(flops=flops, bytes_accessed=moved, transcendentals=0),
    )(*args)


def shape(dims, dtype=BF):
    return jax.ShapeDtypeStruct(dims, dtype)


def mod4(v):
    return lax.rem(v + 8, 4)


def at(chunk, size):
    return pl.ds(pl.multiple_of(chunk * size, size), size)


def lanes_of(rows):
    return lax.broadcasted_iota(jnp.int32, (rows, 128), 1)


def combine_small(real_rows, imag_rows):
    lane = lanes_of(real_rows.shape[0])
    turned = jnp.where(lane < 32, -pltpu.roll(imag_rows, 96, 1), pltpu.roll(imag_rows, 32, 1))
    return jnp.where(lane < 64, real_rows + turned, 0.0)


def packed(block):
    half = block.shape[0] // 2
    return jnp.where(lanes_of(half) < 64, block[:half], pltpu.roll(block[half:], 64, 1))


def halves(block):
    return block, pltpu.roll(block, 64, 1)


def masked(block, first_row, rows_on, chunk, cols_on):
    row = first_row + lax.broadcasted_iota(jnp.int32, (64, 256), 0)
    col = chunk * 256 + lax.broadcasted_iota(jnp.int32, (64, 256), 1)
    return jnp.where((row < rows_on) & (col < cols_on), block.astype(F32), 0.0).astype(BF)


def prepare_kernel(s_ref, d_hbm, a_hbm, c_hbm, b_hbm, piece0, piece1, piece2, piece3,
                   d_ref, a_ref, c_ref, b_ref, sems):
    y, x = s_ref[0], s_ref[1]
    first_row = (y * 4 + x) * 64
    before, own, odd, after = s_ref[2], s_ref[3], s_ref[4], s_ref[5]
    copies = [
        pltpu.make_async_copy(source, target, sems.at[index])
        for index, (source, target) in enumerate(
            (
                (c_hbm.at[1, 0], c_ref.at[0]),
                (c_hbm.at[1, 1], c_ref.at[1]),
                (b_hbm, b_ref),
                (a_hbm.at[1, 0], a_ref.at[0]),
                (a_hbm.at[1, 1], a_ref.at[1]),
                (d_hbm.at[0, 0], d_ref.at[0]),
                (d_hbm.at[0, 1], d_ref.at[1]),
            )
        )
    ]
    for copy in copies:
        copy.start()
    pieces = (piece0, piece1, piece2, piece3)
    row_b = first_row + lax.broadcasted_iota(jnp.int32, (64, 128), 0)
    lane = lanes_of(64)
    copies[0].wait()
    copies[1].wait()
    for shift, piece in enumerate(pieces):
        chunk = mod4(x + shift)
        for part in range(2):
            piece[:, pl.ds(part * 256, 256)] = masked(
                c_ref[part, :, at(chunk, 256)], first_row, odd, chunk, after
            )
    copies[2].wait()
    blocks = [
        jnp.where(row_b < rows_on, b_ref[which, part].astype(F32), 0.0)
        for which, part, rows_on in ((1, 0, odd), (1, 1, odd), (0, 0, own), (0, 1, own))
    ]
    for shift, piece in enumerate(pieces):
        chunk = mod4(x + shift)
        tile = jnp.zeros((64, 128), F32)
        for place, block in enumerate(blocks):
            turned = pltpu.roll(block, mod4(place - chunk) * 32, 1)
            tile = jnp.where((lane >= place * 32) & (lane < place * 32 + 32), turned, tile)
        piece[:, pl.ds(512, 128)] = tile.astype(BF)
    copies[3].wait()
    copies[4].wait()
    for shift, piece in enumerate(pieces):
        chunk = mod4(x + shift)
        for part in range(2):
            piece[:, pl.ds(640 + part * 256, 256)] = masked(
                a_ref[part, :, at(chunk, 256)], first_row, odd, chunk, own
            )
    copies[5].wait()
    copies[6].wait()
    for shift, piece in enumerate(pieces):
        chunk = mod4(x + shift)
        for part in range(2):
            piece[:, pl.ds(1152 + part * 256, 256)] = d_ref[part, :, at(chunk, 256)]


def couplings_kernel(s_ref, a_ref, c_ref, a_even, c_even):
    first_row = (s_ref[0] * 4 + s_ref[1]) * 64
    before, own, odd = s_ref[2], s_ref[3], s_ref[4]
    for chunk in range(4):
        cols = pl.ds(chunk * 256, 256)
        for part in range(2):
            a_even[part, :, cols] = masked(a_ref[part, :, cols], first_row, own, chunk, before)
            c_even[part, :, cols] = masked(c_ref[part, :, cols], first_row, own, chunk, odd)


def assemble_kernel(s_ref, piece0, piece1, piece2, piece3, panel, panel_a, diagonal):
    x = s_ref[1]
    for shift, piece in enumerate((piece0, piece1, piece2, piece3)):
        rows = at(mod4(x - shift), 64)
        panel[rows, :] = piece[:, pl.ds(0, 640)]
        panel_a[rows, :] = piece[:, pl.ds(640, 512)]
        diagonal[rows, :] = piece[:, pl.ds(1152, 512)]


def stack_rows(x, blocks, held):
    for shift, block in enumerate(blocks):
        held[at(mod4(x - shift), 128), :] = block[...].reshape(128, 1024)


def wide_dot(y, held, panels, start, width):
    total = None
    for place, panel in enumerate(panels):
        term = jnp.dot(
            held[:, at(mod4(y + place), 256)],
            panel[:, pl.ds(start, width)],
            preferred_element_type=F32,
        )
        total = term if total is None else total + term
    parts = total.reshape(4, 2, 64, width)
    return parts[:, 0].reshape(256, width), parts[:, 1].reshape(256, width)


def wide_product(y, held, panels):
    real_rows, imag_rows = wide_dot(y, held, panels, 0, 512)
    real = real_rows[:, :256] - imag_rows[:, 256:]
    imag = real_rows[:, 256:] + imag_rows[:, :256]
    return real, imag


def small_product(y, held, panels):
    return combine_small(*wide_dot(y, held, panels, 512, 128))


def put_pair(out, real, imag):
    out[:, pl.ds(0, 256)] = real.astype(out.dtype)
    out[:, pl.ds(256, 256)] = imag.astype(out.dtype)


def odd_kernel(s_ref, g0, g1, g2, g3, panel0, panel1, panel2, panel3, out, g_rows, held):
    y, x = s_ref[0], s_ref[1]
    panels = (panel0, panel1, panel2, panel3)
    stack_rows(x, (g0, g1, g2, g3), held)
    g_rows[...] = held[...]
    put_pair(out, *wide_product(y, held, panels))
    out[:, pl.ds(512, 128)] = small_product(y, held, panels).astype(BF)


def odd_second_kernel(s_ref, g_rows, panel0, panel1, panel2, panel3, out):
    put_pair(out, *wide_product(s_ref[0], g_rows, (panel0, panel1, panel2, panel3)))


def even_kernel(s_ref, ca0, ca1, ca2, ca3, panel0, panel1, panel2, panel3, source,
                ship, upper_new, source_part, a_rows, c_rows):
    y, x = s_ref[0], s_ref[1]
    panels = (panel0, panel1, panel2, panel3)
    blocks = (ca0, ca1, ca2, ca3)
    stack_rows(x, [b.at[1] for b in blocks], a_rows)
    stack_rows(x, [b.at[0] for b in blocks], c_rows)
    ship[:, pl.ds(512, 128)] = small_product(y, a_rows, panels).astype(BF)
    put_pair(ship, *wide_product(y, a_rows, panels))
    own = pltpu.roll(source[:, pl.ds(512, 128)].astype(F32), 64, 1)
    own = jnp.where(lanes_of(256) < 64, own, 0.0)
    source_part[...] = own - small_product(y, c_rows, panels)
    real, imag = wide_product(y, c_rows, panels)
    put_pair(upper_new, -real, -imag)


def source_kernel(s_ref, source_part, shipped, source_new):
    source_new[...] = packed(
        source_part[...] - shipped[:, pl.ds(512, 128)].astype(F32)
    ).astype(BF)


def diagonal_kernel(s_ref, c_rows, panel0, panel1, panel2, panel3, diagonal, shipped, out):
    real, imag = wide_product(s_ref[0], c_rows, (panel0, panel1, panel2, panel3))
    real = diagonal[:, pl.ds(0, 256)].astype(F32) - real - shipped[:, pl.ds(0, 256)].astype(F32)
    imag = diagonal[:, pl.ds(256, 256)].astype(F32) - imag - shipped[:, pl.ds(256, 256)].astype(F32)
    put_pair(out, real, imag)


def lower_kernel(s_ref, a_rows, panel0, panel1, panel2, panel3, out):
    real, imag = wide_product(s_ref[0], a_rows, (panel0, panel1, panel2, panel3))
    put_pair(out, -real, -imag)


def pair_kernel(s_ref, lower, upper, out):
    out[:, pl.ds(0, 512)] = lower[...]
    out[:, pl.ds(512, 512)] = upper[...]


def whole_inverse(y, g_ref, pieces, vector):
    for place, piece in enumerate(pieces):
        for index, half in enumerate(halves(piece[...].astype(F32))):
            rows = pl.ds(pl.multiple_of(mod4(y + place) * 256 + index * 128, 128), 128)
            vector[rows, :] = half.astype(BF)
    right = vector[...]
    for block in range(4):
        left = g_ref[pl.ds(block * 4, 4)].reshape(512, 1024)
        total = jnp.dot(left, right, preferred_element_type=F32).reshape(4, 2, 64, 128)
        yield block, combine_small(
            total[:, 0].reshape(256, 128), total[:, 1].reshape(256, 128)
        )


def solve_kernel(s_ref, g_ref, piece0, piece1, piece2, piece3, out, vector):
    pieces = (piece0, piece1, piece2, piece3)
    for block, value in whole_inverse(s_ref[0], g_ref, pieces, vector):
        out[pl.ds(block * 256, 256), :] = value.astype(BF)


def block_product(block, right):
    real = jnp.dot(block[:, pl.ds(0, 256)], right, preferred_element_type=F32)
    imag = jnp.dot(block[:, pl.ds(256, 256)], right, preferred_element_type=F32)
    return real, imag


def residue_of(x, blocks, source, solved):
    real_rows = imag_rows = None
    for shift, block in enumerate(blocks):
        real, imag = block_product(block, solved[at(mod4(x - shift), 256), :])
        real_rows = real if real_rows is None else real_rows + real
        imag_rows = imag if imag_rows is None else imag_rows + imag
    value = packed(combine_small(real_rows, imag_rows))
    return (source[...].astype(F32) - value).astype(BF)


def residue_kernel(s_ref, block0, block1, block2, block3, source, solved, out):
    out[...] = residue_of(s_ref[1], (block0, block1, block2, block3), source, solved)


def turn_kernel(s_ref, g_ref, piece0, piece1, piece2, piece3, solved,
                block0, block1, block2, block3, source, out, residue, vector):
    pieces = (piece0, piece1, piece2, piece3)
    for block, value in whole_inverse(s_ref[0], g_ref, pieces, vector):
        rows = pl.ds(block * 256, 256)
        out[rows, :] = (solved[rows, :].astype(F32) + value).astype(BF)
    residue[...] = residue_of(s_ref[1], (block0, block1, block2, block3), source, out)


def last_kernel(s_ref, g_ref, piece0, piece1, piece2, piece3, solved, out, ship, vector):
    pieces = (piece0, piece1, piece2, piece3)
    for block, value in whole_inverse(s_ref[0], g_ref, pieces, vector):
        rows = pl.ds(block * 256, 256)
        out[rows, :] = (solved[rows, :].astype(F32) + value).astype(BF)
    ship[...] = packed(out[...].astype(F32)).astype(BF)


def diagonal_rows_kernel(s_ref, block0, block1, block2, block3, rows_out):
    x = s_ref[1]
    rows = at(x, 64)
    for shift, block in enumerate((block0, block1, block2, block3)):
        cols = at(mod4(x - shift), 256)
        rows_out[0, :, cols] = block[rows, pl.ds(0, 256)]
        rows_out[1, :, cols] = block[rows, pl.ds(256, 256)]


def coupling_rows_kernel(s_ref, pairs, lower_out, upper_out):
    rows = at(s_ref[1], 64)
    for chunk in range(4):
        cols = pl.ds(chunk * 256, 256)
        lower_out[0, :, cols] = pairs[chunk, rows, pl.ds(0, 256)]
        lower_out[1, :, cols] = pairs[chunk, rows, pl.ds(256, 256)]
        upper_out[0, :, cols] = pairs[chunk, rows, pl.ds(512, 256)]
        upper_out[1, :, cols] = pairs[chunk, rows, pl.ds(768, 256)]


def coupled(pairs, start, neighbour):
    parts = []
    for half in range(2):
        real_rows = imag_rows = None
        for index in range(2):
            block = pairs.at[half * 2 + index, :, pl.ds(start, 512)]
            real, imag = block_product(block, neighbour[pl.ds(index * 256, 256), :])
            real_rows = real if real_rows is None else real_rows + real
            imag_rows = imag if imag_rows is None else imag_rows + imag
        parts.append((real_rows, imag_rows))
    real_rows = parts[0][0] + pltpu.roll(parts[1][0], 64, 1)
    imag_rows = parts[0][1] + pltpu.roll(parts[1][1], 64, 1)
    return combine_small(real_rows, imag_rows)


def couple_kernel(s_ref, pairs, source, solved, below, above, out0, out1, out2, out3, held):
    y, x = s_ref[0], s_ref[1]
    combined = -coupled(pairs, 0, below) - coupled(pairs, 512, above)
    for index, half in enumerate(halves(source[...].astype(F32))):
        rows = pl.ds(index * 128, 128)
        moved = pltpu.roll(
            solved[pl.ds(pl.multiple_of(y * 256 + index * 128, 128), 128), :].astype(F32), 64, 1
        )
        total = half + combined[index * 128 : index * 128 + 128]
        held[rows, :] = jnp.where(lanes_of(128) < 64, total, moved)
    for shift, out in enumerate((out0, out1, out2, out3)):
        out[...] = held[at(mod4(x + shift), 64), :]


def spread_kernel(s_ref, piece0, piece1, piece2, piece3, combined, solved):
    x = s_ref[1]
    lane = lanes_of(64)
    totals = [jnp.zeros((64, 128), F32) for _ in range(4)]
    for shift, piece in enumerate((piece0, piece1, piece2, piece3)):
        chunk = mod4(x - shift)
        value = piece[...]
        on = (lane >= chunk * 32) & (lane < chunk * 32 + 32)
        for place in range(4):
            turned = pltpu.roll(value, mod4(chunk - place) * 32, 1)
            totals[place] = jnp.where(on, turned, totals[place])
    combined[0] = totals[0]
    combined[1] = totals[1]
    solved[0] = totals[2]
    solved[1] = totals[3]


def moved_x(block, by):
    pairs = [(y * 4 + x, y * 4 + (x + by) % 4) for y in range(4) for x in range(4)]
    return lax.ppermute(block, "row", pairs)


def moved_y(block, by):
    pairs = [(y * 4 + x, ((y + by) % 4) * 4 + x) for y in range(4) for x in range(4)]
    return lax.ppermute(block, "row", pairs)


def gathered_y(block):
    return (block, moved_y(block, 3), moved_y(block, 2), moved_y(block, 1))


def gathered_x(block):
    groups = [[y * 4 + x for x in range(4)] for y in range(4)]
    return lax.all_gather(block, "row", axis_index_groups=groups)


def along_cuts(block, by):
    count = lax.axis_size("cuts")
    pairs = [(i, i + by) for i in range(count) if 0 <= i + by < count]
    return lax.ppermute(block, "cuts", pairs)


def body(diagonal_blocks, diagonal_inverses, lower_blocks, upper_blocks, injection, orbitals):
    cut = lax.axis_index("cuts")
    place = lax.axis_index("row")
    zero = jnp.zeros((1,), jnp.int32)
    window = lax.dynamic_slice_in_dim(jnp.concatenate([zero, orbitals, zero]), 2 * cut, 4)
    scalars = jnp.concatenate([jnp.stack([place // 4, place % 4]).astype(jnp.int32), window])
    turns = (1, 2, 3)
    wide_flops = 2 * 512 * 1024 * 512
    solve_flops = 2 * 2048 * 1024 * 128
    vector = pltpu.VMEM((1024, 128), BF)

    pieces = call(
        prepare_kernel,
        [shape((64, 1664))] * 4,
        0,
        scalars, diagonal_blocks, lower_blocks, upper_blocks, injection,
        hbm=4,
        scratch=[pltpu.VMEM((2, 64, 1024), BF)] * 3
        + [pltpu.VMEM((2, 2, 64, 128), BF), pltpu.SemaphoreType.DMA((7,))],
    )
    inverse_even = lax.all_gather(diagonal_inverses[0], "row")
    pieces = [pieces[0]] + [moved_x(pieces[by], by) for by in turns]
    a_even, c_even = call(
        couplings_kernel,
        [shape((2, 64, 1024))] * 2,
        0,
        scalars, lower_blocks[0], upper_blocks[0],
    )
    couplings = jnp.stack([c_even, along_cuts(a_even, -1)])
    g_odd = diagonal_inverses[1]
    g_blocks = [g_odd] + [moved_x(g_odd, by) for by in turns]
    panel, panel_a, diagonal = call(
        assemble_kernel,
        [shape((256, 640)), shape((256, 512)), shape((256, 512))],
        0, scalars, *pieces,
    )
    panels = gathered_y(panel)
    panels_a = gathered_y(panel_a)
    ca_blocks = [couplings] + [moved_x(couplings, by) for by in turns]
    first, g_rows = call(
        odd_kernel, [shape((256, 640)), shape((512, 1024))], wide_flops,
        scalars, *g_blocks, *panels, scratch=[pltpu.VMEM((512, 1024), BF)],
    )
    firsts = gathered_y(first)
    (second,) = call(
        odd_second_kernel, [shape((256, 512))], wide_flops, scalars, g_rows, *panels_a
    )
    seconds = gathered_y(second)
    ship, upper_new, source_part, a_rows, c_rows = call(
        even_kernel,
        [shape((256, 640)), shape((256, 512)), shape((256, 128), F32), shape((512, 1024)),
         shape((512, 1024))],
        2 * wide_flops,
        scalars, *ca_blocks, *firsts, panel,
    )
    shipped = along_cuts(ship, 1)
    (source,) = call(source_kernel, [shape((128, 128))], 0, scalars, source_part, shipped)
    sources = gathered_y(source)
    (diagonal_new,) = call(
        diagonal_kernel, [shape((256, 512))], wide_flops,
        scalars, c_rows, *seconds, diagonal, shipped,
    )
    diagonals = [diagonal_new] + [moved_x(diagonal_new, by) for by in turns]
    (ship_lower,) = call(
        lower_kernel, [shape((256, 512))], wide_flops, scalars, a_rows, *seconds
    )
    lower_new = along_cuts(ship_lower, 1)
    (pair,) = call(pair_kernel, [shape((256, 1024))], 0, scalars, lower_new, upper_new)
    pairs = gathered_x(pair)
    (solved,) = call(
        solve_kernel, [shape((1024, 128))], solve_flops,
        scalars, inverse_even, *sources, scratch=[vector],
    )
    (residue,) = call(
        residue_kernel, [shape((128, 128))], solve_flops // 4,
        scalars, *diagonals, source, solved,
    )
    for _ in range(REFINE - 1):
        solved, residue = call(
            turn_kernel, [shape((1024, 128)), shape((128, 128))], solve_flops,
            scalars, inverse_even, *gathered_y(residue), solved, *diagonals, source,
            scratch=[vector],
        )
    solved, ship_solved = call(
        last_kernel, [shape((1024, 128)), shape((512, 128))], solve_flops,
        scalars, inverse_even, *gathered_y(residue), solved, scratch=[vector],
    )
    below, above = along_cuts(ship_solved, 1), along_cuts(ship_solved, -1)
    (diagonal_rows,) = call(
        diagonal_rows_kernel, [shape((2, 64, 1024))], 0, scalars, *diagonals
    )
    lower_rows, upper_rows = call(
        coupling_rows_kernel, [shape((2, 64, 1024))] * 2, 0, scalars, pairs
    )
    ends = call(
        couple_kernel, [shape((64, 128), F32)] * 4, solve_flops // 2,
        scalars, pairs, source, solved, below, above,
        scratch=[pltpu.VMEM((256, 128), F32)],
    )
    ends = [ends[0]] + [moved_x(ends[by], by) for by in turns]
    combined, solved_rows = call(
        spread_kernel, [shape((2, 64, 128), F32)] * 2, 0, scalars, *ends
    )
    return (
        diagonal_rows[None],
        lower_rows[None],
        upper_rows[None],
        combined[None],
        solved_rows[None],
    )


def solution(mesh):
    split = P("cuts", None, "row", None)
    return jax.shard_map(
        body,
        mesh=mesh,
        in_specs=(split, split, split, split, split, P()),
        out_specs=(split,) * 5,
        check_vma=False,
    )
```

```python
import functools

import jax
import jax.numpy as jnp
from jax import lax
from jax.experimental import pallas as pl
from jax.experimental.pallas import tpu as pltpu
from jax.sharding import PartitionSpec as P

REFINE = 2
BF = jnp.bfloat16
F32 = jnp.float32
VMEM = pl.BlockSpec(memory_space=pltpu.VMEM)
SMEM = pl.BlockSpec(memory_space=pltpu.SMEM)


def call(kernel, out_shapes, flops, *args, scratch=(), hbm=0, mib=32):
    moved = sum(a.size * a.dtype.itemsize for a in args) + sum(
        s.size * s.dtype.itemsize for s in out_shapes
    )
    anywhere = pl.BlockSpec(memory_space=pl.ANY)
    return pl.pallas_call(
        kernel,
        out_shape=tuple(out_shapes),
        in_specs=[SMEM] + [anywhere] * hbm + [VMEM] * (len(args) - 1 - hbm),
        out_specs=tuple([VMEM] * len(out_shapes)),
        scratch_shapes=list(scratch),
        compiler_params=pltpu.CompilerParams(vmem_limit_bytes=mib * 1024 * 1024),
        cost_estimate=pl.CostEstimate(flops=flops, bytes_accessed=moved, transcendentals=0),
    )(*args)


def shape(dims, dtype=BF):
    return jax.ShapeDtypeStruct(dims, dtype)


def mod4(v):
    return lax.rem(v + 8, 4)


def at(chunk, size):
    return pl.ds(pl.multiple_of(chunk * size, size), size)


def lanes_of(rows):
    return lax.broadcasted_iota(jnp.int32, (rows, 128), 1)


def combine_small(real_rows, imag_rows):
    lane = lanes_of(real_rows.shape[0])
    turned = jnp.where(lane < 32, -pltpu.roll(imag_rows, 96, 1), pltpu.roll(imag_rows, 32, 1))
    return jnp.where(lane < 64, real_rows + turned, 0.0)


def packed(block):
    half = block.shape[0] // 2
    return jnp.where(lanes_of(half) < 64, block[:half], pltpu.roll(block[half:], 64, 1))


def halves(block):
    return block, pltpu.roll(block, 64, 1)


def masked(block, first_row, rows_on, chunk, cols_on):
    row = first_row + lax.broadcasted_iota(jnp.int32, (64, 256), 0)
    col = chunk * 256 + lax.broadcasted_iota(jnp.int32, (64, 256), 1)
    return jnp.where((row < rows_on) & (col < cols_on), block.astype(F32), 0.0).astype(BF)


def prepare_kernel(s_ref, d_hbm, g_hbm, a_hbm, c_hbm, b_hbm, piece0, piece1, piece2, piece3,
                   a_even, c_even, g0, g1, g2, g3,
                   d_ref, a_ref, c_ref, b_ref, a_first, c_first, g_first, sems):
    y, x = s_ref[0], s_ref[1]
    first_row = (y * 4 + x) * 64
    before, own, odd, after = s_ref[2], s_ref[3], s_ref[4], s_ref[5]
    copies = [
        pltpu.make_async_copy(source, target, sems.at[index])
        for index, (source, target) in enumerate(
            (
                (c_hbm.at[1, 0], c_ref.at[0]),
                (c_hbm.at[1, 1], c_ref.at[1]),
                (b_hbm, b_ref),
                (a_hbm.at[1, 0], a_ref.at[0]),
                (a_hbm.at[1, 1], a_ref.at[1]),
                (d_hbm.at[0, 0], d_ref.at[0]),
                (d_hbm.at[0, 1], d_ref.at[1]),
                (a_hbm.at[0], a_first),
                (c_hbm.at[0], c_first),
                (g_hbm.at[0], g_first),
            )
        )
    ]
    for copy in copies:
        copy.start()
    pieces = (piece0, piece1, piece2, piece3)
    row_b = first_row + lax.broadcasted_iota(jnp.int32, (64, 128), 0)
    lane = lanes_of(64)
    copies[0].wait()
    copies[1].wait()
    for shift, piece in enumerate(pieces):
        chunk = mod4(x + shift)
        for part in range(2):
            piece[:, pl.ds(part * 256, 256)] = masked(
                c_ref[part, :, at(chunk, 256)], first_row, odd, chunk, after
            )
    copies[2].wait()
    blocks = [
        jnp.where(row_b < rows_on, b_ref[which, part].astype(F32), 0.0)
        for which, part, rows_on in ((1, 0, odd), (1, 1, odd), (0, 0, own), (0, 1, own))
    ]
    for shift, piece in enumerate(pieces):
        chunk = mod4(x + shift)
        tile = jnp.zeros((64, 128), F32)
        for place, block in enumerate(blocks):
            turned = pltpu.roll(block, mod4(place - chunk) * 32, 1)
            tile = jnp.where((lane >= place * 32) & (lane < place * 32 + 32), turned, tile)
        piece[:, pl.ds(512, 128)] = tile.astype(BF)
    copies[3].wait()
    copies[4].wait()
    for shift, piece in enumerate(pieces):
        chunk = mod4(x + shift)
        for part in range(2):
            piece[:, pl.ds(640 + part * 256, 256)] = masked(
                a_ref[part, :, at(chunk, 256)], first_row, odd, chunk, own
            )
    copies[5].wait()
    copies[6].wait()
    for shift, piece in enumerate(pieces):
        chunk = mod4(x + shift)
        for part in range(2):
            piece[:, pl.ds(1152 + part * 256, 256)] = d_ref[part, :, at(chunk, 256)]
    copies[7].wait()
    copies[8].wait()
    for chunk in range(4):
        cols = pl.ds(chunk * 256, 256)
        for part in range(2):
            a_even[part, :, cols] = masked(a_first[part, :, cols], first_row, own, chunk, before)
            c_even[part, :, cols] = masked(c_first[part, :, cols], first_row, own, chunk, odd)
    copies[9].wait()
    for shift, piece in enumerate((g0, g1, g2, g3)):
        for part in range(2):
            piece[part] = g_first[part, :, at(mod4(y + shift), 256)]


def columns_kernel(s_ref, g0, g1, g2, g3, out):
    for shift, piece in enumerate((g0, g1, g2, g3)):
        out[mod4(s_ref[0] - shift)] = piece[...]


def assemble_kernel(s_ref, piece0, piece1, piece2, piece3, panel, panel_a, diagonal):
    x = s_ref[1]
    for shift, piece in enumerate((piece0, piece1, piece2, piece3)):
        rows = at(mod4(x - shift), 64)
        panel[rows, :] = piece[:, pl.ds(0, 640)]
        panel_a[rows, :] = piece[:, pl.ds(640, 512)]
        diagonal[rows, :] = piece[:, pl.ds(1152, 512)]


def stack_rows(x, blocks, held):
    for shift, block in enumerate(blocks):
        held[at(mod4(x - shift), 128), :] = block[...].reshape(128, 1024)


def wide_dot(y, held, panels, start, width):
    total = None
    for place, panel in enumerate(panels):
        term = jnp.dot(
            held[:, at(mod4(y + place), 256)],
            panel[:, pl.ds(start, width)],
            preferred_element_type=F32,
        )
        total = term if total is None else total + term
    parts = total.reshape(4, 2, 64, width)
    return parts[:, 0].reshape(256, width), parts[:, 1].reshape(256, width)


def wide_product(y, held, panels):
    real_rows, imag_rows = wide_dot(y, held, panels, 0, 512)
    real = real_rows[:, :256] - imag_rows[:, 256:]
    imag = real_rows[:, 256:] + imag_rows[:, :256]
    return real, imag


def small_product(y, held, panels):
    return combine_small(*wide_dot(y, held, panels, 512, 128))


def put_pair(out, real, imag):
    out[:, pl.ds(0, 256)] = real.astype(out.dtype)
    out[:, pl.ds(256, 256)] = imag.astype(out.dtype)


def odd_kernel(s_ref, g0, g1, g2, g3, panel0, panel1, panel2, panel3, out, g_rows, held):
    y, x = s_ref[0], s_ref[1]
    panels = (panel0, panel1, panel2, panel3)
    stack_rows(x, (g0, g1, g2, g3), held)
    g_rows[...] = held[...]
    put_pair(out, *wide_product(y, held, panels))
    out[:, pl.ds(512, 128)] = small_product(y, held, panels).astype(BF)


def odd_second_kernel(s_ref, g_rows, panel0, panel1, panel2, panel3, out):
    put_pair(out, *wide_product(s_ref[0], g_rows, (panel0, panel1, panel2, panel3)))


def even_kernel(s_ref, ca, panel0, panel1, panel2, panel3, source,
                ship, upper_new, source_part, a_rows, c_rows):
    y = s_ref[0]
    panels = (panel0, panel1, panel2, panel3)
    for index in range(4):
        rows = pl.ds(index * 128, 128)
        c_rows[rows, :] = ca[index, 0].reshape(128, 1024)
        a_rows[rows, :] = ca[index, 1].reshape(128, 1024)
    ship[:, pl.ds(512, 128)] = small_product(y, a_rows, panels).astype(BF)
    put_pair(ship, *wide_product(y, a_rows, panels))
    own = pltpu.roll(source[:, pl.ds(512, 128)].astype(F32), 64, 1)
    own = jnp.where(lanes_of(256) < 64, own, 0.0)
    source_part[...] = own - small_product(y, c_rows, panels)
    real, imag = wide_product(y, c_rows, panels)
    put_pair(upper_new, -real, -imag)


def diagonal_kernel(s_ref, c_rows, a_rows, panel0, panel1, panel2, panel3, diagonal, shipped,
                    out, lower):
    real, imag = wide_product(s_ref[0], c_rows, (panel0, panel1, panel2, panel3))
    real = diagonal[:, pl.ds(0, 256)].astype(F32) - real - shipped[:, pl.ds(0, 256)].astype(F32)
    imag = diagonal[:, pl.ds(256, 256)].astype(F32) - imag - shipped[:, pl.ds(256, 256)].astype(F32)
    put_pair(out, real, imag)
    real, imag = wide_product(s_ref[0], a_rows, (panel0, panel1, panel2, panel3))
    put_pair(lower, -real, -imag)


def pair_kernel(s_ref, lower, upper, out):
    out[:, pl.ds(0, 512)] = lower[...]
    out[:, pl.ds(512, 512)] = upper[...]


def block_product(block, right):
    real = jnp.dot(block[:, pl.ds(0, 256)], right, preferred_element_type=F32)
    imag = jnp.dot(block[:, pl.ds(256, 256)], right, preferred_element_type=F32)
    return real, imag


def put_partial(g_ref, right, own, send, whole):
    for index in range(4):
        total = jnp.dot(g_ref[index].reshape(512, 256), right, preferred_element_type=F32)
        parts = total.reshape(4, 2, 64, 128)
        value = combine_small(parts[:, 0].reshape(256, 128), parts[:, 1].reshape(256, 128))
        value = value.reshape(4, 64, 128)
        for group in range(4):
            whole[pl.ds(group * 256 + index * 64, 64), :] = value[group]
    total = packed(whole[...])
    own[...] = total
    send[...] = total.astype(BF)


def source_kernel(s_ref, g_ref, source_part, shipped, source_new, own, send, whole):
    source = (source_part[...] - shipped[:, pl.ds(512, 128)].astype(F32)).astype(BF)
    source_new[...] = source
    put_partial(g_ref, source, own, send, whole)


def summed(own, got):
    total = own[...]
    for other in got:
        total = total + other[...].astype(F32)
    return total


def turn_kernel(s_ref, own, got1, got2, got3, *refs, first):
    solved = None if first else refs[0]
    blocks, refs = refs[:4] if first else refs[1:5], refs[4:] if first else refs[5:]
    source, g_ref, out, own_new, send, vector, whole = refs
    x = s_ref[1]
    total = summed(own, (got1, got2, got3))
    if not first:
        total = solved[...].astype(F32) + total
    out[...] = total.astype(BF)
    low, high = halves(out[...].astype(F32))
    vector[pl.ds(0, 512), :] = low.astype(BF)
    vector[pl.ds(512, 512), :] = high.astype(BF)
    real_rows = imag_rows = None
    for shift, block in enumerate(blocks):
        real, imag = block_product(block, vector[at(mod4(x - shift), 256), :])
        real_rows = real if real_rows is None else real_rows + real
        imag_rows = imag if imag_rows is None else imag_rows + imag
    residue = (source[...].astype(F32) - combine_small(real_rows, imag_rows)).astype(BF)
    put_partial(g_ref, residue, own_new, send, whole)


def last_kernel(s_ref, own, got1, got2, got3, solved, out):
    out[...] = (solved[...].astype(F32) + summed(own, (got1, got2, got3))).astype(BF)


def diagonal_rows_kernel(s_ref, block0, block1, block2, block3, rows_out):
    x = s_ref[1]
    rows = at(x, 64)
    for shift, block in enumerate((block0, block1, block2, block3)):
        cols = at(mod4(x - shift), 256)
        rows_out[0, :, cols] = block[rows, pl.ds(0, 256)]
        rows_out[1, :, cols] = block[rows, pl.ds(256, 256)]


def coupling_rows_kernel(s_ref, pairs, lower_out, upper_out):
    rows = at(s_ref[1], 64)
    for chunk in range(4):
        cols = pl.ds(chunk * 256, 256)
        lower_out[0, :, cols] = pairs[chunk, rows, pl.ds(0, 256)]
        lower_out[1, :, cols] = pairs[chunk, rows, pl.ds(256, 256)]
        upper_out[0, :, cols] = pairs[chunk, rows, pl.ds(512, 256)]
        upper_out[1, :, cols] = pairs[chunk, rows, pl.ds(768, 256)]


def coupled(pairs, start, neighbour):
    parts = []
    for half in range(2):
        real_rows = imag_rows = None
        for index in range(2):
            block = pairs.at[half * 2 + index, :, pl.ds(start, 512)]
            real, imag = block_product(block, neighbour[pl.ds(index * 256, 256), :])
            real_rows = real if real_rows is None else real_rows + real
            imag_rows = imag if imag_rows is None else imag_rows + imag
        parts.append((real_rows, imag_rows))
    real_rows = parts[0][0] + pltpu.roll(parts[1][0], 64, 1)
    imag_rows = parts[0][1] + pltpu.roll(parts[1][1], 64, 1)
    return combine_small(real_rows, imag_rows)


def couple_kernel(s_ref, pairs, source, solved, below, above, out0, out1, out2, out3, held):
    y, x = s_ref[0], s_ref[1]
    combined = source[...].astype(F32) - coupled(pairs, 0, below) - coupled(pairs, 512, above)
    rows = pl.ds(pl.multiple_of(lax.rem(y, 2) * 256, 256), 256)
    moved = pltpu.roll(solved[rows, :].astype(F32), jnp.where(y < 2, 64, 0), 1)
    held[...] = jnp.where(lanes_of(256) < 64, combined, moved)
    for shift, out in enumerate((out0, out1, out2, out3)):
        out[...] = held[at(mod4(x + shift), 64), :]


def spread_kernel(s_ref, piece0, piece1, piece2, piece3, combined, solved):
    x = s_ref[1]
    lane = lanes_of(64)
    totals = [jnp.zeros((64, 128), F32) for _ in range(4)]
    for shift, piece in enumerate((piece0, piece1, piece2, piece3)):
        chunk = mod4(x - shift)
        value = piece[...]
        on = (lane >= chunk * 32) & (lane < chunk * 32 + 32)
        for place in range(4):
            turned = pltpu.roll(value, mod4(chunk - place) * 32, 1)
            totals[place] = jnp.where(on, turned, totals[place])
    combined[0] = totals[0]
    combined[1] = totals[1]
    solved[0] = totals[2]
    solved[1] = totals[3]


def moved_x(block, by):
    pairs = [(y * 4 + x, y * 4 + (x + by) % 4) for y in range(4) for x in range(4)]
    return lax.ppermute(block, "row", pairs)


def moved_y(block, by):
    pairs = [(y * 4 + x, ((y + by) % 4) * 4 + x) for y in range(4) for x in range(4)]
    return lax.ppermute(block, "row", pairs)


def gathered_y(block):
    return (block, moved_y(block, 3), moved_y(block, 2), moved_y(block, 1))


def gathered_x(block):
    groups = [[y * 4 + x for x in range(4)] for y in range(4)]
    return lax.all_gather(block, "row", axis_index_groups=groups)


def along_cuts(block, by):
    count = lax.axis_size("cuts")
    pairs = [(i, i + by) for i in range(count) if 0 <= i + by < count]
    return lax.ppermute(block, "cuts", pairs)


def body(diagonal_blocks, diagonal_inverses, lower_blocks, upper_blocks, injection, orbitals):
    cut = lax.axis_index("cuts")
    place = lax.axis_index("row")
    zero = jnp.zeros((1,), jnp.int32)
    window = lax.dynamic_slice_in_dim(jnp.concatenate([zero, orbitals, zero]), 2 * cut, 4)
    scalars = jnp.concatenate([jnp.stack([place // 4, place % 4]).astype(jnp.int32), window])
    turns = (1, 2, 3)
    after = lax.optimization_barrier
    wide_flops = 2 * 512 * 1024 * 512
    solve_flops = 2 * 2048 * 256 * 128

    *pieces, a_even, c_even, g0, g1, g2, g3 = call(
        prepare_kernel,
        [shape((64, 1664))] * 4 + [shape((2, 64, 1024))] * 2 + [shape((2, 64, 256))] * 4,
        0,
        scalars, diagonal_blocks, diagonal_inverses, lower_blocks, upper_blocks, injection,
        hbm=5, mib=60,
        scratch=[pltpu.VMEM((2, 64, 1024), BF)] * 3
        + [pltpu.VMEM((2, 2, 64, 128), BF)]
        + [pltpu.VMEM((2, 64, 1024), BF)] * 3
        + [pltpu.SemaphoreType.DMA((10,))],
    )
    pieces = [pieces[0]] + [moved_x(pieces[by], by) for by in turns]
    a_next = along_cuts(a_even, -1)
    a_next, g_odd, g1, g2, g3, *pieces = after(
        (a_next, diagonal_inverses[1], g1, g2, g3, *pieces)
    )
    couplings = gathered_x(jnp.stack([c_even, a_next]))
    g_pieces = [g0] + [moved_y(piece, by) for by, piece in zip(turns, (g1, g2, g3))]
    panel, panel_a, diagonal = call(
        assemble_kernel,
        [shape((256, 640)), shape((256, 512)), shape((256, 512))],
        0, scalars, *pieces,
    )
    panels = gathered_y(panel)
    g_blocks = [g_odd] + [moved_x(g_odd, by) for by in turns]
    panel_a, *panels_and = after((panel_a, *panels, *g_pieces))
    panels, g_pieces = panels_and[:4], panels_and[4:]
    (g_columns,) = call(columns_kernel, [shape((4, 2, 64, 256))], 0, scalars, *g_pieces)
    panels_a = gathered_y(panel_a)
    first, g_rows = call(
        odd_kernel, [shape((256, 640)), shape((512, 1024))], wide_flops,
        scalars, *g_blocks, *panels, scratch=[pltpu.VMEM((512, 1024), BF)],
    )
    firsts = gathered_y(first)
    (second,) = call(
        odd_second_kernel, [shape((256, 512))], wide_flops, scalars, g_rows, *panels_a
    )
    seconds = gathered_y(second)
    ship, upper_new, source_part, a_rows, c_rows = call(
        even_kernel,
        [shape((256, 640)), shape((256, 512)), shape((256, 128), F32), shape((512, 1024)),
         shape((512, 1024))],
        2 * wide_flops,
        scalars, couplings, *firsts, panel,
    )
    shipped = along_cuts(ship, 1)
    g_columns = gathered_x(g_columns)
    shipped, *seconds = after((shipped, *seconds))
    diagonal_new, ship_lower = call(
        diagonal_kernel, [shape((256, 512))] * 2, 2 * wide_flops,
        scalars, c_rows, a_rows, *seconds, diagonal, shipped,
    )
    source_part, diagonal_new = after((source_part, diagonal_new))
    diagonals = [diagonal_new] + [moved_x(diagonal_new, by) for by in turns]
    packed_shapes = [shape((512, 128), F32), shape((512, 128))]
    whole = pltpu.VMEM((1024, 128), F32)
    vector = pltpu.VMEM((1024, 128), BF)
    source, own, send = call(
        source_kernel, [shape((256, 128))] + packed_shapes, solve_flops,
        scalars, g_columns, source_part, shipped, scratch=[whole],
    )
    lower_new = along_cuts(ship_lower, 1)
    got = gathered_y(send)[1:]
    lower_new, *both = after((lower_new, *diagonals, *got))
    diagonals, got = both[:4], both[4:]
    (pair,) = call(pair_kernel, [shape((256, 1024))], 0, scalars, lower_new, upper_new)
    pairs = gathered_x(pair)
    solved = ()
    for turn in range(REFINE):
        *solved, own, send = call(
            functools.partial(turn_kernel, first=turn == 0),
            [shape((512, 128))] + packed_shapes, 2 * solve_flops,
            scalars, own, *got, *solved, *diagonals, source, g_columns,
            scratch=[vector, whole],
        )
        got = gathered_y(send)[1:]
    (solved,) = call(
        last_kernel, [shape((512, 128))], 0,
        scalars, own, *got, *solved,
    )
    below, above = along_cuts(solved, 1), along_cuts(solved, -1)
    (diagonal_rows,) = call(
        diagonal_rows_kernel, [shape((2, 64, 1024))], 0, scalars, *diagonals
    )
    lower_rows, upper_rows = call(
        coupling_rows_kernel, [shape((2, 64, 1024))] * 2, 0, scalars, pairs
    )
    ends = call(
        couple_kernel, [shape((64, 128), F32)] * 4, solve_flops // 2,
        scalars, pairs, source, solved, below, above,
        scratch=[pltpu.VMEM((256, 128), F32)],
    )
    ends = [ends[0]] + [moved_x(ends[by], by) for by in turns]
    combined, solved_rows = call(
        spread_kernel, [shape((2, 64, 128), F32)] * 2, 0, scalars, *ends
    )
    return (
        diagonal_rows[None],
        lower_rows[None],
        upper_rows[None],
        combined[None],
        solved_rows[None],
    )


def solution(mesh):
    split = P("cuts", None, "row", None)
    return jax.shard_map(
        body,
        mesh=mesh,
        in_specs=(split, split, split, split, split, P()),
        out_specs=(split,) * 5,
        check_vma=False,
    )
```

```python
import functools

import jax
import jax.numpy as jnp
from jax import lax
from jax.experimental import pallas as pl
from jax.experimental.pallas import tpu as pltpu
from jax.sharding import PartitionSpec as P

REFINE = 2
BF = jnp.bfloat16
F32 = jnp.float32
VMEM = pl.BlockSpec(memory_space=pltpu.VMEM)
MIB = 16
SMEM = pl.BlockSpec(memory_space=pltpu.SMEM)


def call(kernel, out_shapes, flops, *args, scratch=(), hbm=0, mib=MIB, hbm_out=False):
    moved = sum(a.size * a.dtype.itemsize for a in args) + sum(
        s.size * s.dtype.itemsize for s in out_shapes
    )
    anywhere = pl.BlockSpec(memory_space=pl.ANY)
    return pl.pallas_call(
        kernel,
        out_shape=tuple(out_shapes),
        in_specs=[SMEM] + [anywhere] * hbm + [VMEM] * (len(args) - 1 - hbm),
        out_specs=tuple([anywhere if hbm_out else VMEM] * len(out_shapes)),
        scratch_shapes=list(scratch),
        compiler_params=pltpu.CompilerParams(vmem_limit_bytes=mib * 1024 * 1024),
        cost_estimate=pl.CostEstimate(flops=0, bytes_accessed=moved, transcendentals=0),
    )(*args)


def shape(dims, dtype=BF):
    return jax.ShapeDtypeStruct(dims, dtype)


def mod4(v):
    return lax.rem(v + 8, 4)


def at(chunk, size):
    return pl.ds(pl.multiple_of(chunk * size, size), size)


def lanes_of(rows):
    return lax.broadcasted_iota(jnp.int32, (rows, 128), 1)


def combine_small(real_rows, imag_rows):
    lane = lanes_of(real_rows.shape[0])
    turned = jnp.where(lane < 32, -pltpu.roll(imag_rows, 96, 1), pltpu.roll(imag_rows, 32, 1))
    return jnp.where(lane < 64, real_rows + turned, 0.0)


def packed(block):
    half = block.shape[0] // 2
    return jnp.where(lanes_of(half) < 64, block[:half], pltpu.roll(block[half:], 64, 1))


def halves(block):
    return block, pltpu.roll(block, 64, 1)


def masked(block, first_row, rows_on, chunk, cols_on):
    row = first_row + lax.broadcasted_iota(jnp.int32, (64, 256), 0)
    col = chunk * 256 + lax.broadcasted_iota(jnp.int32, (64, 256), 1)
    return jnp.where((row < rows_on) & (col < cols_on), block.astype(F32), 0.0).astype(BF)


def prepare_kernel(s_ref, d_hbm, g_hbm, a_hbm, c_hbm, b_hbm, piece0, piece1, piece2, piece3,
                   a_even, c_even, g0, g1, g2, g3, g_odd,
                   d_ref, a_ref, c_ref, b_ref, a_first, c_first, g_first, sems):
    y, x = s_ref[0], s_ref[1]
    first_row = (y * 4 + x) * 64
    before, own, odd, after = s_ref[2], s_ref[3], s_ref[4], s_ref[5]
    copies = [
        pltpu.make_async_copy(source, target, sems.at[index])
        for index, (source, target) in enumerate(
            (
                (c_hbm.at[1, 0], c_ref.at[0]),
                (c_hbm.at[1, 1], c_ref.at[1]),
                (b_hbm, b_ref),
                (a_hbm.at[1, 0], a_ref.at[0]),
                (a_hbm.at[1, 1], a_ref.at[1]),
                (d_hbm.at[0, 0], d_ref.at[0]),
                (d_hbm.at[0, 1], d_ref.at[1]),
                (a_hbm.at[0], a_first),
                (c_hbm.at[0], c_first),
                (g_hbm.at[0], g_first),
                (g_hbm.at[1], g_odd),
            )
        )
    ]
    for copy in copies:
        copy.start()
    pieces = (piece0, piece1, piece2, piece3)
    row_b = first_row + lax.broadcasted_iota(jnp.int32, (64, 128), 0)
    lane = lanes_of(64)
    copies[0].wait()
    copies[1].wait()
    for shift, piece in enumerate(pieces):
        chunk = mod4(x + shift)
        for part in range(2):
            piece[:, pl.ds(part * 256, 256)] = masked(
                c_ref[part, :, at(chunk, 256)], first_row, odd, chunk, after
            )
    copies[2].wait()
    blocks = [
        jnp.where(row_b < rows_on, b_ref[which, part].astype(F32), 0.0)
        for which, part, rows_on in ((1, 0, odd), (1, 1, odd), (0, 0, own), (0, 1, own))
    ]
    for shift, piece in enumerate(pieces):
        chunk = mod4(x + shift)
        tile = jnp.zeros((64, 128), F32)
        for place, block in enumerate(blocks):
            turned = pltpu.roll(block, mod4(place - chunk) * 32, 1)
            tile = jnp.where((lane >= place * 32) & (lane < place * 32 + 32), turned, tile)
        piece[:, pl.ds(512, 128)] = tile.astype(BF)
    copies[3].wait()
    copies[4].wait()
    for shift, piece in enumerate(pieces):
        chunk = mod4(x + shift)
        for part in range(2):
            piece[:, pl.ds(640 + part * 256, 256)] = masked(
                a_ref[part, :, at(chunk, 256)], first_row, odd, chunk, own
            )
    copies[5].wait()
    copies[6].wait()
    for shift, piece in enumerate(pieces):
        chunk = mod4(x + shift)
        for part in range(2):
            piece[:, pl.ds(1152 + part * 256, 256)] = d_ref[part, :, at(chunk, 256)]
    copies[7].wait()
    copies[8].wait()
    for chunk in range(4):
        cols = pl.ds(chunk * 256, 256)
        for part in range(2):
            a_even[part, :, cols] = masked(a_first[part, :, cols], first_row, own, chunk, before)
            c_even[part, :, cols] = masked(c_first[part, :, cols], first_row, own, chunk, odd)
    copies[9].wait()
    for shift, piece in enumerate((g0, g1, g2, g3)):
        for part in range(2):
            piece[part] = g_first[part, :, at(mod4(y + shift), 256)]
    copies[10].wait()


def assemble_kernel(s_ref, piece0, piece1, piece2, piece3, c_even, a_next, g0, g1, g2, g3,
                    panel, panel_a, diagonal, couplings, g_columns, sems):
    y, x = s_ref[0], s_ref[1]
    moves = []
    for shift, piece in enumerate((piece0, piece1, piece2, piece3)):
        rows = at(mod4(x - shift), 64)
        moves.append((piece.at[:, pl.ds(0, 640)], panel.at[rows, :]))
        moves.append((piece.at[:, pl.ds(640, 512)], panel_a.at[rows, :]))
        moves.append((piece.at[:, pl.ds(1152, 512)], diagonal.at[rows, :]))
    moves.append((c_even, couplings.at[0]))
    moves.append((a_next, couplings.at[1]))
    for shift, piece in enumerate((g0, g1, g2, g3)):
        moves.append((piece, g_columns.at[mod4(y - shift)]))
    copies = [
        pltpu.make_async_copy(source, target, sems.at[index])
        for index, (source, target) in enumerate(moves)
    ]
    for copy in copies:
        copy.start()
    for copy in copies:
        copy.wait()


def stack_rows(x, blocks, held):
    for shift, block in enumerate(blocks):
        held[at(mod4(x - shift), 128), :] = block[...].reshape(128, 1024)


def wide_dot(y, held, panels, start, width):
    total = None
    for place, panel in enumerate(panels):
        term = jnp.dot(
            held[:, at(mod4(y + place), 256)],
            panel[:, pl.ds(start, width)],
            preferred_element_type=F32,
        )
        total = term if total is None else total + term
    parts = total.reshape(4, 2, 64, width)
    return parts[:, 0].reshape(256, width), parts[:, 1].reshape(256, width)


def wide_product(y, held, panels):
    real_rows, imag_rows = wide_dot(y, held, panels, 0, 512)
    real = real_rows[:, :256] - imag_rows[:, 256:]
    imag = real_rows[:, 256:] + imag_rows[:, :256]
    return real, imag


def small_product(y, held, panels):
    return combine_small(*wide_dot(y, held, panels, 512, 128))


def put_pair(out, real, imag):
    out[:, pl.ds(0, 256)] = real.astype(out.dtype)
    out[:, pl.ds(256, 256)] = imag.astype(out.dtype)


def odd_kernel(s_ref, g_ref, panel0, panel1, panel2, panel3, out, held):
    y = s_ref[0]
    panels = (panel0, panel1, panel2, panel3)
    held[...] = g_ref[...].reshape(512, 1024)
    put_pair(out, *wide_product(y, held, panels))
    out[:, pl.ds(512, 128)] = small_product(y, held, panels).astype(BF)


def odd_second_kernel(s_ref, g_ref, panel0, panel1, panel2, panel3, out, held):
    held[...] = g_ref[...].reshape(512, 1024)
    put_pair(out, *wide_product(s_ref[0], held, (panel0, panel1, panel2, panel3)))


def even_kernel(s_ref, ca0, ca1, ca2, ca3, panel0, panel1, panel2, panel3, source,
                ship, upper_new, source_part, a_rows, c_rows):
    y, x = s_ref[0], s_ref[1]
    panels = (panel0, panel1, panel2, panel3)
    stack_rows(x, [block.at[0] for block in (ca0, ca1, ca2, ca3)], c_rows)
    stack_rows(x, [block.at[1] for block in (ca0, ca1, ca2, ca3)], a_rows)
    ship[:, pl.ds(512, 128)] = small_product(y, a_rows, panels).astype(BF)
    put_pair(ship, *wide_product(y, a_rows, panels))
    own = pltpu.roll(source[:, pl.ds(512, 128)].astype(F32), 64, 1)
    own = jnp.where(lanes_of(256) < 64, own, 0.0)
    source_part[...] = own - small_product(y, c_rows, panels)
    real, imag = wide_product(y, c_rows, panels)
    put_pair(upper_new, -real, -imag)


def diagonal_kernel(s_ref, c_rows, a_rows, panel0, panel1, panel2, panel3, diagonal, shipped,
                    out, lower):
    real, imag = wide_product(s_ref[0], c_rows, (panel0, panel1, panel2, panel3))
    real = diagonal[:, pl.ds(0, 256)].astype(F32) - real - shipped[:, pl.ds(0, 256)].astype(F32)
    imag = diagonal[:, pl.ds(256, 256)].astype(F32) - imag - shipped[:, pl.ds(256, 256)].astype(F32)
    put_pair(out, real, imag)
    real, imag = wide_product(s_ref[0], a_rows, (panel0, panel1, panel2, panel3))
    put_pair(lower, -real, -imag)


def pair_kernel(s_ref, lower, upper, out):
    out[:, pl.ds(0, 512)] = lower[...]
    out[:, pl.ds(512, 512)] = upper[...]


def block_product(block, right):
    real = jnp.dot(block[:, pl.ds(0, 256)], right, preferred_element_type=F32)
    imag = jnp.dot(block[:, pl.ds(256, 256)], right, preferred_element_type=F32)
    return real, imag


def put_partial(g_ref, right, own, send, whole):
    for index in range(4):
        total = jnp.dot(g_ref[index].reshape(512, 256), right, preferred_element_type=F32)
        parts = total.reshape(4, 2, 64, 128)
        value = combine_small(parts[:, 0].reshape(256, 128), parts[:, 1].reshape(256, 128))
        value = value.reshape(4, 64, 128)
        for group in range(4):
            whole[pl.ds(group * 256 + index * 64, 64), :] = value[group]
    total = packed(whole[...])
    own[...] = total
    send[...] = total.astype(BF)


def source_kernel(s_ref, g_ref, source_part, shipped, source_new, own, send, whole):
    source = (source_part[...] - shipped[:, pl.ds(512, 128)].astype(F32)).astype(BF)
    source_new[...] = source
    put_partial(g_ref, source, own, send, whole)


def summed(own, got):
    total = own[...]
    for other in got:
        total = total + other[...].astype(F32)
    return total


def turn_kernel(s_ref, own, got1, got2, got3, *refs, first):
    solved = None if first else refs[0]
    blocks, refs = refs[:4] if first else refs[1:5], refs[4:] if first else refs[5:]
    source, g_ref, out, own_new, send, vector, whole = refs
    x = s_ref[1]
    total = summed(own, (got1, got2, got3))
    if not first:
        total = solved[...].astype(F32) + total
    out[...] = total.astype(BF)
    unpack(out, vector)
    residue = (source[...].astype(F32) - blocks_product(x, blocks, vector)).astype(BF)
    put_partial(g_ref, residue, own_new, send, whole)


def last_kernel(s_ref, own, got1, got2, got3, solved, out):
    out[...] = (solved[...].astype(F32) + summed(own, (got1, got2, got3))).astype(BF)


def diagonal_rows_kernel(s_ref, block0, block1, block2, block3, rows_out):
    x = s_ref[1]
    rows = at(x, 64)
    for shift, block in enumerate((block0, block1, block2, block3)):
        cols = at(mod4(x - shift), 256)
        rows_out[0, :, cols] = block[rows, pl.ds(0, 256)]
        rows_out[1, :, cols] = block[rows, pl.ds(256, 256)]


def coupling_rows_kernel(s_ref, pair0, pair1, pair2, pair3, lower_out, upper_out):
    x = s_ref[1]
    rows = at(x, 64)
    for shift, pair in enumerate((pair0, pair1, pair2, pair3)):
        cols = at(mod4(x - shift), 256)
        lower_out[0, :, cols] = pair[rows, pl.ds(0, 256)]
        lower_out[1, :, cols] = pair[rows, pl.ds(256, 256)]
        upper_out[0, :, cols] = pair[rows, pl.ds(512, 256)]
        upper_out[1, :, cols] = pair[rows, pl.ds(768, 256)]


def unpack(solved, vector):
    low, high = halves(solved[...].astype(F32))
    vector[pl.ds(0, 512), :] = low.astype(BF)
    vector[pl.ds(512, 512), :] = high.astype(BF)


def blocks_product(x, blocks, vector):
    real_rows = imag_rows = None
    for shift, block in enumerate(blocks):
        real, imag = block_product(block, vector[at(mod4(x - shift), 256), :])
        real_rows = real if real_rows is None else real_rows + real
        imag_rows = imag if imag_rows is None else imag_rows + imag
    return combine_small(real_rows, imag_rows)


def couple_kernel(s_ref, pair0, pair1, pair2, pair3, source, solved, below, above,
                  out0, out1, out2, out3, held, vector):
    y, x = s_ref[0], s_ref[1]
    pairs = (pair0, pair1, pair2, pair3)
    unpack(below, vector)
    combined = source[...].astype(F32)
    combined = combined - blocks_product(x, [p.at[:, pl.ds(0, 512)] for p in pairs], vector)
    unpack(above, vector)
    combined = combined - blocks_product(x, [p.at[:, pl.ds(512, 512)] for p in pairs], vector)
    rows = pl.ds(pl.multiple_of(lax.rem(y, 2) * 256, 256), 256)
    moved = pltpu.roll(solved[rows, :].astype(F32), jnp.where(y < 2, 64, 0), 1)
    held[...] = jnp.where(lanes_of(256) < 64, combined, moved)
    for shift, out in enumerate((out0, out1, out2, out3)):
        out[...] = held[at(mod4(x + shift), 64), :]


def spread_kernel(s_ref, piece0, piece1, piece2, piece3, combined, solved):
    x = s_ref[1]
    lane = lanes_of(64)
    totals = [jnp.zeros((64, 128), F32) for _ in range(4)]
    for shift, piece in enumerate((piece0, piece1, piece2, piece3)):
        chunk = mod4(x - shift)
        value = piece[...]
        on = (lane >= chunk * 32) & (lane < chunk * 32 + 32)
        for place in range(4):
            turned = pltpu.roll(value, mod4(chunk - place) * 32, 1)
            totals[place] = jnp.where(on, turned, totals[place])
    combined[0] = totals[0]
    combined[1] = totals[1]
    solved[0] = totals[2]
    solved[1] = totals[3]


def moved_x(block, by):
    pairs = [(y * 4 + x, y * 4 + (x + by) % 4) for y in range(4) for x in range(4)]
    return lax.ppermute(block, "row", pairs)


def moved_y(block, by):
    pairs = [(y * 4 + x, ((y + by) % 4) * 4 + x) for y in range(4) for x in range(4)]
    return lax.ppermute(block, "row", pairs)


def gathered_y(block):
    return (block, moved_y(block, 3), moved_y(block, 2), moved_y(block, 1))


def gathered_x(block):
    groups = [[y * 4 + x for x in range(4)] for y in range(4)]
    return lax.all_gather(block, "row", axis_index_groups=groups)


def along_cuts(block, by):
    count = lax.axis_size("cuts")
    pairs = [(i, i + by) for i in range(count) if 0 <= i + by < count]
    return lax.ppermute(block, "cuts", pairs)


def body(diagonal_blocks, diagonal_inverses, lower_blocks, upper_blocks, injection, orbitals):
    cut = lax.axis_index("cuts")
    place = lax.axis_index("row")
    zero = jnp.zeros((1,), jnp.int32)
    window = lax.dynamic_slice_in_dim(jnp.concatenate([zero, orbitals, zero]), 2 * cut, 4)
    scalars = jnp.concatenate([jnp.stack([place // 4, place % 4]).astype(jnp.int32), window])
    turns = (1, 2, 3)
    after = lax.optimization_barrier
    wide_flops = 2 * 512 * 1024 * 512
    solve_flops = 2 * 2048 * 256 * 128

    *pieces, a_even, c_even, g0, g1, g2, g3, g_odd = call(
        prepare_kernel,
        [shape((64, 1664))] * 4 + [shape((2, 64, 1024))] * 2 + [shape((2, 64, 256))] * 4
        + [shape((2, 64, 1024))],
        0,
        scalars, diagonal_blocks, diagonal_inverses, lower_blocks, upper_blocks, injection,
        hbm=5, mib=60,
        scratch=[pltpu.VMEM((2, 64, 1024), BF)] * 3
        + [pltpu.VMEM((2, 2, 64, 128), BF)]
        + [pltpu.VMEM((2, 64, 1024), BF)] * 3
        + [pltpu.SemaphoreType.DMA((11,))],
    )
    g_rows = gathered_x(g_odd)
    pieces = [pieces[0]] + [moved_x(pieces[by], by) for by in turns]
    a_next = along_cuts(a_even, -1)
    g1, g2, g3 = [moved_y(piece, by) for by, piece in zip(turns, (g1, g2, g3))]
    a_next, g1, g2, g3, *pieces = after((a_next, g1, g2, g3, *pieces))
    panel, panel_a, diagonal, couplings, g_columns = call(
        assemble_kernel,
        [shape((256, 640)), shape((256, 512)), shape((256, 512)), shape((2, 2, 64, 1024)),
         shape((4, 2, 64, 256))],
        0, scalars, *pieces, c_even, a_next, g0, g1, g2, g3,
        hbm=10, hbm_out=True, mib=MIB, scratch=[pltpu.SemaphoreType.DMA((18,))],
    )
    g_columns = gathered_x(g_columns)
    panels = gathered_y(panel)
    ca_blocks = [couplings] + [moved_x(couplings, by) for by in turns]
    panel_a, *panels = after((panel_a, *panels))
    panels_a = gathered_y(panel_a)
    rows_held = pltpu.VMEM((512, 1024), BF)
    (first,) = call(
        odd_kernel, [shape((256, 640))], wide_flops,
        scalars, g_rows, *panels, scratch=[rows_held],
    )
    first, *ca_blocks = after((first, *ca_blocks))
    firsts = gathered_y(first)
    (second,) = call(
        odd_second_kernel, [shape((256, 512))], wide_flops, scalars, g_rows, *panels_a,
        scratch=[rows_held],
    )
    seconds = gathered_y(second)
    firsts = after((second, *firsts))[1:]
    ship, upper_new, source_part, a_rows, c_rows = call(
        even_kernel,
        [shape((256, 640)), shape((256, 512)), shape((256, 128), F32), shape((512, 1024)),
         shape((512, 1024))],
        2 * wide_flops,
        scalars, *ca_blocks, *firsts, panel,
    )
    shipped = along_cuts(ship, 1)
    diagonal_new, ship_lower = call(
        diagonal_kernel, [shape((256, 512))] * 2, 2 * wide_flops,
        scalars, c_rows, a_rows, *seconds, diagonal, shipped,
    )
    diagonals = [diagonal_new] + [moved_x(diagonal_new, by) for by in turns]
    packed_shapes = [shape((512, 128), F32), shape((512, 128))]
    whole = pltpu.VMEM((1024, 128), F32)
    vector = pltpu.VMEM((1024, 128), BF)
    source, own, send = call(
        source_kernel, [shape((256, 128))] + packed_shapes, solve_flops,
        scalars, g_columns, source_part, shipped, scratch=[whole],
    )
    lower_new = along_cuts(ship_lower, 1)
    got = gathered_y(send)[1:]
    lower_new, *both = after((lower_new, *diagonals, *got))
    diagonals, got = both[:4], both[4:]
    (pair,) = call(pair_kernel, [shape((256, 1024))], 0, scalars, lower_new, upper_new)
    pairs = [pair] + [moved_x(pair, by) for by in turns]
    solved = ()
    for turn in range(REFINE):
        *solved, own, send = call(
            functools.partial(turn_kernel, first=turn == 0),
            [shape((512, 128))] + packed_shapes, 2 * solve_flops,
            scalars, own, *got, *solved, *diagonals, source, g_columns,
            scratch=[vector, whole],
        )
        got = gathered_y(send)[1:]
    (solved,) = call(
        last_kernel, [shape((512, 128))], 0,
        scalars, own, *got, *solved,
    )
    below, above = along_cuts(solved, 1), along_cuts(solved, -1)
    (diagonal_rows,) = call(
        diagonal_rows_kernel, [shape((2, 64, 1024))], 0, scalars, *diagonals
    )
    lower_rows, upper_rows = call(
        coupling_rows_kernel, [shape((2, 64, 1024))] * 2, 0, scalars, *pairs
    )
    ends = call(
        couple_kernel, [shape((64, 128), F32)] * 4, solve_flops // 2,
        scalars, *pairs, source, solved, below, above,
        scratch=[pltpu.VMEM((256, 128), F32), vector],
    )
    ends = [ends[0]] + [moved_x(ends[by], by) for by in turns]
    combined, solved_rows = call(
        spread_kernel, [shape((2, 64, 128), F32)] * 2, 0, scalars, *ends
    )
    return (
        diagonal_rows[None],
        lower_rows[None],
        upper_rows[None],
        combined[None],
        solved_rows[None],
    )


def solution(mesh):
    split = P("cuts", None, "row", None)
    return jax.shard_map(
        body,
        mesh=mesh,
        in_specs=(split, split, split, split, split, P()),
        out_specs=(split,) * 5,
        check_vma=False,
    )
```

```python
import functools

import jax
import jax.numpy as jnp
from jax import lax
from jax.experimental import pallas as pl
from jax.experimental.pallas import tpu as pltpu
from jax.sharding import PartitionSpec as P

REFINE = 2
BF = jnp.bfloat16
F32 = jnp.float32
VMEM = pl.BlockSpec(memory_space=pltpu.VMEM)
MIB = 24
SMEM = pl.BlockSpec(memory_space=pltpu.SMEM)


def call(kernel, out_shapes, flops, *args, scratch=(), hbm=0, mib=MIB, hbm_out=False):
    moved = sum(a.size * a.dtype.itemsize for a in args) + sum(
        s.size * s.dtype.itemsize for s in out_shapes
    )
    anywhere = pl.BlockSpec(memory_space=pl.ANY)
    return pl.pallas_call(
        kernel,
        out_shape=tuple(out_shapes),
        in_specs=[SMEM] + [anywhere] * hbm + [VMEM] * (len(args) - 1 - hbm),
        out_specs=tuple([anywhere if hbm_out else VMEM] * len(out_shapes)),
        scratch_shapes=list(scratch),
        compiler_params=pltpu.CompilerParams(vmem_limit_bytes=mib * 1024 * 1024),
        cost_estimate=pl.CostEstimate(flops=0, bytes_accessed=moved, transcendentals=0),
    )(*args)


def shape(dims, dtype=BF):
    return jax.ShapeDtypeStruct(dims, dtype)


def mod4(v):
    return lax.rem(v + 8, 4)


def at(chunk, size):
    return pl.ds(pl.multiple_of(chunk * size, size), size)


def lanes_of(rows):
    return lax.broadcasted_iota(jnp.int32, (rows, 128), 1)


def combine_small(real_rows, imag_rows):
    lane = lanes_of(real_rows.shape[0])
    turned = jnp.where(lane < 32, -pltpu.roll(imag_rows, 96, 1), pltpu.roll(imag_rows, 32, 1))
    return jnp.where(lane < 64, real_rows + turned, 0.0)


def packed(block):
    half = block.shape[0] // 2
    return jnp.where(lanes_of(half) < 64, block[:half], pltpu.roll(block[half:], 64, 1))


def halves(block):
    return block, pltpu.roll(block, 64, 1)


def masked(block, first_row, rows_on, chunk, cols_on):
    row = first_row + lax.broadcasted_iota(jnp.int32, (64, 256), 0)
    col = chunk * 256 + lax.broadcasted_iota(jnp.int32, (64, 256), 1)
    return jnp.where((row < rows_on) & (col < cols_on), block.astype(F32), 0.0).astype(BF)


def prepare_kernel(s_ref, d_hbm, g_hbm, a_hbm, c_hbm, b_hbm, piece0, piece1, piece2, piece3,
                   a_even, c_even, g0, g1, g2, g3, g_odd,
                   d_ref, a_ref, c_ref, b_ref, a_first, c_first, g_first, sems):
    y, x = s_ref[0], s_ref[1]
    first_row = (y * 4 + x) * 64
    before, own, odd, after = s_ref[2], s_ref[3], s_ref[4], s_ref[5]
    copies = [
        pltpu.make_async_copy(source, target, sems.at[index])
        for index, (source, target) in enumerate(
            (
                (c_hbm.at[1, 0], c_ref.at[0]),
                (c_hbm.at[1, 1], c_ref.at[1]),
                (b_hbm, b_ref),
                (a_hbm.at[1, 0], a_ref.at[0]),
                (a_hbm.at[1, 1], a_ref.at[1]),
                (d_hbm.at[0, 0], d_ref.at[0]),
                (d_hbm.at[0, 1], d_ref.at[1]),
                (a_hbm.at[0], a_first),
                (c_hbm.at[0], c_first),
                (g_hbm.at[0], g_first),
                (g_hbm.at[1], g_odd),
            )
        )
    ]
    for copy in copies:
        copy.start()
    pieces = (piece0, piece1, piece2, piece3)
    row_b = first_row + lax.broadcasted_iota(jnp.int32, (64, 128), 0)
    lane = lanes_of(64)
    copies[0].wait()
    copies[1].wait()
    for shift, piece in enumerate(pieces):
        chunk = mod4(x + shift)
        for part in range(2):
            piece[:, pl.ds(part * 256, 256)] = masked(
                c_ref[part, :, at(chunk, 256)], first_row, odd, chunk, after
            )
    copies[2].wait()
    blocks = [
        jnp.where(row_b < rows_on, b_ref[which, part].astype(F32), 0.0)
        for which, part, rows_on in ((1, 0, odd), (1, 1, odd), (0, 0, own), (0, 1, own))
    ]
    for shift, piece in enumerate(pieces):
        chunk = mod4(x + shift)
        tile = jnp.zeros((64, 128), F32)
        for place, block in enumerate(blocks):
            turned = pltpu.roll(block, mod4(place - chunk) * 32, 1)
            tile = jnp.where((lane >= place * 32) & (lane < place * 32 + 32), turned, tile)
        piece[:, pl.ds(512, 128)] = tile.astype(BF)
    copies[3].wait()
    copies[4].wait()
    for shift, piece in enumerate(pieces):
        chunk = mod4(x + shift)
        for part in range(2):
            piece[:, pl.ds(640 + part * 256, 256)] = masked(
                a_ref[part, :, at(chunk, 256)], first_row, odd, chunk, own
            )
    copies[5].wait()
    copies[6].wait()
    for shift, piece in enumerate(pieces):
        chunk = mod4(x + shift)
        for part in range(2):
            piece[:, pl.ds(1152 + part * 256, 256)] = d_ref[part, :, at(chunk, 256)]
    copies[7].wait()
    copies[8].wait()
    for chunk in range(4):
        cols = pl.ds(chunk * 256, 256)
        for part in range(2):
            a_even[part, :, cols] = masked(a_first[part, :, cols], first_row, own, chunk, before)
            c_even[part, :, cols] = masked(c_first[part, :, cols], first_row, own, chunk, odd)
    copies[9].wait()
    for shift, piece in enumerate((g0, g1, g2, g3)):
        for part in range(2):
            piece[part] = g_first[part, :, at(mod4(y + shift), 256)]
    copies[10].wait()


def assemble_kernel(s_ref, piece0, piece1, piece2, piece3, g0, g1, g2, g3,
                    panel, diagonal, g_columns):
    y, x = s_ref[0], s_ref[1]
    for shift, piece in enumerate((piece0, piece1, piece2, piece3)):
        rows = at(mod4(x - shift), 64)
        panel[rows, :] = piece[:, pl.ds(0, 1152)]
        diagonal[rows, :] = piece[:, pl.ds(1152, 512)]
    for shift, piece in enumerate((g0, g1, g2, g3)):
        g_columns[mod4(y - shift)] = piece[...]


def stack_rows(x, blocks, held):
    for shift, block in enumerate(blocks):
        held[at(mod4(x - shift), 128), :] = block[...].reshape(128, 1024)


def wide_dot(y, held, panels, start, width):
    total = None
    for place, panel in enumerate(panels):
        term = jnp.dot(
            held[:, at(mod4(y + place), 256)],
            panel[pl.ds(0, 256), pl.ds(start, width)],
            preferred_element_type=F32,
        )
        total = term if total is None else total + term
    parts = total.reshape(4, 2, 64, width)
    return parts[:, 0].reshape(256, width), parts[:, 1].reshape(256, width)


def wide_product(y, held, panels, start=0):
    real_rows, imag_rows = wide_dot(y, held, panels, start, 512)
    real = real_rows[:, :256] - imag_rows[:, 256:]
    imag = real_rows[:, 256:] + imag_rows[:, :256]
    return real, imag


def small_product(y, held, panels):
    return combine_small(*wide_dot(y, held, panels, 512, 128))


def put_pair(out, real, imag):
    out[pl.ds(0, 256), pl.ds(0, 256)] = real.astype(out.dtype)
    out[pl.ds(0, 256), pl.ds(256, 256)] = imag.astype(out.dtype)


def odd_kernel(s_ref, g0, g1, g2, g3, panel0, panel1, panel2, panel3, out, out_second, held):
    y, x = s_ref[0], s_ref[1]
    panels = (panel0, panel1, panel2, panel3)
    stack_rows(x, (g0, g1, g2, g3), held)
    put_pair(out, *wide_product(y, held, panels))
    out[:, pl.ds(512, 128)] = small_product(y, held, panels).astype(BF)
    put_pair(out_second, *wide_product(y, held, panels, 640))
    out_second[pl.ds(256, 16), :] = jnp.zeros((16, 512), BF)


def even_kernel(s_ref, a0, a1, a2, a3, c_ref, panel0, panel1, panel2, panel3, source,
                ship, ship_source, upper_new, source_part, a_rows, c_rows):
    y, x = s_ref[0], s_ref[1]
    panels = (panel0, panel1, panel2, panel3)
    stack_rows(x, (a0, a1, a2, a3), a_rows)
    c_rows[...] = c_ref[...].reshape(512, 1024)
    ship_source[...] = small_product(y, a_rows, panels).astype(BF)
    put_pair(ship, *wide_product(y, a_rows, panels))
    own = pltpu.roll(source[:, pl.ds(512, 128)].astype(F32), 64, 1)
    own = jnp.where(lanes_of(256) < 64, own, 0.0)
    source_part[...] = own - small_product(y, c_rows, panels)
    real, imag = wide_product(y, c_rows, panels)
    put_pair(upper_new, -real, -imag)


def diagonal_kernel(s_ref, c_rows, a_rows, panel0, panel1, panel2, panel3, diagonal, shipped,
                    out, lower):
    real, imag = wide_product(s_ref[0], c_rows, (panel0, panel1, panel2, panel3))
    real = diagonal[:, pl.ds(0, 256)].astype(F32) - real - shipped[:, pl.ds(0, 256)].astype(F32)
    imag = diagonal[:, pl.ds(256, 256)].astype(F32) - imag - shipped[:, pl.ds(256, 256)].astype(F32)
    put_pair(out, real, imag)
    real, imag = wide_product(s_ref[0], a_rows, (panel0, panel1, panel2, panel3))
    put_pair(lower, -real, -imag)


def pair_kernel(s_ref, lower, upper, out):
    out[:, pl.ds(0, 512)] = lower[...]
    out[:, pl.ds(512, 512)] = upper[...]


def block_product(block, right):
    real = jnp.dot(block[:, pl.ds(0, 256)], right, preferred_element_type=F32)
    imag = jnp.dot(block[:, pl.ds(256, 256)], right, preferred_element_type=F32)
    return real, imag


def put_partial(g_ref, right, own, send, whole):
    for index in range(4):
        total = jnp.dot(g_ref[index].reshape(512, 256), right, preferred_element_type=F32)
        parts = total.reshape(4, 2, 64, 128)
        value = combine_small(parts[:, 0].reshape(256, 128), parts[:, 1].reshape(256, 128))
        value = value.reshape(4, 64, 128)
        for group in range(4):
            whole[pl.ds(group * 256 + index * 64, 64), :] = value[group]
    total = packed(whole[...])
    own[...] = total
    send[...] = total.astype(BF)


def source_kernel(s_ref, g_ref, source_part, shipped, source_new, own, send, whole):
    source = (source_part[...] - shipped[...].astype(F32)).astype(BF)
    source_new[...] = source
    put_partial(g_ref, source, own, send, whole)


def summed(own, got):
    total = own[...]
    for other in got:
        total = total + other[...].astype(F32)
    return total


def turn_kernel(s_ref, own, got1, got2, got3, *refs, first):
    solved = None if first else refs[0]
    blocks, refs = refs[:4] if first else refs[1:5], refs[4:] if first else refs[5:]
    source, g_ref, out, own_new, send, vector, whole = refs
    x = s_ref[1]
    total = summed(own, (got1, got2, got3))
    if not first:
        total = solved[...].astype(F32) + total
    out[...] = total.astype(BF)
    unpack(out, vector)
    residue = (source[...].astype(F32) - blocks_product(x, blocks, vector)).astype(BF)
    put_partial(g_ref, residue, own_new, send, whole)


def last_kernel(s_ref, own, got1, got2, got3, solved, out):
    out[...] = (solved[...].astype(F32) + summed(own, (got1, got2, got3))).astype(BF)


def diagonal_rows_kernel(s_ref, block0, block1, block2, block3, rows_out):
    x = s_ref[1]
    rows = at(x, 64)
    for shift, block in enumerate((block0, block1, block2, block3)):
        cols = at(mod4(x - shift), 256)
        rows_out[0, :, cols] = block[rows, pl.ds(0, 256)]
        rows_out[1, :, cols] = block[rows, pl.ds(256, 256)]


def coupling_rows_kernel(s_ref, pair0, pair1, pair2, pair3, lower_out, upper_out):
    x = s_ref[1]
    rows = at(x, 64)
    for shift, pair in enumerate((pair0, pair1, pair2, pair3)):
        cols = at(mod4(x - shift), 256)
        lower_out[0, :, cols] = pair[rows, pl.ds(0, 256)]
        lower_out[1, :, cols] = pair[rows, pl.ds(256, 256)]
        upper_out[0, :, cols] = pair[rows, pl.ds(512, 256)]
        upper_out[1, :, cols] = pair[rows, pl.ds(768, 256)]


def unpack(solved, vector):
    low, high = halves(solved[...].astype(F32))
    vector[pl.ds(0, 512), :] = low.astype(BF)
    vector[pl.ds(512, 512), :] = high.astype(BF)


def blocks_product(x, blocks, vector):
    real_rows = imag_rows = None
    for shift, block in enumerate(blocks):
        real, imag = block_product(block, vector[at(mod4(x - shift), 256), :])
        real_rows = real if real_rows is None else real_rows + real
        imag_rows = imag if imag_rows is None else imag_rows + imag
    return combine_small(real_rows, imag_rows)


def couple_kernel(s_ref, pair0, pair1, pair2, pair3, source, solved, below, above,
                  out0, out1, out2, out3, held, vector):
    y, x = s_ref[0], s_ref[1]
    pairs = (pair0, pair1, pair2, pair3)
    unpack(below, vector)
    combined = source[...].astype(F32)
    combined = combined - blocks_product(x, [p.at[:, pl.ds(0, 512)] for p in pairs], vector)
    unpack(above, vector)
    combined = combined - blocks_product(x, [p.at[:, pl.ds(512, 512)] for p in pairs], vector)
    rows = pl.ds(pl.multiple_of(lax.rem(y, 2) * 256, 256), 256)
    moved = pltpu.roll(solved[rows, :].astype(F32), jnp.where(y < 2, 64, 0), 1)
    held[...] = jnp.where(lanes_of(256) < 64, combined, moved)
    for shift, out in enumerate((out0, out1, out2, out3)):
        out[...] = held[at(mod4(x + shift), 64), :]


def spread_kernel(s_ref, piece0, piece1, piece2, piece3, combined, solved):
    x = s_ref[1]
    lane = lanes_of(64)
    totals = [jnp.zeros((64, 128), F32) for _ in range(4)]
    for shift, piece in enumerate((piece0, piece1, piece2, piece3)):
        chunk = mod4(x - shift)
        value = piece[...]
        on = (lane >= chunk * 32) & (lane < chunk * 32 + 32)
        for place in range(4):
            turned = pltpu.roll(value, mod4(chunk - place) * 32, 1)
            totals[place] = jnp.where(on, turned, totals[place])
    combined[0] = totals[0]
    combined[1] = totals[1]
    solved[0] = totals[2]
    solved[1] = totals[3]


def moved_x(block, by):
    pairs = [(y * 4 + x, y * 4 + (x + by) % 4) for y in range(4) for x in range(4)]
    return lax.ppermute(block, "row", pairs)


def moved_y(block, by):
    pairs = [(y * 4 + x, ((y + by) % 4) * 4 + x) for y in range(4) for x in range(4)]
    return lax.ppermute(block, "row", pairs)


def gathered_y(block):
    return (block, moved_y(block, 3), moved_y(block, 2), moved_y(block, 1))


def gathered_x(block):
    groups = [[y * 4 + x for x in range(4)] for y in range(4)]
    return lax.all_gather(block, "row", axis_index_groups=groups)


def along_cuts(block, by):
    count = lax.axis_size("cuts")
    pairs = [(i, i + by) for i in range(count) if 0 <= i + by < count]
    return lax.ppermute(block, "cuts", pairs)


def body(diagonal_blocks, diagonal_inverses, lower_blocks, upper_blocks, injection, orbitals):
    cut = lax.axis_index("cuts")
    place = lax.axis_index("row")
    zero = jnp.zeros((1,), jnp.int32)
    window = lax.dynamic_slice_in_dim(jnp.concatenate([zero, orbitals, zero]), 2 * cut, 4)
    scalars = jnp.concatenate([jnp.stack([place // 4, place % 4]).astype(jnp.int32), window])
    turns = (1, 2, 3)
    after = lax.optimization_barrier
    wide_flops = 2 * 512 * 1024 * 512
    solve_flops = 2 * 2048 * 256 * 128

    *pieces, a_even, c_even, g0, g1, g2, g3, g_odd = call(
        prepare_kernel,
        [shape((64, 1664))] * 4 + [shape((2, 64, 1024))] * 2 + [shape((2, 64, 256))] * 4
        + [shape((2, 64, 1024))],
        0,
        scalars, diagonal_blocks, diagonal_inverses, lower_blocks, upper_blocks, injection,
        hbm=5, mib=52,
        scratch=[pltpu.VMEM((2, 64, 1024), BF)] * 3
        + [pltpu.VMEM((2, 2, 64, 128), BF)]
        + [pltpu.VMEM((2, 64, 1024), BF)] * 3
        + [pltpu.SemaphoreType.DMA((11,))],
    )
    pieces = [pieces[0]] + [moved_x(pieces[by], by) for by in turns]
    c_gathered = gathered_x(c_even)
    a_next = along_cuts(a_even, -1)
    g1, g2, g3 = [moved_y(piece, by) for by, piece in zip(turns, (g1, g2, g3))]
    a_next, g1, g2, g3, g_odd, *pieces = after((a_next, g1, g2, g3, g_odd, *pieces))
    panel, diagonal, g_columns = call(
        assemble_kernel,
        [shape((256, 1152)), shape((256, 512)), shape((4, 2, 64, 256))],
        0, scalars, *pieces, g0, g1, g2, g3,
    )
    g_columns = gathered_x(g_columns)
    panels = gathered_y(panel)
    g_blocks = [g_odd] + [moved_x(g_odd, by) for by in turns]
    a_blocks = [a_next] + [moved_x(a_next, by) for by in turns]
    first, second = call(
        odd_kernel, [shape((256, 640)), shape((272, 512))], wide_flops,
        scalars, *g_blocks, *panels, scratch=[pltpu.VMEM((512, 1024), BF)],
    )
    first, *a_blocks = after((first, *a_blocks))
    firsts = gathered_y(first)
    seconds = gathered_y(second)
    ship, ship_source, upper_new, source_part, a_rows, c_rows = call(
        even_kernel,
        [shape((256, 512)), shape((256, 128)), shape((256, 512)), shape((256, 128), F32),
         shape((512, 1024)),
         shape((512, 1024))],
        2 * wide_flops,
        scalars, *a_blocks, c_gathered, *firsts, panel,
    )
    shipped = along_cuts(ship, 1)
    shipped_source = along_cuts(ship_source, 1)
    diagonal_new, ship_lower = call(
        diagonal_kernel, [shape((256, 512))] * 2, 2 * wide_flops,
        scalars, c_rows, a_rows, *seconds, diagonal, shipped,
    )
    diagonals = [diagonal_new] + [moved_x(diagonal_new, by) for by in turns]
    packed_shapes = [shape((512, 128), F32), shape((512, 128))]
    whole = pltpu.VMEM((1024, 128), F32)
    vector = pltpu.VMEM((1024, 128), BF)
    source, own, send = call(
        source_kernel, [shape((256, 128))] + packed_shapes, solve_flops,
        scalars, g_columns, source_part, shipped_source, scratch=[whole],
    )
    got = gathered_y(send)[1:]
    ship_lower, *both = after((ship_lower, *diagonals, *got))
    diagonals, got = both[:4], both[4:]
    lower_new = along_cuts(ship_lower, 1)
    (pair,) = call(pair_kernel, [shape((256, 1024))], 0, scalars, lower_new, upper_new)
    pairs = [pair] + [moved_x(pair, by) for by in turns]
    solved = ()
    for turn in range(REFINE):
        *solved, own, send = call(
            functools.partial(turn_kernel, first=turn == 0),
            [shape((512, 128))] + packed_shapes, 2 * solve_flops,
            scalars, own, *got, *solved, *diagonals, source, g_columns,
            scratch=[vector, whole],
        )
        got = gathered_y(send)[1:]
    (solved,) = call(
        last_kernel, [shape((512, 128))], 0,
        scalars, own, *got, *solved,
    )
    below, above = along_cuts(solved, 1), along_cuts(solved, -1)
    (diagonal_rows,) = call(
        diagonal_rows_kernel, [shape((2, 64, 1024))], 0, scalars, *diagonals
    )
    lower_rows, upper_rows = call(
        coupling_rows_kernel, [shape((2, 64, 1024))] * 2, 0, scalars, *pairs
    )
    ends = call(
        couple_kernel, [shape((64, 128), F32)] * 4, solve_flops // 2,
        scalars, *pairs, source, solved, below, above,
        scratch=[pltpu.VMEM((256, 128), F32), vector],
    )
    ends = [ends[0]] + [moved_x(ends[by], by) for by in turns]
    combined, solved_rows = call(
        spread_kernel, [shape((2, 64, 128), F32)] * 2, 0, scalars, *ends
    )
    return (
        diagonal_rows[None],
        lower_rows[None],
        upper_rows[None],
        combined[None],
        solved_rows[None],
    )


def solution(mesh):
    split = P("cuts", None, "row", None)
    return jax.shard_map(
        body,
        mesh=mesh,
        in_specs=(split, split, split, split, split, P()),
        out_specs=(split,) * 5,
        check_vma=False,
    )
```

```python
import functools

import jax
import jax.numpy as jnp
from jax import lax
from jax.experimental import pallas as pl
from jax.experimental.pallas import tpu as pltpu
from jax.sharding import PartitionSpec as P

REFINE = 2
BF = jnp.bfloat16
F32 = jnp.float32
VMEM = pl.BlockSpec(memory_space=pltpu.VMEM)
MIB = 24
SMEM = pl.BlockSpec(memory_space=pltpu.SMEM)


def call(kernel, out_shapes, flops, *args, scratch=(), hbm=0, mib=MIB, hbm_out=False):
    moved = sum(a.size * a.dtype.itemsize for a in args) + sum(
        s.size * s.dtype.itemsize for s in out_shapes
    )
    anywhere = pl.BlockSpec(memory_space=pltpu.HBM)
    args = [
        pltpu.with_memory_space_constraint(a, pltpu.HBM) if 0 < index <= hbm else a
        for index, a in enumerate(args)
    ]
    return pl.pallas_call(
        kernel,
        out_shape=tuple(out_shapes),
        in_specs=[SMEM] + [anywhere] * hbm + [VMEM] * (len(args) - 1 - hbm),
        out_specs=tuple([anywhere if hbm_out else VMEM] * len(out_shapes)),
        scratch_shapes=list(scratch),
        compiler_params=pltpu.CompilerParams(vmem_limit_bytes=mib * 1024 * 1024),
        cost_estimate=pl.CostEstimate(flops=0, bytes_accessed=moved, transcendentals=0),
    )(*args)


def shape(dims, dtype=BF):
    return jax.ShapeDtypeStruct(dims, dtype)


def mod4(v):
    return lax.rem(v + 8, 4)


def at(chunk, size):
    return pl.ds(pl.multiple_of(chunk * size, size), size)


def lanes_of(rows):
    return lax.broadcasted_iota(jnp.int32, (rows, 128), 1)


def combine_small(real_rows, imag_rows):
    lane = lanes_of(real_rows.shape[0])
    turned = jnp.where(lane < 32, -pltpu.roll(imag_rows, 96, 1), pltpu.roll(imag_rows, 32, 1))
    return jnp.where(lane < 64, real_rows + turned, 0.0)


def packed(block):
    half = block.shape[0] // 2
    return jnp.where(lanes_of(half) < 64, block[:half], pltpu.roll(block[half:], 64, 1))


def halves(block):
    return block, pltpu.roll(block, 64, 1)


def masked(block, first_row, rows_on, chunk, cols_on):
    row = first_row + lax.broadcasted_iota(jnp.int32, (64, 256), 0)
    col = chunk * 256 + lax.broadcasted_iota(jnp.int32, (64, 256), 1)
    return jnp.where((row < rows_on) & (col < cols_on), block.astype(F32), 0.0).astype(BF)


def prepare_kernel(s_ref, d_hbm, g_hbm, a_hbm, c_hbm, b_hbm, piece0, piece1, piece2, piece3,
                   a_even, c_even, g0, g1, g2, g3, g_odd,
                   d_ref, a_ref, c_ref, b_ref, a_first, c_first, g_first, sems):
    y, x = s_ref[0], s_ref[1]
    first_row = (y * 4 + x) * 64
    before, own, odd, after = s_ref[2], s_ref[3], s_ref[4], s_ref[5]
    copies = [
        pltpu.make_async_copy(source, target, sems.at[index])
        for index, (source, target) in enumerate(
            (
                (c_hbm.at[1, 0], c_ref.at[0]),
                (c_hbm.at[1, 1], c_ref.at[1]),
                (b_hbm, b_ref),
                (a_hbm.at[1, 0], a_ref.at[0]),
                (a_hbm.at[1, 1], a_ref.at[1]),
                (d_hbm.at[0, 0], d_ref.at[0]),
                (d_hbm.at[0, 1], d_ref.at[1]),
                (a_hbm.at[0], a_first),
                (c_hbm.at[0], c_first),
                (g_hbm.at[0], g_first),
                (g_hbm.at[1], g_odd),
            )
        )
    ]
    for copy in copies:
        copy.start()
    pieces = (piece0, piece1, piece2, piece3)
    row_b = first_row + lax.broadcasted_iota(jnp.int32, (64, 128), 0)
    lane = lanes_of(64)
    copies[0].wait()
    copies[1].wait()
    for shift, piece in enumerate(pieces):
        chunk = mod4(x + shift)
        for part in range(2):
            piece[:, pl.ds(part * 256, 256)] = masked(
                c_ref[part, :, at(chunk, 256)], first_row, odd, chunk, after
            )
    copies[2].wait()
    blocks = [
        jnp.where(row_b < rows_on, b_ref[which, part].astype(F32), 0.0)
        for which, part, rows_on in ((1, 0, odd), (1, 1, odd), (0, 0, own), (0, 1, own))
    ]
    for shift, piece in enumerate(pieces):
        chunk = mod4(x + shift)
        tile = jnp.zeros((64, 128), F32)
        for place, block in enumerate(blocks):
            turned = pltpu.roll(block, mod4(place - chunk) * 32, 1)
            tile = jnp.where((lane >= place * 32) & (lane < place * 32 + 32), turned, tile)
        piece[:, pl.ds(512, 128)] = tile.astype(BF)
    copies[3].wait()
    copies[4].wait()
    for shift, piece in enumerate(pieces):
        chunk = mod4(x + shift)
        for part in range(2):
            piece[:, pl.ds(640 + part * 256, 256)] = masked(
                a_ref[part, :, at(chunk, 256)], first_row, odd, chunk, own
            )
    copies[5].wait()
    copies[6].wait()
    for shift, piece in enumerate(pieces):
        chunk = mod4(x + shift)
        for part in range(2):
            piece[:, pl.ds(1152 + part * 256, 256)] = d_ref[part, :, at(chunk, 256)]
    copies[7].wait()
    copies[8].wait()
    for chunk in range(4):
        cols = pl.ds(chunk * 256, 256)
        for part in range(2):
            a_even[part, :, cols] = masked(a_first[part, :, cols], first_row, own, chunk, before)
            c_even[part, :, cols] = masked(c_first[part, :, cols], first_row, own, chunk, odd)
    copies[9].wait()
    for shift, piece in enumerate((g0, g1, g2, g3)):
        for part in range(2):
            piece[part] = g_first[part, :, at(mod4(y + shift), 256)]
    copies[10].wait()


def assemble_kernel(s_ref, piece0, piece1, piece2, piece3, g0, g1, g2, g3,
                    panel, diagonal, g_columns):
    y, x = s_ref[0], s_ref[1]
    for shift, piece in enumerate((piece0, piece1, piece2, piece3)):
        rows = at(mod4(x - shift), 64)
        panel[rows, :] = piece[:, pl.ds(0, 1152)]
        diagonal[rows, :] = piece[:, pl.ds(1152, 512)]
    for shift, piece in enumerate((g0, g1, g2, g3)):
        g_columns[mod4(y - shift)] = piece[...]


def stack_rows(x, blocks, held):
    for shift, block in enumerate(blocks):
        held[at(mod4(x - shift), 128), :] = block[...].reshape(128, 1024)


def wide_dot(y, held, panels, start, width):
    total = None
    for place, panel in enumerate(panels):
        term = jnp.dot(
            held[:, at(mod4(y + place), 256)],
            panel[pl.ds(0, 256), pl.ds(start, width)],
            preferred_element_type=F32,
        )
        total = term if total is None else total + term
    parts = total.reshape(4, 2, 64, width)
    return parts[:, 0].reshape(256, width), parts[:, 1].reshape(256, width)


def wide_product(y, held, panels, start=0):
    real_rows, imag_rows = wide_dot(y, held, panels, start, 512)
    real = real_rows[:, :256] - imag_rows[:, 256:]
    imag = real_rows[:, 256:] + imag_rows[:, :256]
    return real, imag


def small_product(y, held, panels):
    return combine_small(*wide_dot(y, held, panels, 512, 128))


def put_pair(out, real, imag):
    out[pl.ds(0, 256), pl.ds(0, 256)] = real.astype(out.dtype)
    out[pl.ds(0, 256), pl.ds(256, 256)] = imag.astype(out.dtype)


def odd_kernel(s_ref, g0, g1, g2, g3, panel0, panel1, panel2, panel3, out, out_second, held):
    y, x = s_ref[0], s_ref[1]
    panels = (panel0, panel1, panel2, panel3)
    stack_rows(x, (g0, g1, g2, g3), held)
    put_pair(out, *wide_product(y, held, panels))
    out[:, pl.ds(512, 128)] = small_product(y, held, panels).astype(BF)
    put_pair(out_second, *wide_product(y, held, panels, 640))
    out_second[pl.ds(256, 16), :] = jnp.zeros((16, 512), BF)


def even_kernel(s_ref, a0, a1, a2, a3, c_ref, panel0, panel1, panel2, panel3, source,
                ship, ship_source, upper_new, source_part, a_rows, c_rows):
    y, x = s_ref[0], s_ref[1]
    panels = (panel0, panel1, panel2, panel3)
    stack_rows(x, (a0, a1, a2, a3), a_rows)
    c_rows[...] = c_ref[...].reshape(512, 1024)
    ship_source[...] = small_product(y, a_rows, panels).astype(BF)
    put_pair(ship, *wide_product(y, a_rows, panels))
    own = pltpu.roll(source[:, pl.ds(512, 128)].astype(F32), 64, 1)
    own = jnp.where(lanes_of(256) < 64, own, 0.0)
    source_part[...] = own - small_product(y, c_rows, panels)
    real, imag = wide_product(y, c_rows, panels)
    put_pair(upper_new, -real, -imag)


def diagonal_kernel(s_ref, c_rows, a_rows, panel0, panel1, panel2, panel3, diagonal, shipped,
                    out, lower_real, lower_imag):
    real, imag = wide_product(s_ref[0], c_rows, (panel0, panel1, panel2, panel3))
    real = diagonal[:, pl.ds(0, 256)].astype(F32) - real - shipped[:, pl.ds(0, 256)].astype(F32)
    imag = diagonal[:, pl.ds(256, 256)].astype(F32) - imag - shipped[:, pl.ds(256, 256)].astype(F32)
    put_pair(out, real, imag)
    real, imag = wide_product(s_ref[0], a_rows, (panel0, panel1, panel2, panel3))
    lower_real[...] = (-real).astype(BF)
    lower_imag[...] = (-imag).astype(BF)


def pair_kernel(s_ref, lower_real, lower_imag, upper, out):
    out[:, pl.ds(0, 256)] = lower_real[...]
    out[:, pl.ds(256, 256)] = lower_imag[...]
    out[:, pl.ds(512, 512)] = upper[...]


def block_product(block, right):
    real = jnp.dot(block[:, pl.ds(0, 256)], right, preferred_element_type=F32)
    imag = jnp.dot(block[:, pl.ds(256, 256)], right, preferred_element_type=F32)
    return real, imag


def put_partial(g_ref, right, own, send, whole):
    for index in range(4):
        total = jnp.dot(g_ref[index].reshape(512, 256), right, preferred_element_type=F32)
        parts = total.reshape(4, 2, 64, 128)
        value = combine_small(parts[:, 0].reshape(256, 128), parts[:, 1].reshape(256, 128))
        value = value.reshape(4, 64, 128)
        for group in range(4):
            whole[pl.ds(group * 256 + index * 64, 64), :] = value[group]
    total = packed(whole[...])
    own[...] = total
    send[...] = total.astype(BF)


def source_kernel(s_ref, g_ref, source_part, shipped, source_new, own, send, whole):
    source = (source_part[...] - shipped[...].astype(F32)).astype(BF)
    source_new[...] = source
    put_partial(g_ref, source, own, send, whole)


def summed(own, got):
    total = own[...]
    for other in got:
        total = total + other[...].astype(F32)
    return total


def turn_kernel(s_ref, own, got1, got2, got3, *refs, first):
    solved = None if first else refs[0]
    blocks, refs = refs[:4] if first else refs[1:5], refs[4:] if first else refs[5:]
    source, g_ref, out, own_new, send, vector, whole = refs
    x = s_ref[1]
    total = summed(own, (got1, got2, got3))
    if not first:
        total = solved[...].astype(F32) + total
    out[...] = total.astype(BF)
    unpack(out, vector)
    residue = (source[...].astype(F32) - blocks_product(x, blocks, vector)).astype(BF)
    put_partial(g_ref, residue, own_new, send, whole)


def last_kernel(s_ref, own, got1, got2, got3, solved, out):
    out[...] = (solved[...].astype(F32) + summed(own, (got1, got2, got3))).astype(BF)


def diagonal_rows_kernel(s_ref, block0, block1, block2, block3, rows_out):
    x = s_ref[1]
    rows = at(x, 64)
    for shift, block in enumerate((block0, block1, block2, block3)):
        cols = at(mod4(x - shift), 256)
        rows_out[0, :, cols] = block[rows, pl.ds(0, 256)]
        rows_out[1, :, cols] = block[rows, pl.ds(256, 256)]


def coupling_rows_kernel(s_ref, pair0, pair1, pair2, pair3, lower_out, upper_out):
    x = s_ref[1]
    rows = at(x, 64)
    for shift, pair in enumerate((pair0, pair1, pair2, pair3)):
        cols = at(mod4(x - shift), 256)
        lower_out[0, :, cols] = pair[rows, pl.ds(0, 256)]
        lower_out[1, :, cols] = pair[rows, pl.ds(256, 256)]
        upper_out[0, :, cols] = pair[rows, pl.ds(512, 256)]
        upper_out[1, :, cols] = pair[rows, pl.ds(768, 256)]


def unpack(solved, vector):
    low, high = halves(solved[...].astype(F32))
    vector[pl.ds(0, 512), :] = low.astype(BF)
    vector[pl.ds(512, 512), :] = high.astype(BF)


def blocks_product(x, blocks, vector):
    real_rows = imag_rows = None
    for shift, block in enumerate(blocks):
        real, imag = block_product(block, vector[at(mod4(x - shift), 256), :])
        real_rows = real if real_rows is None else real_rows + real
        imag_rows = imag if imag_rows is None else imag_rows + imag
    return combine_small(real_rows, imag_rows)


def couple_kernel(s_ref, pair0, pair1, pair2, pair3, source, solved, below, above,
                  out0, out1, out2, out3, held, vector):
    y, x = s_ref[0], s_ref[1]
    pairs = (pair0, pair1, pair2, pair3)
    unpack(below, vector)
    combined = source[...].astype(F32)
    combined = combined - blocks_product(x, [p.at[:, pl.ds(0, 512)] for p in pairs], vector)
    unpack(above, vector)
    combined = combined - blocks_product(x, [p.at[:, pl.ds(512, 512)] for p in pairs], vector)
    rows = pl.ds(pl.multiple_of(lax.rem(y, 2) * 256, 256), 256)
    moved = pltpu.roll(solved[rows, :].astype(F32), jnp.where(y < 2, 64, 0), 1)
    held[...] = jnp.where(lanes_of(256) < 64, combined, moved)
    for shift, out in enumerate((out0, out1, out2, out3)):
        out[...] = held[at(mod4(x + shift), 64), :]


def spread_kernel(s_ref, piece0, piece1, piece2, piece3, combined, solved):
    x = s_ref[1]
    lane = lanes_of(64)
    totals = [jnp.zeros((64, 128), F32) for _ in range(4)]
    for shift, piece in enumerate((piece0, piece1, piece2, piece3)):
        chunk = mod4(x - shift)
        value = piece[...]
        on = (lane >= chunk * 32) & (lane < chunk * 32 + 32)
        for place in range(4):
            turned = pltpu.roll(value, mod4(chunk - place) * 32, 1)
            totals[place] = jnp.where(on, turned, totals[place])
    combined[0] = totals[0]
    combined[1] = totals[1]
    solved[0] = totals[2]
    solved[1] = totals[3]


def moved_x(block, by):
    pairs = [(y * 4 + x, y * 4 + (x + by) % 4) for y in range(4) for x in range(4)]
    return lax.ppermute(block, "row", pairs)


def moved_y(block, by):
    pairs = [(y * 4 + x, ((y + by) % 4) * 4 + x) for y in range(4) for x in range(4)]
    return lax.ppermute(block, "row", pairs)


def gathered_y(block):
    return (block, moved_y(block, 3), moved_y(block, 2), moved_y(block, 1))


def gathered_x(block):
    groups = [[y * 4 + x for x in range(4)] for y in range(4)]
    return lax.all_gather(block, "row", axis_index_groups=groups)


def along_cuts(block, by):
    count = lax.axis_size("cuts")
    pairs = [(i, i + by) for i in range(count) if 0 <= i + by < count]
    return lax.ppermute(block, "cuts", pairs)


def body(diagonal_blocks, diagonal_inverses, lower_blocks, upper_blocks, injection, orbitals):
    cut = lax.axis_index("cuts")
    place = lax.axis_index("row")
    zero = jnp.zeros((1,), jnp.int32)
    window = lax.dynamic_slice_in_dim(jnp.concatenate([zero, orbitals, zero]), 2 * cut, 4)
    scalars = jnp.concatenate([jnp.stack([place // 4, place % 4]).astype(jnp.int32), window])
    turns = (1, 2, 3)
    after = lax.optimization_barrier
    wide_flops = 2 * 512 * 1024 * 512
    solve_flops = 2 * 2048 * 256 * 128

    *pieces, a_even, c_even, g0, g1, g2, g3, g_odd = call(
        prepare_kernel,
        [shape((64, 1664))] * 4 + [shape((2, 64, 1024))] * 2 + [shape((2, 64, 256))] * 4
        + [shape((2, 64, 1024))],
        0,
        scalars, diagonal_blocks, diagonal_inverses, lower_blocks, upper_blocks, injection,
        hbm=5,
        scratch=[pltpu.VMEM((2, 64, 1024), BF)] * 3
        + [pltpu.VMEM((2, 2, 64, 128), BF)]
        + [pltpu.VMEM((2, 64, 1024), BF)] * 3
        + [pltpu.SemaphoreType.DMA((11,))],
    )
    pieces = [pieces[0]] + [moved_x(pieces[by], by) for by in turns]
    c_gathered = gathered_x(c_even)
    a_next = along_cuts(a_even, -1)
    g1, g2, g3 = [moved_y(piece, by) for by, piece in zip(turns, (g1, g2, g3))]
    a_next, g1, g2, g3, g_odd, *pieces = after((a_next, g1, g2, g3, g_odd, *pieces))
    panel, diagonal, g_columns = call(
        assemble_kernel,
        [shape((256, 1152)), shape((256, 512)), shape((4, 2, 64, 256))],
        0, scalars, *pieces, g0, g1, g2, g3,
    )
    g_columns = gathered_x(g_columns)
    panels = gathered_y(panel)
    g_blocks = [g_odd] + [moved_x(g_odd, by) for by in turns]
    a_blocks = [a_next] + [moved_x(a_next, by) for by in turns]
    first, second = call(
        odd_kernel, [shape((256, 640)), shape((272, 512))], wide_flops,
        scalars, *g_blocks, *panels, scratch=[pltpu.VMEM((512, 1024), BF)],
    )
    first, c_gathered = after((first, c_gathered))
    firsts = gathered_y(first)
    second, g_columns, *a_blocks = after((second, g_columns, *a_blocks))
    seconds = gathered_y(second)
    ship, ship_source, upper_new, source_part, a_rows, c_rows = call(
        even_kernel,
        [shape((256, 512)), shape((256, 128)), shape((256, 512)), shape((256, 128), F32),
         shape((512, 1024)),
         shape((512, 1024))],
        2 * wide_flops,
        scalars, *a_blocks, c_gathered, *firsts, panel,
    )
    shipped = along_cuts(ship, 1)
    shipped_source = along_cuts(ship_source, 1)
    diagonal_new, *ship_lower = call(
        diagonal_kernel, [shape((256, 512))] + [shape((256, 256))] * 2, 2 * wide_flops,
        scalars, c_rows, a_rows, *seconds, diagonal, shipped,
    )
    diagonals = [diagonal_new] + [moved_x(diagonal_new, by) for by in turns]
    packed_shapes = [shape((512, 128), F32), shape((512, 128))]
    whole = pltpu.VMEM((1024, 128), F32)
    vector = pltpu.VMEM((1024, 128), BF)
    source, own, send = call(
        source_kernel, [shape((256, 128))] + packed_shapes, solve_flops,
        scalars, g_columns, source_part, shipped_source, scratch=[whole],
    )
    got = gathered_y(send)[1:]
    lower_new = [along_cuts(half, 1) for half in ship_lower]
    (pair,) = call(pair_kernel, [shape((256, 1024))], 0, scalars, *lower_new, upper_new)
    pairs = [pair] + [moved_x(pair, by) for by in turns]
    solved = ()
    for turn in range(REFINE):
        *solved, own, send = call(
            functools.partial(turn_kernel, first=turn == 0),
            [shape((512, 128))] + packed_shapes, 2 * solve_flops,
            scalars, own, *got, *solved, *diagonals, source, g_columns,
            scratch=[vector, whole],
        )
        got = gathered_y(send)[1:]
    (solved,) = call(
        last_kernel, [shape((512, 128))], 0,
        scalars, own, *got, *solved,
    )
    below, above = along_cuts(solved, 1), along_cuts(solved, -1)
    (diagonal_rows,) = call(
        diagonal_rows_kernel, [shape((2, 64, 1024))], 0, scalars, *diagonals
    )
    lower_rows, upper_rows = call(
        coupling_rows_kernel, [shape((2, 64, 1024))] * 2, 0, scalars, *pairs
    )
    ends = call(
        couple_kernel, [shape((64, 128), F32)] * 4, solve_flops // 2,
        scalars, *pairs, source, solved, below, above,
        scratch=[pltpu.VMEM((256, 128), F32), vector],
    )
    ends = [ends[0]] + [moved_x(ends[by], by) for by in turns]
    combined, solved_rows = call(
        spread_kernel, [shape((2, 64, 128), F32)] * 2, 0, scalars, *ends
    )
    return (
        diagonal_rows[None],
        lower_rows[None],
        upper_rows[None],
        combined[None],
        solved_rows[None],
    )


def solution(mesh):
    split = P("cuts", None, "row", None)
    return jax.shard_map(
        body,
        mesh=mesh,
        in_specs=(split, split, split, split, split, P()),
        out_specs=(split,) * 5,
        check_vma=False,
    )
```

```python
import functools

import jax
import jax.numpy as jnp
from jax import lax
from jax.experimental import pallas as pl
from jax.experimental.pallas import tpu as pltpu
from jax.sharding import PartitionSpec as P

REFINE = 2
BF = jnp.bfloat16
F32 = jnp.float32
VMEM = pl.BlockSpec(memory_space=pltpu.VMEM)
MIB = 24
SMEM = pl.BlockSpec(memory_space=pltpu.SMEM)


def call(kernel, out_shapes, flops, *args, scratch=(), hbm=0, mib=MIB, hbm_out=False):
    moved = sum(a.size * a.dtype.itemsize for a in args) + sum(
        s.size * s.dtype.itemsize for s in out_shapes
    )
    anywhere = pl.BlockSpec(memory_space=pltpu.HBM)
    args = [
        pltpu.with_memory_space_constraint(a, pltpu.HBM) if 0 < index <= hbm else a
        for index, a in enumerate(args)
    ]
    return pl.pallas_call(
        kernel,
        out_shape=tuple(out_shapes),
        in_specs=[SMEM] + [anywhere] * hbm + [VMEM] * (len(args) - 1 - hbm),
        out_specs=tuple([anywhere if hbm_out else VMEM] * len(out_shapes)),
        scratch_shapes=list(scratch),
        compiler_params=pltpu.CompilerParams(vmem_limit_bytes=mib * 1024 * 1024),
        cost_estimate=pl.CostEstimate(flops=0, bytes_accessed=moved, transcendentals=0),
    )(*args)


def shape(dims, dtype=BF):
    return jax.ShapeDtypeStruct(dims, dtype)


def mod4(v):
    return lax.rem(v + 8, 4)


def at(chunk, size):
    return pl.ds(pl.multiple_of(chunk * size, size), size)


def lanes_of(rows):
    return lax.broadcasted_iota(jnp.int32, (rows, 128), 1)


def combine_small(real_rows, imag_rows):
    lane = lanes_of(real_rows.shape[0])
    turned = jnp.where(lane < 32, -pltpu.roll(imag_rows, 96, 1), pltpu.roll(imag_rows, 32, 1))
    return jnp.where(lane < 64, real_rows + turned, 0.0)


def packed(block):
    half = block.shape[0] // 2
    return jnp.where(lanes_of(half) < 64, block[:half], pltpu.roll(block[half:], 64, 1))


def halves(block):
    return block, pltpu.roll(block, 64, 1)


def masked(block, first_row, rows_on, chunk, cols_on):
    row = first_row + lax.broadcasted_iota(jnp.int32, (64, 256), 0)
    col = chunk * 256 + lax.broadcasted_iota(jnp.int32, (64, 256), 1)
    return jnp.where((row < rows_on) & (col < cols_on), block.astype(F32), 0.0).astype(BF)


def prepare_kernel(s_ref, d_hbm, g_hbm, a_hbm, c_hbm, b_hbm, piece0, piece1, piece2, piece3,
                   a_even, c_even, g0, g1, g2, g3, g_odd,
                   d_ref, a_ref, c_ref, b_ref, a_first, c_first, g_first, sems):
    y, x = s_ref[0], s_ref[1]
    first_row = (y * 4 + x) * 64
    before, own, odd, after = s_ref[2], s_ref[3], s_ref[4], s_ref[5]
    copies = [
        pltpu.make_async_copy(source, target, sems.at[index])
        for index, (source, target) in enumerate(
            (
                (c_hbm.at[1, 0], c_ref.at[0]),
                (c_hbm.at[1, 1], c_ref.at[1]),
                (b_hbm, b_ref),
                (a_hbm.at[1, 0], a_ref.at[0]),
                (a_hbm.at[1, 1], a_ref.at[1]),
                (d_hbm.at[0, 0], d_ref.at[0]),
                (d_hbm.at[0, 1], d_ref.at[1]),
                (a_hbm.at[0], a_first),
                (c_hbm.at[0], c_first),
                (g_hbm.at[0], g_first),
                (g_hbm.at[1], g_odd),
            )
        )
    ]
    for copy in copies:
        copy.start()
    pieces = (piece0, piece1, piece2, piece3)
    row_b = first_row + lax.broadcasted_iota(jnp.int32, (64, 128), 0)
    lane = lanes_of(64)
    copies[0].wait()
    copies[1].wait()
    for shift, piece in enumerate(pieces):
        chunk = mod4(x + shift)
        for part in range(2):
            piece[:, pl.ds(part * 256, 256)] = masked(
                c_ref[part, :, at(chunk, 256)], first_row, odd, chunk, after
            )
    copies[2].wait()
    blocks = [
        jnp.where(row_b < rows_on, b_ref[which, part].astype(F32), 0.0)
        for which, part, rows_on in ((1, 0, odd), (1, 1, odd), (0, 0, own), (0, 1, own))
    ]
    for shift, piece in enumerate(pieces):
        chunk = mod4(x + shift)
        tile = jnp.zeros((64, 128), F32)
        for place, block in enumerate(blocks):
            turned = pltpu.roll(block, mod4(place - chunk) * 32, 1)
            tile = jnp.where((lane >= place * 32) & (lane < place * 32 + 32), turned, tile)
        piece[:, pl.ds(512, 128)] = tile.astype(BF)
    copies[3].wait()
    copies[4].wait()
    for shift, piece in enumerate(pieces):
        chunk = mod4(x + shift)
        for part in range(2):
            piece[:, pl.ds(640 + part * 256, 256)] = masked(
                a_ref[part, :, at(chunk, 256)], first_row, odd, chunk, own
            )
    copies[5].wait()
    copies[6].wait()
    for shift, piece in enumerate(pieces):
        chunk = mod4(x + shift)
        for part in range(2):
            piece[:, pl.ds(1152 + part * 256, 256)] = d_ref[part, :, at(chunk, 256)]
    copies[7].wait()
    copies[8].wait()
    for chunk in range(4):
        cols = pl.ds(chunk * 256, 256)
        for part in range(2):
            a_even[part, :, cols] = masked(a_first[part, :, cols], first_row, own, chunk, before)
            c_even[part, :, cols] = masked(c_first[part, :, cols], first_row, own, chunk, odd)
    copies[9].wait()
    for shift, piece in enumerate((g0, g1, g2, g3)):
        for part in range(2):
            piece[part] = g_first[part, :, at(mod4(y + shift), 256)]
    copies[10].wait()


def assemble_kernel(s_ref, piece0, piece1, piece2, piece3, c_even, a_next, g0, g1, g2, g3,
                    panel, diagonal, couplings, g_columns):
    y, x = s_ref[0], s_ref[1]
    for shift, piece in enumerate((piece0, piece1, piece2, piece3)):
        rows = at(mod4(x - shift), 64)
        panel[rows, :] = piece[:, pl.ds(0, 1152)]
        diagonal[rows, :] = piece[:, pl.ds(1152, 512)]
    couplings[0] = c_even[...]
    couplings[1] = a_next[...]
    for shift, piece in enumerate((g0, g1, g2, g3)):
        g_columns[mod4(y - shift)] = piece[...]


def stack_rows(x, blocks, held):
    for shift, block in enumerate(blocks):
        held[at(mod4(x - shift), 128), :] = block[...].reshape(128, 1024)


def wide_dot(y, held, panels, start, width):
    total = None
    for place, panel in enumerate(panels):
        term = jnp.dot(
            held[:, at(mod4(y + place), 256)],
            panel[pl.ds(0, 256), pl.ds(start, width)],
            preferred_element_type=F32,
        )
        total = term if total is None else total + term
    parts = total.reshape(4, 2, 64, width)
    return parts[:, 0].reshape(256, width), parts[:, 1].reshape(256, width)


def wide_product(y, held, panels, start=0):
    real_rows, imag_rows = wide_dot(y, held, panels, start, 512)
    real = real_rows[:, :256] - imag_rows[:, 256:]
    imag = real_rows[:, 256:] + imag_rows[:, :256]
    return real, imag


def small_product(y, held, panels):
    return combine_small(*wide_dot(y, held, panels, 512, 128))


def put_pair(out, real, imag):
    out[pl.ds(0, 256), pl.ds(0, 256)] = real.astype(out.dtype)
    out[pl.ds(0, 256), pl.ds(256, 256)] = imag.astype(out.dtype)


def odd_kernel(s_ref, g_ref, panel0, panel1, panel2, panel3, out, out_second, held):
    y, x = s_ref[0], s_ref[1]
    panels = (panel0, panel1, panel2, panel3)
    held[...] = g_ref[...].reshape(512, 1024)
    put_pair(out, *wide_product(y, held, panels))
    out[:, pl.ds(512, 128)] = small_product(y, held, panels).astype(BF)
    put_pair(out_second, *wide_product(y, held, panels, 640))
    out_second[pl.ds(256, 48), :] = jnp.zeros((48, 512), BF)


def even_kernel(s_ref, ca0, ca1, ca2, ca3, panel0, panel1, panel2, panel3, source,
                ship, upper_new, source_part, a_rows, c_rows):
    y, x = s_ref[0], s_ref[1]
    panels = (panel0, panel1, panel2, panel3)
    stack_rows(x, [block.at[1] for block in (ca0, ca1, ca2, ca3)], a_rows)
    stack_rows(x, [block.at[0] for block in (ca0, ca1, ca2, ca3)], c_rows)
    value = small_product(y, a_rows, panels)
    lane = lanes_of(32)
    for index in range(4):
        low, high = value[index * 64 : index * 64 + 32], value[index * 64 + 32 : index * 64 + 64]
        tile = jnp.where(lane < 64, low, pltpu.roll(high, 64, 1))
        ship[pl.ds(256, 32), pl.ds(index * 128, 128)] = tile.astype(BF)
    put_pair(ship, *wide_product(y, a_rows, panels))
    own = pltpu.roll(source[:, pl.ds(512, 128)].astype(F32), 64, 1)
    own = jnp.where(lanes_of(256) < 64, own, 0.0)
    source_part[...] = own - small_product(y, c_rows, panels)
    real, imag = wide_product(y, c_rows, panels)
    put_pair(upper_new, -real, -imag)


def diagonal_kernel(s_ref, c_rows, a_rows, panel0, panel1, panel2, panel3, diagonal, shipped,
                    out, lower_real, lower_imag):
    real, imag = wide_product(s_ref[0], c_rows, (panel0, panel1, panel2, panel3))
    real = diagonal[:, pl.ds(0, 256)].astype(F32) - real - shipped[pl.ds(0, 256), pl.ds(0, 256)].astype(F32)
    imag = diagonal[:, pl.ds(256, 256)].astype(F32) - imag - shipped[pl.ds(0, 256), pl.ds(256, 256)].astype(F32)
    put_pair(out, real, imag)
    real, imag = wide_product(s_ref[0], a_rows, (panel0, panel1, panel2, panel3))
    lower_real[...] = (-real).astype(BF)
    lower_imag[...] = (-imag).astype(BF)


def pair_kernel(s_ref, lower_real, lower_imag, upper, out):
    out[:, pl.ds(0, 256)] = lower_real[...]
    out[:, pl.ds(256, 256)] = lower_imag[...]
    out[:, pl.ds(512, 512)] = upper[...]


def block_product(block, right):
    real = jnp.dot(block[:, pl.ds(0, 256)], right, preferred_element_type=F32)
    imag = jnp.dot(block[:, pl.ds(256, 256)], right, preferred_element_type=F32)
    return real, imag


def put_partial(g_ref, right, own, send, whole):
    for index in range(4):
        total = jnp.dot(g_ref[index].reshape(512, 256), right, preferred_element_type=F32)
        parts = total.reshape(4, 2, 64, 128)
        value = combine_small(parts[:, 0].reshape(256, 128), parts[:, 1].reshape(256, 128))
        value = value.reshape(4, 64, 128)
        for group in range(4):
            whole[pl.ds(group * 256 + index * 64, 64), :] = value[group]
    total = packed(whole[...])
    own[...] = total
    send[...] = total.astype(BF)


def source_kernel(s_ref, g_ref, source_part, shipped, source_new, own, send, whole):
    lane = lanes_of(32)
    for index in range(4):
        tile = shipped[pl.ds(256, 32), pl.ds(index * 128, 128)].astype(F32)
        for half, moved in enumerate(halves(tile)):
            rows = pl.ds(index * 64 + half * 32, 32)
            value = source_part[rows, :] - jnp.where(lane < 64, moved, 0.0)
            source_new[rows, :] = value.astype(BF)
    source = source_new[...]
    put_partial(g_ref, source, own, send, whole)


def summed(own, got):
    total = own[...]
    for other in got:
        total = total + other[...].astype(F32)
    return total


def turn_kernel(s_ref, own, got1, got2, got3, *refs, first):
    solved = None if first else refs[0]
    blocks, refs = refs[:4] if first else refs[1:5], refs[4:] if first else refs[5:]
    source, g_ref, out, own_new, send, vector, whole = refs
    x = s_ref[1]
    total = summed(own, (got1, got2, got3))
    if not first:
        total = solved[...].astype(F32) + total
    out[...] = total.astype(BF)
    unpack(out, vector)
    residue = (source[...].astype(F32) - blocks_product(x, blocks, vector)).astype(BF)
    put_partial(g_ref, residue, own_new, send, whole)


def last_kernel(s_ref, own, got1, got2, got3, solved, out):
    out[...] = (solved[...].astype(F32) + summed(own, (got1, got2, got3))).astype(BF)


def diagonal_rows_kernel(s_ref, block0, block1, block2, block3, rows_out):
    x = s_ref[1]
    rows = at(x, 64)
    for shift, block in enumerate((block0, block1, block2, block3)):
        cols = at(mod4(x - shift), 256)
        rows_out[0, :, cols] = block[rows, pl.ds(0, 256)]
        rows_out[1, :, cols] = block[rows, pl.ds(256, 256)]


def coupling_rows_kernel(s_ref, pair0, pair1, pair2, pair3, lower_out, upper_out):
    x = s_ref[1]
    rows = at(x, 64)
    for shift, pair in enumerate((pair0, pair1, pair2, pair3)):
        cols = at(mod4(x - shift), 256)
        lower_out[0, :, cols] = pair[rows, pl.ds(0, 256)]
        lower_out[1, :, cols] = pair[rows, pl.ds(256, 256)]
        upper_out[0, :, cols] = pair[rows, pl.ds(512, 256)]
        upper_out[1, :, cols] = pair[rows, pl.ds(768, 256)]


def unpack(solved, vector):
    low, high = halves(solved[...].astype(F32))
    vector[pl.ds(0, 512), :] = low.astype(BF)
    vector[pl.ds(512, 512), :] = high.astype(BF)


def blocks_product(x, blocks, vector):
    real_rows = imag_rows = None
    for shift, block in enumerate(blocks):
        real, imag = block_product(block, vector[at(mod4(x - shift), 256), :])
        real_rows = real if real_rows is None else real_rows + real
        imag_rows = imag if imag_rows is None else imag_rows + imag
    return combine_small(real_rows, imag_rows)


def couple_kernel(s_ref, pair0, pair1, pair2, pair3, source, solved, below, above,
                  out0, out1, out2, out3, held, vector):
    y, x = s_ref[0], s_ref[1]
    pairs = (pair0, pair1, pair2, pair3)
    unpack(below, vector)
    combined = source[...].astype(F32)
    combined = combined - blocks_product(x, [p.at[:, pl.ds(0, 512)] for p in pairs], vector)
    unpack(above, vector)
    combined = combined - blocks_product(x, [p.at[:, pl.ds(512, 512)] for p in pairs], vector)
    rows = pl.ds(pl.multiple_of(lax.rem(y, 2) * 256, 256), 256)
    moved = pltpu.roll(solved[rows, :].astype(F32), jnp.where(y < 2, 64, 0), 1)
    held[...] = jnp.where(lanes_of(256) < 64, combined, moved)
    for shift, out in enumerate((out0, out1, out2, out3)):
        out[...] = held[at(mod4(x + shift), 64), :]


def spread_kernel(s_ref, piece0, piece1, piece2, piece3, combined, solved):
    x = s_ref[1]
    lane = lanes_of(64)
    totals = [jnp.zeros((64, 128), F32) for _ in range(4)]
    for shift, piece in enumerate((piece0, piece1, piece2, piece3)):
        chunk = mod4(x - shift)
        value = piece[...]
        on = (lane >= chunk * 32) & (lane < chunk * 32 + 32)
        for place in range(4):
            turned = pltpu.roll(value, mod4(chunk - place) * 32, 1)
            totals[place] = jnp.where(on, turned, totals[place])
    combined[0] = totals[0]
    combined[1] = totals[1]
    solved[0] = totals[2]
    solved[1] = totals[3]


def moved_x(block, by):
    pairs = [(y * 4 + x, y * 4 + (x + by) % 4) for y in range(4) for x in range(4)]
    return lax.ppermute(block, "row", pairs)


def moved_y(block, by):
    pairs = [(y * 4 + x, ((y + by) % 4) * 4 + x) for y in range(4) for x in range(4)]
    return lax.ppermute(block, "row", pairs)


def gathered_y(block):
    return (block, moved_y(block, 3), moved_y(block, 2), moved_y(block, 1))


def gathered_x(block):
    groups = [[y * 4 + x for x in range(4)] for y in range(4)]
    return lax.all_gather(block, "row", axis_index_groups=groups)


def along_cuts(block, by):
    count = lax.axis_size("cuts")
    pairs = [(i, i + by) for i in range(count) if 0 <= i + by < count]
    return lax.ppermute(block, "cuts", pairs)


def body(diagonal_blocks, diagonal_inverses, lower_blocks, upper_blocks, injection, orbitals):
    cut = lax.axis_index("cuts")
    place = lax.axis_index("row")
    zero = jnp.zeros((1,), jnp.int32)
    window = lax.dynamic_slice_in_dim(jnp.concatenate([zero, orbitals, zero]), 2 * cut, 4)
    scalars = jnp.concatenate([jnp.stack([place // 4, place % 4]).astype(jnp.int32), window])
    turns = (1, 2, 3)
    after = lax.optimization_barrier
    wide_flops = 2 * 512 * 1024 * 512
    solve_flops = 2 * 2048 * 256 * 128

    *pieces, a_even, c_even, g0, g1, g2, g3, g_odd = call(
        prepare_kernel,
        [shape((64, 1664))] * 4 + [shape((2, 64, 1024))] * 2 + [shape((2, 64, 256))] * 4
        + [shape((2, 64, 1024))],
        0,
        scalars, diagonal_blocks, diagonal_inverses, lower_blocks, upper_blocks, injection,
        hbm=5,
        scratch=[pltpu.VMEM((2, 64, 1024), BF)] * 3
        + [pltpu.VMEM((2, 2, 64, 128), BF)]
        + [pltpu.VMEM((2, 64, 1024), BF)] * 3
        + [pltpu.SemaphoreType.DMA((11,))],
    )
    pieces = [pieces[0]] + [moved_x(pieces[by], by) for by in turns]
    g_rows = gathered_x(g_odd)
    a_next = along_cuts(a_even, -1)
    g1, g2, g3 = [moved_y(piece, by) for by, piece in zip(turns, (g1, g2, g3))]
    a_next, g1, g2, g3, *pieces = after((a_next, g1, g2, g3, *pieces))
    panel, diagonal, couplings, g_columns = call(
        assemble_kernel,
        [shape((256, 1152)), shape((256, 512)), shape((2, 2, 64, 1024)), shape((4, 2, 64, 256))],
        0, scalars, *pieces, c_even, a_next, g0, g1, g2, g3,
    )
    g_columns = gathered_x(g_columns)
    panels = gathered_y(panel)
    ca_blocks = [couplings] + [moved_x(couplings, by) for by in turns]
    first, second = call(
        odd_kernel, [shape((256, 640)), shape((304, 512))], wide_flops,
        scalars, g_rows, *panels, scratch=[pltpu.VMEM((512, 1024), BF)],
    )
    firsts = gathered_y(first)
    second, g_columns, *ca_blocks = after((second, g_columns, *ca_blocks))
    seconds = gathered_y(second)
    ship, upper_new, source_part, a_rows, c_rows = call(
        even_kernel,
        [shape((288, 512)), shape((256, 512)), shape((256, 128), F32),
         shape((512, 1024)),
         shape((512, 1024))],
        2 * wide_flops,
        scalars, *ca_blocks, *firsts, panel,
    )
    shipped = along_cuts(ship, 1)
    diagonal_new, *ship_lower = call(
        diagonal_kernel, [shape((256, 512))] + [shape((256, 256))] * 2, 2 * wide_flops,
        scalars, c_rows, a_rows, *seconds, diagonal, shipped,
    )
    diagonals = [diagonal_new] + [moved_x(diagonal_new, by) for by in turns]
    packed_shapes = [shape((512, 128), F32), shape((512, 128))]
    whole = pltpu.VMEM((1024, 128), F32)
    vector = pltpu.VMEM((1024, 128), BF)
    source, own, send = call(
        source_kernel, [shape((256, 128))] + packed_shapes, solve_flops,
        scalars, g_columns, source_part, shipped, scratch=[whole],
    )
    got = gathered_y(send)[1:]
    lower_new = [along_cuts(half, 1) for half in ship_lower]
    (pair,) = call(pair_kernel, [shape((256, 1024))], 0, scalars, *lower_new, upper_new)
    pairs = [pair] + [moved_x(pair, by) for by in turns]
    solved = ()
    for turn in range(REFINE):
        *solved, own, send = call(
            functools.partial(turn_kernel, first=turn == 0),
            [shape((512, 128))] + packed_shapes, 2 * solve_flops,
            scalars, own, *got, *solved, *diagonals, source, g_columns,
            scratch=[vector, whole],
        )
        got = gathered_y(send)[1:]
    (solved,) = call(
        last_kernel, [shape((512, 128))], 0,
        scalars, own, *got, *solved,
    )
    below, above = along_cuts(solved, 1), along_cuts(solved, -1)
    (diagonal_rows,) = call(
        diagonal_rows_kernel, [shape((2, 64, 1024))], 0, scalars, *diagonals
    )
    lower_rows, upper_rows = call(
        coupling_rows_kernel, [shape((2, 64, 1024))] * 2, 0, scalars, *pairs
    )
    ends = call(
        couple_kernel, [shape((64, 128), F32)] * 4, solve_flops // 2,
        scalars, *pairs, source, solved, below, above,
        scratch=[pltpu.VMEM((256, 128), F32), vector],
    )
    ends = [ends[0]] + [moved_x(ends[by], by) for by in turns]
    combined, solved_rows = call(
        spread_kernel, [shape((2, 64, 128), F32)] * 2, 0, scalars, *ends
    )
    return (
        diagonal_rows[None],
        lower_rows[None],
        upper_rows[None],
        combined[None],
        solved_rows[None],
    )


def solution(mesh):
    split = P("cuts", None, "row", None)
    return jax.shard_map(
        body,
        mesh=mesh,
        in_specs=(split, split, split, split, split, P()),
        out_specs=(split,) * 5,
        check_vma=False,
    )
```

```python
import functools

import jax
import jax.numpy as jnp
from jax import lax
from jax.experimental import pallas as pl
from jax.experimental.pallas import tpu as pltpu
from jax.sharding import PartitionSpec as P

REFINE = 2
BF = jnp.bfloat16
F32 = jnp.float32
VMEM = pl.BlockSpec(memory_space=pltpu.VMEM)
MIB = 24
SMEM = pl.BlockSpec(memory_space=pltpu.SMEM)


def call(kernel, out_shapes, flops, *args, scratch=(), hbm=0, mib=MIB, hbm_out=False):
    moved = sum(a.size * a.dtype.itemsize for a in args) + sum(
        s.size * s.dtype.itemsize for s in out_shapes
    )
    anywhere = pl.BlockSpec(memory_space=pltpu.HBM)
    args = [
        pltpu.with_memory_space_constraint(a, pltpu.HBM) if 0 < index <= hbm else a
        for index, a in enumerate(args)
    ]
    return pl.pallas_call(
        kernel,
        out_shape=tuple(out_shapes),
        in_specs=[SMEM] + [anywhere] * hbm + [VMEM] * (len(args) - 1 - hbm),
        out_specs=tuple([anywhere if hbm_out else VMEM] * len(out_shapes)),
        scratch_shapes=list(scratch),
        compiler_params=pltpu.CompilerParams(vmem_limit_bytes=mib * 1024 * 1024),
        cost_estimate=pl.CostEstimate(flops=0, bytes_accessed=moved, transcendentals=0),
    )(*args)


def shape(dims, dtype=BF):
    return jax.ShapeDtypeStruct(dims, dtype)


def mod4(v):
    return lax.rem(v + 8, 4)


def at(chunk, size):
    return pl.ds(pl.multiple_of(chunk * size, size), size)


def lanes_of(rows):
    return lax.broadcasted_iota(jnp.int32, (rows, 128), 1)


def combine_small(real_rows, imag_rows):
    lane = lanes_of(real_rows.shape[0])
    turned = jnp.where(lane < 32, -pltpu.roll(imag_rows, 96, 1), pltpu.roll(imag_rows, 32, 1))
    return jnp.where(lane < 64, real_rows + turned, 0.0)


def packed(block):
    half = block.shape[0] // 2
    return jnp.where(lanes_of(half) < 64, block[:half], pltpu.roll(block[half:], 64, 1))


def halves(block):
    return block, pltpu.roll(block, 64, 1)


def masked(block, first_row, rows_on, chunk, cols_on):
    row = first_row + lax.broadcasted_iota(jnp.int32, (64, 256), 0)
    col = chunk * 256 + lax.broadcasted_iota(jnp.int32, (64, 256), 1)
    return jnp.where((row < rows_on) & (col < cols_on), block.astype(F32), 0.0).astype(BF)


def prepare_kernel(s_ref, d_hbm, g_hbm, a_hbm, c_hbm, b_hbm, piece0, piece1, piece2, piece3,
                   a_even, c_even, g_pieces, g_odd,
                   d_ref, a_ref, c_ref, b_ref, a_first, c_first, g_first, sems):
    y, x = s_ref[0], s_ref[1]
    first_row = (y * 4 + x) * 64
    before, own, odd, after = s_ref[2], s_ref[3], s_ref[4], s_ref[5]
    copies = [
        pltpu.make_async_copy(source, target, sems.at[index])
        for index, (source, target) in enumerate(
            (
                (c_hbm.at[1, 0], c_ref.at[0]),
                (c_hbm.at[1, 1], c_ref.at[1]),
                (b_hbm, b_ref),
                (a_hbm.at[1, 0], a_ref.at[0]),
                (a_hbm.at[1, 1], a_ref.at[1]),
                (d_hbm.at[0, 0], d_ref.at[0]),
                (d_hbm.at[0, 1], d_ref.at[1]),
                (a_hbm.at[0], a_first),
                (c_hbm.at[0], c_first),
                (g_hbm.at[0], g_first),
                (g_hbm.at[1], g_odd),
            )
        )
    ]
    for copy in copies:
        copy.start()
    pieces = (piece0, piece1, piece2, piece3)
    row_b = first_row + lax.broadcasted_iota(jnp.int32, (64, 128), 0)
    lane = lanes_of(64)
    copies[0].wait()
    copies[1].wait()
    for shift, piece in enumerate(pieces):
        chunk = mod4(x + shift)
        for part in range(2):
            piece[:, pl.ds(part * 256, 256)] = masked(
                c_ref[part, :, at(chunk, 256)], first_row, odd, chunk, after
            )
    copies[2].wait()
    blocks = [
        jnp.where(row_b < rows_on, b_ref[which, part].astype(F32), 0.0)
        for which, part, rows_on in ((1, 0, odd), (1, 1, odd), (0, 0, own), (0, 1, own))
    ]
    for shift, piece in enumerate(pieces):
        chunk = mod4(x + shift)
        tile = jnp.zeros((64, 128), F32)
        for place, block in enumerate(blocks):
            turned = pltpu.roll(block, mod4(place - chunk) * 32, 1)
            tile = jnp.where((lane >= place * 32) & (lane < place * 32 + 32), turned, tile)
        piece[:, pl.ds(512, 128)] = tile.astype(BF)
    copies[3].wait()
    copies[4].wait()
    for shift, piece in enumerate(pieces):
        chunk = mod4(x + shift)
        for part in range(2):
            piece[:, pl.ds(640 + part * 256, 256)] = masked(
                a_ref[part, :, at(chunk, 256)], first_row, odd, chunk, own
            )
    copies[5].wait()
    copies[6].wait()
    for shift, piece in enumerate(pieces):
        chunk = mod4(x + shift)
        for part in range(2):
            piece[:, pl.ds(1152 + part * 256, 256)] = d_ref[part, :, at(chunk, 256)]
    copies[7].wait()
    copies[8].wait()
    for chunk in range(4):
        cols = pl.ds(chunk * 256, 256)
        for part in range(2):
            a_even[part, :, cols] = masked(a_first[part, :, cols], first_row, own, chunk, before)
            c_even[part, :, cols] = masked(c_first[part, :, cols], first_row, own, chunk, odd)
    copies[9].wait()
    for chunk in range(4):
        for part in range(2):
            g_pieces[chunk, part] = g_first[part, :, pl.ds(chunk * 256, 256)]
    copies[10].wait()


def assemble_kernel(s_ref, piece0, piece1, piece2, piece3, c_even, a_next,
                    panel, diagonal, couplings):
    y, x = s_ref[0], s_ref[1]
    for shift, piece in enumerate((piece0, piece1, piece2, piece3)):
        rows = at(mod4(x - shift), 64)
        panel[rows, :] = piece[:, pl.ds(0, 1152)]
        diagonal[rows, :] = piece[:, pl.ds(1152, 512)]
    couplings[0] = c_even[...]
    couplings[1] = a_next[...]


def stack_rows(x, blocks, held):
    for shift, block in enumerate(blocks):
        held[at(mod4(x - shift), 128), :] = block[...].reshape(128, 1024)


def wide_dot(y, held, panels, start, width):
    total = None
    for place, panel in enumerate(panels):
        term = jnp.dot(
            held[:, at(mod4(y + place), 256)],
            panel[pl.ds(0, 256), pl.ds(start, width)],
            preferred_element_type=F32,
        )
        total = term if total is None else total + term
    parts = total.reshape(4, 2, 64, width)
    return parts[:, 0].reshape(256, width), parts[:, 1].reshape(256, width)


def wide_product(y, held, panels, start=0):
    real_rows, imag_rows = wide_dot(y, held, panels, start, 512)
    real = real_rows[:, :256] - imag_rows[:, 256:]
    imag = real_rows[:, 256:] + imag_rows[:, :256]
    return real, imag


def small_product(y, held, panels):
    return combine_small(*wide_dot(y, held, panels, 512, 128))


def put_pair(out, real, imag):
    out[pl.ds(0, 256), pl.ds(0, 256)] = real.astype(out.dtype)
    out[pl.ds(0, 256), pl.ds(256, 256)] = imag.astype(out.dtype)


def odd_kernel(s_ref, g_ref, panel0, panel1, panel2, panel3, out, out_second, held):
    y, x = s_ref[0], s_ref[1]
    panels = (panel0, panel1, panel2, panel3)
    held[...] = g_ref[...].reshape(512, 1024)
    put_pair(out, *wide_product(y, held, panels))
    out[:, pl.ds(512, 128)] = small_product(y, held, panels).astype(BF)
    put_pair(out_second, *wide_product(y, held, panels, 640))
    out_second[pl.ds(256, 48), :] = jnp.zeros((48, 512), BF)


def even_kernel(s_ref, ca0, ca1, ca2, ca3, panel0, panel1, panel2, panel3, source,
                ship, upper_new, source_part, a_rows, c_rows):
    y, x = s_ref[0], s_ref[1]
    panels = (panel0, panel1, panel2, panel3)
    stack_rows(x, [block.at[1] for block in (ca0, ca1, ca2, ca3)], a_rows)
    stack_rows(x, [block.at[0] for block in (ca0, ca1, ca2, ca3)], c_rows)
    value = small_product(y, a_rows, panels)
    lane = lanes_of(32)
    for index in range(4):
        low, high = value[index * 64 : index * 64 + 32], value[index * 64 + 32 : index * 64 + 64]
        tile = jnp.where(lane < 64, low, pltpu.roll(high, 64, 1))
        ship[pl.ds(256, 32), pl.ds(index * 128, 128)] = tile.astype(BF)
    put_pair(ship, *wide_product(y, a_rows, panels))
    own = pltpu.roll(source[:, pl.ds(512, 128)].astype(F32), 64, 1)
    own = jnp.where(lanes_of(256) < 64, own, 0.0)
    source_part[...] = own - small_product(y, c_rows, panels)
    real, imag = wide_product(y, c_rows, panels)
    put_pair(upper_new, -real, -imag)


def diagonal_kernel(s_ref, c_rows, a_rows, panel0, panel1, panel2, panel3, diagonal, shipped,
                    out, lower):
    real, imag = wide_product(s_ref[0], c_rows, (panel0, panel1, panel2, panel3))
    real = diagonal[:, pl.ds(0, 256)].astype(F32) - real - shipped[pl.ds(0, 256), pl.ds(0, 256)].astype(F32)
    imag = diagonal[:, pl.ds(256, 256)].astype(F32) - imag - shipped[pl.ds(0, 256), pl.ds(256, 256)].astype(F32)
    put_pair(out, real, imag)
    real, imag = wide_product(s_ref[0], a_rows, (panel0, panel1, panel2, panel3))
    put_pair(lower, -real, -imag)


def pair_kernel(s_ref, lower, upper, out):
    out[:, pl.ds(0, 512)] = lower[...]
    out[:, pl.ds(512, 512)] = upper[...]


def block_product(block, right):
    real = jnp.dot(block[:, pl.ds(0, 256)], right, preferred_element_type=F32)
    imag = jnp.dot(block[:, pl.ds(256, 256)], right, preferred_element_type=F32)
    return real, imag


def put_partial(g_ref, right, own, send, whole):
    for index in range(4):
        total = jnp.dot(g_ref[index].reshape(512, 256), right, preferred_element_type=F32)
        parts = total.reshape(4, 2, 64, 128)
        value = combine_small(parts[:, 0].reshape(256, 128), parts[:, 1].reshape(256, 128))
        value = value.reshape(4, 64, 128)
        for group in range(4):
            whole[pl.ds(group * 256 + index * 64, 64), :] = value[group]
    total = packed(whole[...])
    own[...] = total
    send[...] = total.astype(BF)


def source_kernel(s_ref, g_ref, source_part, shipped, source_new, own, send, whole):
    lane = lanes_of(32)
    for index in range(4):
        tile = shipped[pl.ds(256, 32), pl.ds(index * 128, 128)].astype(F32)
        for half, moved in enumerate(halves(tile)):
            rows = pl.ds(index * 64 + half * 32, 32)
            value = source_part[rows, :] - jnp.where(lane < 64, moved, 0.0)
            source_new[rows, :] = value.astype(BF)
    source = source_new[...]
    put_partial(g_ref, source, own, send, whole)


def summed(own, got):
    total = own[...]
    for other in got:
        total = total + other[...].astype(F32)
    return total


def turn_kernel(s_ref, own, got1, got2, got3, *refs, first):
    solved = None if first else refs[0]
    blocks, refs = refs[:4] if first else refs[1:5], refs[4:] if first else refs[5:]
    source, g_ref, out, own_new, send, vector, whole = refs
    x = s_ref[1]
    total = summed(own, (got1, got2, got3))
    if not first:
        total = solved[...].astype(F32) + total
    out[...] = total.astype(BF)
    unpack(out, vector)
    residue = (source[...].astype(F32) - blocks_product(x, blocks, vector)).astype(BF)
    put_partial(g_ref, residue, own_new, send, whole)


def last_kernel(s_ref, own, got1, got2, got3, solved, out):
    out[...] = (solved[...].astype(F32) + summed(own, (got1, got2, got3))).astype(BF)


def diagonal_rows_kernel(s_ref, block0, block1, block2, block3, rows_out):
    x = s_ref[1]
    rows = at(x, 64)
    for shift, block in enumerate((block0, block1, block2, block3)):
        cols = at(mod4(x - shift), 256)
        rows_out[0, :, cols] = block[rows, pl.ds(0, 256)]
        rows_out[1, :, cols] = block[rows, pl.ds(256, 256)]


def coupling_rows_kernel(s_ref, pair0, pair1, pair2, pair3, lower_out, upper_out):
    x = s_ref[1]
    rows = at(x, 64)
    for shift, pair in enumerate((pair0, pair1, pair2, pair3)):
        cols = at(mod4(x - shift), 256)
        lower_out[0, :, cols] = pair[rows, pl.ds(0, 256)]
        lower_out[1, :, cols] = pair[rows, pl.ds(256, 256)]
        upper_out[0, :, cols] = pair[rows, pl.ds(512, 256)]
        upper_out[1, :, cols] = pair[rows, pl.ds(768, 256)]


def unpack(solved, vector):
    low, high = halves(solved[...].astype(F32))
    vector[pl.ds(0, 512), :] = low.astype(BF)
    vector[pl.ds(512, 512), :] = high.astype(BF)


def blocks_product(x, blocks, vector):
    real_rows = imag_rows = None
    for shift, block in enumerate(blocks):
        real, imag = block_product(block, vector[at(mod4(x - shift), 256), :])
        real_rows = real if real_rows is None else real_rows + real
        imag_rows = imag if imag_rows is None else imag_rows + imag
    return combine_small(real_rows, imag_rows)


def couple_kernel(s_ref, pair0, pair1, pair2, pair3, source, solved, below, above,
                  out0, out1, out2, out3, held, vector):
    y, x = s_ref[0], s_ref[1]
    pairs = (pair0, pair1, pair2, pair3)
    unpack(below, vector)
    combined = source[...].astype(F32)
    combined = combined - blocks_product(x, [p.at[:, pl.ds(0, 512)] for p in pairs], vector)
    unpack(above, vector)
    combined = combined - blocks_product(x, [p.at[:, pl.ds(512, 512)] for p in pairs], vector)
    rows = pl.ds(pl.multiple_of(lax.rem(y, 2) * 256, 256), 256)
    moved = pltpu.roll(solved[rows, :].astype(F32), jnp.where(y < 2, 64, 0), 1)
    held[...] = jnp.where(lanes_of(256) < 64, combined, moved)
    for shift, out in enumerate((out0, out1, out2, out3)):
        out[...] = held[at(mod4(x + shift), 64), :]


def spread_kernel(s_ref, piece0, piece1, piece2, piece3, combined, solved):
    x = s_ref[1]
    lane = lanes_of(64)
    totals = [jnp.zeros((64, 128), F32) for _ in range(4)]
    for shift, piece in enumerate((piece0, piece1, piece2, piece3)):
        chunk = mod4(x - shift)
        value = piece[...]
        on = (lane >= chunk * 32) & (lane < chunk * 32 + 32)
        for place in range(4):
            turned = pltpu.roll(value, mod4(chunk - place) * 32, 1)
            totals[place] = jnp.where(on, turned, totals[place])
    combined[0] = totals[0]
    combined[1] = totals[1]
    solved[0] = totals[2]
    solved[1] = totals[3]


def moved_x(block, by):
    pairs = [(y * 4 + x, y * 4 + (x + by) % 4) for y in range(4) for x in range(4)]
    return lax.ppermute(block, "row", pairs)


def moved_y(block, by):
    pairs = [(y * 4 + x, ((y + by) % 4) * 4 + x) for y in range(4) for x in range(4)]
    return lax.ppermute(block, "row", pairs)


def gathered_y(block):
    return (block, moved_y(block, 3), moved_y(block, 2), moved_y(block, 1))


def gathered_x(block):
    groups = [[y * 4 + x for x in range(4)] for y in range(4)]
    return lax.all_gather(block, "row", axis_index_groups=groups)


def along_cuts(block, by):
    count = lax.axis_size("cuts")
    pairs = [(i, i + by) for i in range(count) if 0 <= i + by < count]
    return lax.ppermute(block, "cuts", pairs)


def body(diagonal_blocks, diagonal_inverses, lower_blocks, upper_blocks, injection, orbitals):
    cut = lax.axis_index("cuts")
    place = lax.axis_index("row")
    zero = jnp.zeros((1,), jnp.int32)
    window = lax.dynamic_slice_in_dim(jnp.concatenate([zero, orbitals, zero]), 2 * cut, 4)
    scalars = jnp.concatenate([jnp.stack([place // 4, place % 4]).astype(jnp.int32), window])
    turns = (1, 2, 3)
    after = lax.optimization_barrier
    wide_flops = 2 * 512 * 1024 * 512
    solve_flops = 2 * 2048 * 256 * 128

    *pieces, a_even, c_even, g_pieces, g_odd = call(
        prepare_kernel,
        [shape((64, 1664))] * 4 + [shape((2, 64, 1024))] * 2 + [shape((4, 2, 64, 256))]
        + [shape((2, 64, 1024))],
        0,
        scalars, diagonal_blocks, diagonal_inverses, lower_blocks, upper_blocks, injection,
        hbm=5,
        scratch=[pltpu.VMEM((2, 64, 1024), BF)] * 3
        + [pltpu.VMEM((2, 2, 64, 128), BF)]
        + [pltpu.VMEM((2, 64, 1024), BF)] * 3
        + [pltpu.SemaphoreType.DMA((11,))],
    )
    pieces = [pieces[0]] + [moved_x(pieces[by], by) for by in turns]
    g_rows = gathered_x(g_odd)
    a_next = along_cuts(a_even, -1)
    groups = [[y * 4 + x for y in range(4)] for x in range(4)]
    g_columns = lax.all_to_all(
        g_pieces, "row", 0, 0, axis_index_groups=groups, tiled=True
    )
    a_next, g_columns, *pieces = after((a_next, g_columns, *pieces))
    panel, diagonal, couplings = call(
        assemble_kernel,
        [shape((256, 1152)), shape((256, 512)), shape((2, 2, 64, 1024))],
        0, scalars, *pieces, c_even, a_next,
    )
    g_columns = gathered_x(g_columns)
    panels = gathered_y(panel)
    ca_blocks = [couplings] + [moved_x(couplings, by) for by in turns]
    first, second = call(
        odd_kernel, [shape((256, 640)), shape((304, 512))], wide_flops,
        scalars, g_rows, *panels, scratch=[pltpu.VMEM((512, 1024), BF)],
    )
    firsts = gathered_y(first)
    second, g_columns, *ca_blocks = after((second, g_columns, *ca_blocks))
    seconds = gathered_y(second)
    ship, upper_new, source_part, a_rows, c_rows = call(
        even_kernel,
        [shape((288, 512)), shape((256, 512)), shape((256, 128), F32),
         shape((512, 1024)),
         shape((512, 1024))],
        2 * wide_flops,
        scalars, *ca_blocks, *firsts, panel,
    )
    shipped = along_cuts(ship, 1)
    diagonal_new, ship_lower = call(
        diagonal_kernel, [shape((256, 512))] * 2, 2 * wide_flops,
        scalars, c_rows, a_rows, *seconds, diagonal, shipped,
    )
    diagonals = [diagonal_new] + [moved_x(diagonal_new, by) for by in turns]
    packed_shapes = [shape((512, 128), F32), shape((512, 128))]
    whole = pltpu.VMEM((1024, 128), F32)
    vector = pltpu.VMEM((1024, 128), BF)
    source, own, send = call(
        source_kernel, [shape((256, 128))] + packed_shapes, solve_flops,
        scalars, g_columns, source_part, shipped, scratch=[whole],
    )
    got = gathered_y(send)[1:]
    lower_new = along_cuts(ship_lower, 1)
    (pair,) = call(pair_kernel, [shape((256, 1024))], 0, scalars, lower_new, upper_new)
    pairs = [pair] + [moved_x(pair, by) for by in turns]
    solved = ()
    for turn in range(REFINE):
        *solved, own, send = call(
            functools.partial(turn_kernel, first=turn == 0),
            [shape((512, 128))] + packed_shapes, 2 * solve_flops,
            scalars, own, *got, *solved, *diagonals, source, g_columns,
            scratch=[vector, whole],
        )
        got = gathered_y(send)[1:]
    (solved,) = call(
        last_kernel, [shape((512, 128))], 0,
        scalars, own, *got, *solved,
    )
    below, above = along_cuts(solved, 1), along_cuts(solved, -1)
    (diagonal_rows,) = call(
        diagonal_rows_kernel, [shape((2, 64, 1024))], 0, scalars, *diagonals
    )
    lower_rows, upper_rows = call(
        coupling_rows_kernel, [shape((2, 64, 1024))] * 2, 0, scalars, *pairs
    )
    ends = call(
        couple_kernel, [shape((64, 128), F32)] * 4, solve_flops // 2,
        scalars, *pairs, source, solved, below, above,
        scratch=[pltpu.VMEM((256, 128), F32), vector],
    )
    ends = [ends[0]] + [moved_x(ends[by], by) for by in turns]
    combined, solved_rows = call(
        spread_kernel, [shape((2, 64, 128), F32)] * 2, 0, scalars, *ends
    )
    return (
        diagonal_rows[None],
        lower_rows[None],
        upper_rows[None],
        combined[None],
        solved_rows[None],
    )


def solution(mesh):
    split = P("cuts", None, "row", None)
    return jax.shard_map(
        body,
        mesh=mesh,
        in_specs=(split, split, split, split, split, P()),
        out_specs=(split,) * 5,
        check_vma=False,
    )
```

```python
import functools

import jax
import jax.numpy as jnp
from jax import lax
from jax.experimental import pallas as pl
from jax.experimental.pallas import tpu as pltpu
from jax.sharding import PartitionSpec as P

REFINE = 2
BF = jnp.bfloat16
F32 = jnp.float32
VMEM = pl.BlockSpec(memory_space=pltpu.VMEM)
MIB = 24
SMEM = pl.BlockSpec(memory_space=pltpu.SMEM)


def call(kernel, out_shapes, flops, *args, scratch=(), hbm=0, mib=MIB, hbm_out=False):
    moved = sum(a.size * a.dtype.itemsize for a in args) + sum(
        s.size * s.dtype.itemsize for s in out_shapes
    )
    anywhere = pl.BlockSpec(memory_space=pltpu.HBM)
    args = [
        pltpu.with_memory_space_constraint(a, pltpu.HBM) if 0 < index <= hbm else a
        for index, a in enumerate(args)
    ]
    return pl.pallas_call(
        kernel,
        out_shape=tuple(out_shapes),
        in_specs=[SMEM] + [anywhere] * hbm + [VMEM] * (len(args) - 1 - hbm),
        out_specs=tuple([anywhere if hbm_out else VMEM] * len(out_shapes)),
        scratch_shapes=list(scratch),
        compiler_params=pltpu.CompilerParams(vmem_limit_bytes=mib * 1024 * 1024),
        cost_estimate=pl.CostEstimate(flops=0, bytes_accessed=moved, transcendentals=0),
    )(*args)


def shape(dims, dtype=BF):
    return jax.ShapeDtypeStruct(dims, dtype)


def mod4(v):
    return lax.rem(v + 8, 4)


def at(chunk, size):
    return pl.ds(pl.multiple_of(chunk * size, size), size)


def lanes_of(rows):
    return lax.broadcasted_iota(jnp.int32, (rows, 128), 1)


def combine_small(real_rows, imag_rows):
    lane = lanes_of(real_rows.shape[0])
    turned = jnp.where(lane < 32, -pltpu.roll(imag_rows, 96, 1), pltpu.roll(imag_rows, 32, 1))
    return jnp.where(lane < 64, real_rows + turned, 0.0)


def packed(block):
    half = block.shape[0] // 2
    return jnp.where(lanes_of(half) < 64, block[:half], pltpu.roll(block[half:], 64, 1))


def halves(block):
    return block, pltpu.roll(block, 64, 1)


def masked(block, first_row, rows_on, chunk, cols_on):
    row = first_row + lax.broadcasted_iota(jnp.int32, (64, 256), 0)
    col = chunk * 256 + lax.broadcasted_iota(jnp.int32, (64, 256), 1)
    return jnp.where((row < rows_on) & (col < cols_on), block.astype(F32), 0.0).astype(BF)


def prepare_kernel(s_ref, d_hbm, g_hbm, a_hbm, c_hbm, b_hbm, piece0, piece1, piece2, piece3,
                   a_even, c_even, g_pieces, g_odd,
                   d_ref, a_ref, c_ref, b_ref, a_first, c_first, g_first, sems):
    y, x = s_ref[0], s_ref[1]
    first_row = (y * 4 + x) * 64
    before, own, odd, after = s_ref[2], s_ref[3], s_ref[4], s_ref[5]
    copies = [
        pltpu.make_async_copy(source, target, sems.at[index])
        for index, (source, target) in enumerate(
            (
                (c_hbm.at[1, 0], c_ref.at[0]),
                (c_hbm.at[1, 1], c_ref.at[1]),
                (b_hbm, b_ref),
                (a_hbm.at[1, 0], a_ref.at[0]),
                (a_hbm.at[1, 1], a_ref.at[1]),
                (d_hbm.at[0, 0], d_ref.at[0]),
                (d_hbm.at[0, 1], d_ref.at[1]),
                (a_hbm.at[0], a_first),
                (c_hbm.at[0], c_first),
                (g_hbm.at[0], g_first),
                (g_hbm.at[1], g_odd),
            )
        )
    ]
    for copy in copies:
        copy.start()
    pieces = (piece0, piece1, piece2, piece3)
    row_b = first_row + lax.broadcasted_iota(jnp.int32, (64, 128), 0)
    lane = lanes_of(64)
    copies[0].wait()
    copies[1].wait()
    for shift, piece in enumerate(pieces):
        chunk = mod4(x + shift)
        for part in range(2):
            piece[:, pl.ds(part * 256, 256)] = masked(
                c_ref[part, :, at(chunk, 256)], first_row, odd, chunk, after
            )
    copies[2].wait()
    blocks = [
        jnp.where(row_b < rows_on, b_ref[which, part].astype(F32), 0.0)
        for which, part, rows_on in ((1, 0, odd), (1, 1, odd), (0, 0, own), (0, 1, own))
    ]
    for shift, piece in enumerate(pieces):
        chunk = mod4(x + shift)
        tile = jnp.zeros((64, 128), F32)
        for place, block in enumerate(blocks):
            turned = pltpu.roll(block, mod4(place - chunk) * 32, 1)
            tile = jnp.where((lane >= place * 32) & (lane < place * 32 + 32), turned, tile)
        piece[:, pl.ds(512, 128)] = tile.astype(BF)
    copies[3].wait()
    copies[4].wait()
    for shift, piece in enumerate(pieces):
        chunk = mod4(x + shift)
        for part in range(2):
            piece[:, pl.ds(640 + part * 256, 256)] = masked(
                a_ref[part, :, at(chunk, 256)], first_row, odd, chunk, own
            )
    copies[5].wait()
    copies[6].wait()
    for shift, piece in enumerate(pieces):
        chunk = mod4(x + shift)
        for part in range(2):
            piece[:, pl.ds(1152 + part * 256, 256)] = d_ref[part, :, at(chunk, 256)]
    copies[7].wait()
    copies[8].wait()
    for chunk in range(4):
        cols = pl.ds(chunk * 256, 256)
        for part in range(2):
            a_even[part, :, cols] = masked(a_first[part, :, cols], first_row, own, chunk, before)
            c_even[part, :, cols] = masked(c_first[part, :, cols], first_row, own, chunk, odd)
    copies[9].wait()
    for chunk in range(4):
        for part in range(2):
            g_pieces[chunk, part] = g_first[part, :, pl.ds(chunk * 256, 256)]
    copies[10].wait()


def assemble_kernel(s_ref, piece0, piece1, piece2, piece3, c_even, a_next,
                    panel, diagonal, couplings):
    y, x = s_ref[0], s_ref[1]
    for shift, piece in enumerate((piece0, piece1, piece2, piece3)):
        rows = at(mod4(x - shift), 64)
        panel[rows, :] = piece[:, pl.ds(0, 1152)]
        diagonal[rows, :] = piece[:, pl.ds(1152, 512)]
    couplings[0] = c_even[...]
    couplings[1] = a_next[...]


def stack_rows(x, blocks, held):
    for shift, block in enumerate(blocks):
        held[at(mod4(x - shift), 128), :] = block[...].reshape(128, 1024)


def wide_dot(y, held, panels, start, width):
    total = None
    for place, panel in enumerate(panels):
        term = jnp.dot(
            held[:, at(mod4(y + place), 256)],
            panel[pl.ds(0, 256), pl.ds(start, width)],
            preferred_element_type=F32,
        )
        total = term if total is None else total + term
    parts = total.reshape(4, 2, 64, width)
    return parts[:, 0].reshape(256, width), parts[:, 1].reshape(256, width)


def wide_product(y, held, panels, start=0):
    real_rows, imag_rows = wide_dot(y, held, panels, start, 512)
    real = real_rows[:, :256] - imag_rows[:, 256:]
    imag = real_rows[:, 256:] + imag_rows[:, :256]
    return real, imag


def small_product(y, held, panels):
    return combine_small(*wide_dot(y, held, panels, 512, 128))


def put_pair(out, real, imag):
    out[pl.ds(0, 256), pl.ds(0, 256)] = real.astype(out.dtype)
    out[pl.ds(0, 256), pl.ds(256, 256)] = imag.astype(out.dtype)


def odd_kernel(s_ref, g_ref, panel0, panel1, panel3, low, high, out, out_second, held, panel2):
    y, x = s_ref[0], s_ref[1]
    panel2[pl.ds(0, 128), :] = low[...]
    panel2[pl.ds(128, 128), :] = high[...]
    panels = (panel0, panel1, panel2, panel3)
    held[...] = g_ref[...].reshape(512, 1024)
    put_pair(out, *wide_product(y, held, panels))
    out[:, pl.ds(512, 128)] = small_product(y, held, panels).astype(BF)
    put_pair(out_second, *wide_product(y, held, panels, 640))
    out_second[pl.ds(256, 48), :] = jnp.zeros((48, 512), BF)


def even_kernel(s_ref, ca0, ca1, ca2, ca3, panel0, panel1, panel2, panel3, source,
                ship, upper_new, source_part, a_rows, c_rows):
    y, x = s_ref[0], s_ref[1]
    panels = (panel0, panel1, panel2, panel3)
    stack_rows(x, [block.at[1] for block in (ca0, ca1, ca2, ca3)], a_rows)
    stack_rows(x, [block.at[0] for block in (ca0, ca1, ca2, ca3)], c_rows)
    value = small_product(y, a_rows, panels)
    lane = lanes_of(32)
    for index in range(4):
        low, high = value[index * 64 : index * 64 + 32], value[index * 64 + 32 : index * 64 + 64]
        tile = jnp.where(lane < 64, low, pltpu.roll(high, 64, 1))
        ship[pl.ds(256, 32), pl.ds(index * 128, 128)] = tile.astype(BF)
    put_pair(ship, *wide_product(y, a_rows, panels))
    own = pltpu.roll(source[:, pl.ds(512, 128)].astype(F32), 64, 1)
    own = jnp.where(lanes_of(256) < 64, own, 0.0)
    source_part[...] = own - small_product(y, c_rows, panels)
    real, imag = wide_product(y, c_rows, panels)
    put_pair(upper_new, -real, -imag)


def diagonal_kernel(s_ref, c_rows, a_rows, panel0, panel1, panel2, panel3, diagonal, shipped,
                    out, lower):
    real, imag = wide_product(s_ref[0], c_rows, (panel0, panel1, panel2, panel3))
    real = diagonal[:, pl.ds(0, 256)].astype(F32) - real - shipped[pl.ds(0, 256), pl.ds(0, 256)].astype(F32)
    imag = diagonal[:, pl.ds(256, 256)].astype(F32) - imag - shipped[pl.ds(0, 256), pl.ds(256, 256)].astype(F32)
    put_pair(out, real, imag)
    real, imag = wide_product(s_ref[0], a_rows, (panel0, panel1, panel2, panel3))
    put_pair(lower, -real, -imag)


def pair_kernel(s_ref, lower, upper, out):
    out[:, pl.ds(0, 512)] = lower[...]
    out[:, pl.ds(512, 512)] = upper[...]


def block_product(block, right):
    real = jnp.dot(block[:, pl.ds(0, 256)], right, preferred_element_type=F32)
    imag = jnp.dot(block[:, pl.ds(256, 256)], right, preferred_element_type=F32)
    return real, imag


def put_partial(g_ref, right, own, send, whole):
    for index in range(4):
        total = jnp.dot(g_ref[index].reshape(512, 256), right, preferred_element_type=F32)
        parts = total.reshape(4, 2, 64, 128)
        value = combine_small(parts[:, 0].reshape(256, 128), parts[:, 1].reshape(256, 128))
        value = value.reshape(4, 64, 128)
        for group in range(4):
            whole[pl.ds(group * 256 + index * 64, 64), :] = value[group]
    total = packed(whole[...])
    own[...] = total
    send[...] = total.astype(BF)


def source_kernel(s_ref, g_ref, source_part, shipped, source_new, own, send, whole):
    lane = lanes_of(32)
    for index in range(4):
        tile = shipped[pl.ds(256, 32), pl.ds(index * 128, 128)].astype(F32)
        for half, moved in enumerate(halves(tile)):
            rows = pl.ds(index * 64 + half * 32, 32)
            value = source_part[rows, :] - jnp.where(lane < 64, moved, 0.0)
            source_new[rows, :] = value.astype(BF)
    source = source_new[...]
    put_partial(g_ref, source, own, send, whole)


def summed(own, got):
    total = own[...]
    for other in got:
        total = total + other[...].astype(F32)
    return total


def turn_kernel(s_ref, own, got1, got2, got3, *refs, first):
    solved = None if first else refs[0]
    blocks, refs = refs[:4] if first else refs[1:5], refs[4:] if first else refs[5:]
    source, g_ref, out, own_new, send, vector, whole = refs
    x = s_ref[1]
    total = summed(own, (got1, got2, got3))
    if not first:
        total = solved[...].astype(F32) + total
    out[...] = total.astype(BF)
    unpack(out, vector)
    residue = (source[...].astype(F32) - blocks_product(x, blocks, vector)).astype(BF)
    put_partial(g_ref, residue, own_new, send, whole)


def last_kernel(s_ref, own, got1, got2, got3, solved, out):
    out[...] = (solved[...].astype(F32) + summed(own, (got1, got2, got3))).astype(BF)


def diagonal_rows_kernel(s_ref, block0, block1, block2, block3, rows_out):
    x = s_ref[1]
    rows = at(x, 64)
    for shift, block in enumerate((block0, block1, block2, block3)):
        cols = at(mod4(x - shift), 256)
        rows_out[0, :, cols] = block[rows, pl.ds(0, 256)]
        rows_out[1, :, cols] = block[rows, pl.ds(256, 256)]


def coupling_rows_kernel(s_ref, pair0, pair1, pair2, pair3, lower_out, upper_out):
    x = s_ref[1]
    rows = at(x, 64)
    for shift, pair in enumerate((pair0, pair1, pair2, pair3)):
        cols = at(mod4(x - shift), 256)
        lower_out[0, :, cols] = pair[rows, pl.ds(0, 256)]
        lower_out[1, :, cols] = pair[rows, pl.ds(256, 256)]
        upper_out[0, :, cols] = pair[rows, pl.ds(512, 256)]
        upper_out[1, :, cols] = pair[rows, pl.ds(768, 256)]


def unpack(solved, vector):
    low, high = halves(solved[...].astype(F32))
    vector[pl.ds(0, 512), :] = low.astype(BF)
    vector[pl.ds(512, 512), :] = high.astype(BF)


def blocks_product(x, blocks, vector):
    real_rows = imag_rows = None
    for shift, block in enumerate(blocks):
        real, imag = block_product(block, vector[at(mod4(x - shift), 256), :])
        real_rows = real if real_rows is None else real_rows + real
        imag_rows = imag if imag_rows is None else imag_rows + imag
    return combine_small(real_rows, imag_rows)


def couple_kernel(s_ref, pair0, pair1, pair2, pair3, source, solved, below, above,
                  out0, out1, out2, out3, held, vector):
    y, x = s_ref[0], s_ref[1]
    pairs = (pair0, pair1, pair2, pair3)
    unpack(below, vector)
    combined = source[...].astype(F32)
    combined = combined - blocks_product(x, [p.at[:, pl.ds(0, 512)] for p in pairs], vector)
    unpack(above, vector)
    combined = combined - blocks_product(x, [p.at[:, pl.ds(512, 512)] for p in pairs], vector)
    rows = pl.ds(pl.multiple_of(lax.rem(y, 2) * 256, 256), 256)
    moved = pltpu.roll(solved[rows, :].astype(F32), jnp.where(y < 2, 64, 0), 1)
    held[...] = jnp.where(lanes_of(256) < 64, combined, moved)
    for shift, out in enumerate((out0, out1, out2, out3)):
        out[...] = held[at(mod4(x + shift), 64), :]


def spread_kernel(s_ref, piece0, piece1, piece2, piece3, combined, solved):
    x = s_ref[1]
    lane = lanes_of(64)
    totals = [jnp.zeros((64, 128), F32) for _ in range(4)]
    for shift, piece in enumerate((piece0, piece1, piece2, piece3)):
        chunk = mod4(x - shift)
        value = piece[...]
        on = (lane >= chunk * 32) & (lane < chunk * 32 + 32)
        for place in range(4):
            turned = pltpu.roll(value, mod4(chunk - place) * 32, 1)
            totals[place] = jnp.where(on, turned, totals[place])
    combined[0] = totals[0]
    combined[1] = totals[1]
    solved[0] = totals[2]
    solved[1] = totals[3]


def moved_x(block, by):
    pairs = [(y * 4 + x, y * 4 + (x + by) % 4) for y in range(4) for x in range(4)]
    return lax.ppermute(block, "row", pairs)


def moved_y(block, by):
    pairs = [(y * 4 + x, ((y + by) % 4) * 4 + x) for y in range(4) for x in range(4)]
    return lax.ppermute(block, "row", pairs)


def gathered_y(block):
    return (block, moved_y(block, 3), moved_y(block, 2), moved_y(block, 1))


def split_kernel(s_ref, block, other, low, high):
    low[...] = block[pl.ds(0, 128), :]
    high[...] = other[pl.ds(128, 128), :]


def ring_gathered_y(scalars, block):
    above, below = moved_y(block, 3), moved_y(block, 1)
    half = shape((128, block.shape[1]))
    low, high = call(split_kernel, [half, half], 0, scalars, below, above)
    return block, above, below, moved_y(low, 1), moved_y(high, 3)


def gathered_x(block):
    groups = [[y * 4 + x for x in range(4)] for y in range(4)]
    return lax.all_gather(block, "row", axis_index_groups=groups)


def along_cuts(block, by):
    count = lax.axis_size("cuts")
    pairs = [(i, i + by) for i in range(count) if 0 <= i + by < count]
    return lax.ppermute(block, "cuts", pairs)


def body(diagonal_blocks, diagonal_inverses, lower_blocks, upper_blocks, injection, orbitals):
    cut = lax.axis_index("cuts")
    place = lax.axis_index("row")
    zero = jnp.zeros((1,), jnp.int32)
    window = lax.dynamic_slice_in_dim(jnp.concatenate([zero, orbitals, zero]), 2 * cut, 4)
    scalars = jnp.concatenate([jnp.stack([place // 4, place % 4]).astype(jnp.int32), window])
    turns = (1, 2, 3)
    after = lax.optimization_barrier
    wide_flops = 2 * 512 * 1024 * 512
    solve_flops = 2 * 2048 * 256 * 128

    *pieces, a_even, c_even, g_pieces, g_odd = call(
        prepare_kernel,
        [shape((64, 1664))] * 4 + [shape((2, 64, 1024))] * 2 + [shape((4, 2, 64, 256))]
        + [shape((2, 64, 1024))],
        0,
        scalars, diagonal_blocks, diagonal_inverses, lower_blocks, upper_blocks, injection,
        hbm=5,
        scratch=[pltpu.VMEM((2, 64, 1024), BF)] * 3
        + [pltpu.VMEM((2, 2, 64, 128), BF)]
        + [pltpu.VMEM((2, 64, 1024), BF)] * 3
        + [pltpu.SemaphoreType.DMA((11,))],
    )
    pieces = [pieces[0]] + [moved_x(pieces[by], by) for by in turns]
    g_rows = gathered_x(g_odd)
    a_next = along_cuts(a_even, -1)
    groups = [[y * 4 + x for y in range(4)] for x in range(4)]
    g_columns = lax.all_to_all(
        g_pieces, "row", 0, 0, axis_index_groups=groups, tiled=True
    )
    a_next, g_columns, *pieces = after((a_next, g_columns, *pieces))
    panel, diagonal, couplings = call(
        assemble_kernel,
        [shape((256, 1152)), shape((256, 512)), shape((2, 2, 64, 1024))],
        0, scalars, *pieces, c_even, a_next,
    )
    g_columns = gathered_x(g_columns)
    panels = ring_gathered_y(scalars, panel)
    ca_blocks = [couplings] + [moved_x(couplings, by) for by in turns]
    first, second = call(
        odd_kernel, [shape((256, 640)), shape((304, 512))], wide_flops,
        scalars, g_rows, *panels,
        scratch=[pltpu.VMEM((512, 1024), BF), pltpu.VMEM((256, 1152), BF)],
    )
    firsts = gathered_y(first)
    second, g_columns, *ca_blocks = after((second, g_columns, *ca_blocks))
    seconds = gathered_y(second)
    ship, upper_new, source_part, a_rows, c_rows = call(
        even_kernel,
        [shape((288, 512)), shape((256, 512)), shape((256, 128), F32),
         shape((512, 1024)),
         shape((512, 1024))],
        2 * wide_flops,
        scalars, *ca_blocks, *firsts, panel,
    )
    shipped = along_cuts(ship, 1)
    diagonal_new, ship_lower = call(
        diagonal_kernel, [shape((256, 512))] * 2, 2 * wide_flops,
        scalars, c_rows, a_rows, *seconds, diagonal, shipped,
    )
    diagonals = [diagonal_new] + [moved_x(diagonal_new, by) for by in turns]
    packed_shapes = [shape((512, 128), F32), shape((512, 128))]
    whole = pltpu.VMEM((1024, 128), F32)
    vector = pltpu.VMEM((1024, 128), BF)
    source, own, send = call(
        source_kernel, [shape((256, 128))] + packed_shapes, solve_flops,
        scalars, g_columns, source_part, shipped, scratch=[whole],
    )
    got = gathered_y(send)[1:]
    lower_new = along_cuts(ship_lower, 1)
    (pair,) = call(pair_kernel, [shape((256, 1024))], 0, scalars, lower_new, upper_new)
    pairs = [pair] + [moved_x(pair, by) for by in turns]
    solved = ()
    for turn in range(REFINE):
        *solved, own, send = call(
            functools.partial(turn_kernel, first=turn == 0),
            [shape((512, 128))] + packed_shapes, 2 * solve_flops,
            scalars, own, *got, *solved, *diagonals, source, g_columns,
            scratch=[vector, whole],
        )
        got = gathered_y(send)[1:]
    (solved,) = call(
        last_kernel, [shape((512, 128))], 0,
        scalars, own, *got, *solved,
    )
    below, above = along_cuts(solved, 1), along_cuts(solved, -1)
    (diagonal_rows,) = call(
        diagonal_rows_kernel, [shape((2, 64, 1024))], 0, scalars, *diagonals
    )
    lower_rows, upper_rows = call(
        coupling_rows_kernel, [shape((2, 64, 1024))] * 2, 0, scalars, *pairs
    )
    ends = call(
        couple_kernel, [shape((64, 128), F32)] * 4, solve_flops // 2,
        scalars, *pairs, source, solved, below, above,
        scratch=[pltpu.VMEM((256, 128), F32), vector],
    )
    ends = [ends[0]] + [moved_x(ends[by], by) for by in turns]
    combined, solved_rows = call(
        spread_kernel, [shape((2, 64, 128), F32)] * 2, 0, scalars, *ends
    )
    return (
        diagonal_rows[None],
        lower_rows[None],
        upper_rows[None],
        combined[None],
        solved_rows[None],
    )


def solution(mesh):
    split = P("cuts", None, "row", None)
    return jax.shard_map(
        body,
        mesh=mesh,
        in_specs=(split, split, split, split, split, P()),
        out_specs=(split,) * 5,
        check_vma=False,
    )
```

```python
import functools

import jax
import jax.numpy as jnp
from jax import lax
from jax.experimental import pallas as pl
from jax.experimental.pallas import tpu as pltpu
from jax.sharding import PartitionSpec as P

REFINE = 2
BF = jnp.bfloat16
F32 = jnp.float32
VMEM = pl.BlockSpec(memory_space=pltpu.VMEM)
MIB = 12
SMEM = pl.BlockSpec(memory_space=pltpu.SMEM)


def call(kernel, out_shapes, flops, *args, scratch=(), hbm=0, mib=MIB, hbm_out=False):
    moved = sum(a.size * a.dtype.itemsize for a in args) + sum(
        s.size * s.dtype.itemsize for s in out_shapes
    )
    anywhere = pl.BlockSpec(memory_space=pltpu.HBM)
    args = [
        pltpu.with_memory_space_constraint(a, pltpu.HBM) if 0 < index <= hbm else a
        for index, a in enumerate(args)
    ]
    return pl.pallas_call(
        kernel,
        out_shape=tuple(out_shapes),
        in_specs=[SMEM] + [anywhere] * hbm + [VMEM] * (len(args) - 1 - hbm),
        out_specs=tuple([anywhere if hbm_out else VMEM] * len(out_shapes)),
        scratch_shapes=list(scratch),
        compiler_params=pltpu.CompilerParams(vmem_limit_bytes=mib * 1024 * 1024),
        cost_estimate=pl.CostEstimate(flops=0, bytes_accessed=moved, transcendentals=0),
    )(*args)


def shape(dims, dtype=BF):
    return jax.ShapeDtypeStruct(dims, dtype)


def mod4(v):
    return lax.rem(v + 8, 4)


def at(chunk, size):
    return pl.ds(pl.multiple_of(chunk * size, size), size)


def lanes_of(rows):
    return lax.broadcasted_iota(jnp.int32, (rows, 128), 1)


def combine_small(real_rows, imag_rows):
    lane = lanes_of(real_rows.shape[0])
    turned = jnp.where(lane < 32, -pltpu.roll(imag_rows, 96, 1), pltpu.roll(imag_rows, 32, 1))
    return jnp.where(lane < 64, real_rows + turned, 0.0)


def packed(block):
    half = block.shape[0] // 2
    return jnp.where(lanes_of(half) < 64, block[:half], pltpu.roll(block[half:], 64, 1))


def halves(block):
    return block, pltpu.roll(block, 64, 1)


def masked(block, first_row, rows_on, chunk, cols_on):
    row = first_row + lax.broadcasted_iota(jnp.int32, (64, 256), 0)
    col = chunk * 256 + lax.broadcasted_iota(jnp.int32, (64, 256), 1)
    return jnp.where((row < rows_on) & (col < cols_on), block.astype(F32), 0.0).astype(BF)


def prepare_kernel(s_ref, d_hbm, g_hbm, a_hbm, c_hbm, b_hbm, piece0, piece1, piece2, piece3,
                   a_even, c_even, g_pieces, g_odd,
                   d_ref, a_ref, c_ref, b_ref, a_first, c_first, g_first, sems):
    y, x = s_ref[0], s_ref[1]
    first_row = (y * 4 + x) * 64
    before, own, odd, after = s_ref[2], s_ref[3], s_ref[4], s_ref[5]
    copies = [
        pltpu.make_async_copy(source, target, sems.at[index])
        for index, (source, target) in enumerate(
            (
                (c_hbm.at[1, 0], c_ref.at[0]),
                (c_hbm.at[1, 1], c_ref.at[1]),
                (b_hbm, b_ref),
                (a_hbm.at[1, 0], a_ref.at[0]),
                (a_hbm.at[1, 1], a_ref.at[1]),
                (d_hbm.at[0, 0], d_ref.at[0]),
                (d_hbm.at[0, 1], d_ref.at[1]),
                (a_hbm.at[0], a_first),
                (c_hbm.at[0], c_first),
                (g_hbm.at[0], g_first),
                (g_hbm.at[1], g_odd),
            )
        )
    ]
    for copy in copies:
        copy.start()
    pieces = (piece0, piece1, piece2, piece3)
    row_b = first_row + lax.broadcasted_iota(jnp.int32, (64, 128), 0)
    lane = lanes_of(64)
    copies[0].wait()
    copies[1].wait()
    for shift, piece in enumerate(pieces):
        chunk = mod4(x + shift)
        for part in range(2):
            piece[:, pl.ds(part * 256, 256)] = masked(
                c_ref[part, :, at(chunk, 256)], first_row, odd, chunk, after
            )
    copies[2].wait()
    blocks = [
        jnp.where(row_b < rows_on, b_ref[which, part].astype(F32), 0.0)
        for which, part, rows_on in ((1, 0, odd), (1, 1, odd), (0, 0, own), (0, 1, own))
    ]
    for shift, piece in enumerate(pieces):
        chunk = mod4(x + shift)
        tile = jnp.zeros((64, 128), F32)
        for place, block in enumerate(blocks):
            turned = pltpu.roll(block, mod4(place - chunk) * 32, 1)
            tile = jnp.where((lane >= place * 32) & (lane < place * 32 + 32), turned, tile)
        piece[:, pl.ds(512, 128)] = tile.astype(BF)
    copies[3].wait()
    copies[4].wait()
    for shift, piece in enumerate(pieces):
        chunk = mod4(x + shift)
        for part in range(2):
            piece[:, pl.ds(640 + part * 256, 256)] = masked(
                a_ref[part, :, at(chunk, 256)], first_row, odd, chunk, own
            )
    copies[5].wait()
    copies[6].wait()
    for shift, piece in enumerate(pieces):
        chunk = mod4(x + shift)
        for part in range(2):
            piece[:, pl.ds(1152 + part * 256, 256)] = d_ref[part, :, at(chunk, 256)]
    copies[7].wait()
    copies[8].wait()
    for chunk in range(4):
        cols = pl.ds(chunk * 256, 256)
        for part in range(2):
            a_even[part, :, cols] = masked(a_first[part, :, cols], first_row, own, chunk, before)
            c_even[part, :, cols] = masked(c_first[part, :, cols], first_row, own, chunk, odd)
    copies[9].wait()
    for chunk in range(4):
        for part in range(2):
            g_pieces[chunk, part] = g_first[part, :, pl.ds(chunk * 256, 256)]
    copies[10].wait()


def assemble_kernel(s_ref, piece0, piece1, piece2, piece3, c_even, a_next,
                    panel, diagonal, couplings):
    y, x = s_ref[0], s_ref[1]
    for shift, piece in enumerate((piece0, piece1, piece2, piece3)):
        rows = at(mod4(x - shift), 64)
        panel[rows, :] = piece[:, pl.ds(0, 1152)]
        diagonal[rows, :] = piece[:, pl.ds(1152, 512)]
    couplings[0] = c_even[...]
    couplings[1] = a_next[...]


def stack_rows(x, blocks, held):
    for shift, block in enumerate(blocks):
        held[at(mod4(x - shift), 128), :] = block[...].reshape(128, 1024)


def wide_dot(y, held, panels, start, width):
    total = None
    for place, panel in enumerate(panels):
        term = jnp.dot(
            held[:, at(mod4(y + place), 256)],
            panel[pl.ds(0, 256), pl.ds(start, width)],
            preferred_element_type=F32,
        )
        total = term if total is None else total + term
    parts = total.reshape(4, 2, 64, width)
    return parts[:, 0].reshape(256, width), parts[:, 1].reshape(256, width)


def wide_product(y, held, panels, start=0):
    real_rows, imag_rows = wide_dot(y, held, panels, start, 512)
    real = real_rows[:, :256] - imag_rows[:, 256:]
    imag = real_rows[:, 256:] + imag_rows[:, :256]
    return real, imag


def small_product(y, held, panels):
    return combine_small(*wide_dot(y, held, panels, 512, 128))


def put_pair(out, real, imag):
    out[pl.ds(0, 256), pl.ds(0, 256)] = real.astype(out.dtype)
    out[pl.ds(0, 256), pl.ds(256, 256)] = imag.astype(out.dtype)


def odd_kernel(s_ref, g_ref, panel0, panel1, panel3, low, high, out, out_second, held, panel2):
    y, x = s_ref[0], s_ref[1]
    panel2[pl.ds(0, 128), :] = low[...]
    panel2[pl.ds(128, 128), :] = high[...]
    panels = (panel0, panel1, panel2, panel3)
    held[...] = g_ref[...].reshape(512, 1024)
    put_pair(out, *wide_product(y, held, panels))
    out[:, pl.ds(512, 128)] = small_product(y, held, panels).astype(BF)
    put_pair(out_second, *wide_product(y, held, panels, 640))
    out_second[pl.ds(256, 48), :] = jnp.zeros((48, 512), BF)


def even_kernel(s_ref, ca0, ca1, ca2, ca3, panel0, panel1, panel2, panel3, source,
                ship, upper_new, source_part, a_rows, c_rows):
    y, x = s_ref[0], s_ref[1]
    panels = (panel0, panel1, panel2, panel3)
    stack_rows(x, [block.at[1] for block in (ca0, ca1, ca2, ca3)], a_rows)
    stack_rows(x, [block.at[0] for block in (ca0, ca1, ca2, ca3)], c_rows)
    value = small_product(y, a_rows, panels)
    lane = lanes_of(32)
    for index in range(4):
        low, high = value[index * 64 : index * 64 + 32], value[index * 64 + 32 : index * 64 + 64]
        tile = jnp.where(lane < 64, low, pltpu.roll(high, 64, 1))
        ship[pl.ds(256, 32), pl.ds(index * 128, 128)] = tile.astype(BF)
    put_pair(ship, *wide_product(y, a_rows, panels))
    own = pltpu.roll(source[:, pl.ds(512, 128)].astype(F32), 64, 1)
    own = jnp.where(lanes_of(256) < 64, own, 0.0)
    source_part[...] = own - small_product(y, c_rows, panels)
    real, imag = wide_product(y, c_rows, panels)
    put_pair(upper_new, -real, -imag)


def diagonal_kernel(s_ref, c_rows, a_rows, panel0, panel1, panel2, panel3, diagonal, shipped,
                    out, lower):
    real, imag = wide_product(s_ref[0], c_rows, (panel0, panel1, panel2, panel3))
    real = diagonal[:, pl.ds(0, 256)].astype(F32) - real - shipped[pl.ds(0, 256), pl.ds(0, 256)].astype(F32)
    imag = diagonal[:, pl.ds(256, 256)].astype(F32) - imag - shipped[pl.ds(0, 256), pl.ds(256, 256)].astype(F32)
    put_pair(out, real, imag)
    real, imag = wide_product(s_ref[0], a_rows, (panel0, panel1, panel2, panel3))
    put_pair(lower, -real, -imag)


def pair_kernel(s_ref, lower, upper, out):
    out[:, pl.ds(0, 512)] = lower[...]
    out[:, pl.ds(512, 512)] = upper[...]


def block_product(block, right):
    real = jnp.dot(block[:, pl.ds(0, 256)], right, preferred_element_type=F32)
    imag = jnp.dot(block[:, pl.ds(256, 256)], right, preferred_element_type=F32)
    return real, imag


def put_partial(g_ref, right, own, send, whole):
    for index in range(4):
        total = jnp.dot(g_ref[index].reshape(512, 256), right, preferred_element_type=F32)
        parts = total.reshape(4, 2, 64, 128)
        value = combine_small(parts[:, 0].reshape(256, 128), parts[:, 1].reshape(256, 128))
        value = value.reshape(4, 64, 128)
        for group in range(4):
            whole[pl.ds(group * 256 + index * 64, 64), :] = value[group]
    total = packed(whole[...])
    own[...] = total
    send[...] = total.astype(BF)


def source_kernel(s_ref, g_ref, source_part, shipped, source_new, own, send, whole):
    lane = lanes_of(32)
    for index in range(4):
        tile = shipped[pl.ds(256, 32), pl.ds(index * 128, 128)].astype(F32)
        for half, moved in enumerate(halves(tile)):
            rows = pl.ds(index * 64 + half * 32, 32)
            value = source_part[rows, :] - jnp.where(lane < 64, moved, 0.0)
            source_new[rows, :] = value.astype(BF)
    source = source_new[...]
    put_partial(g_ref, source, own, send, whole)


def summed(own, got):
    total = own[...]
    for other in got:
        total = total + other[...].astype(F32)
    return total


def turn_kernel(s_ref, own, got1, got2, got3, *refs, first):
    solved = None if first else refs[0]
    blocks, refs = refs[:4] if first else refs[1:5], refs[4:] if first else refs[5:]
    source, g_ref, out, own_new, send, vector, whole = refs
    x = s_ref[1]
    total = summed(own, (got1, got2, got3))
    if not first:
        total = solved[...].astype(F32) + total
    out[...] = total.astype(BF)
    unpack(out, vector)
    residue = (source[...].astype(F32) - blocks_product(x, blocks, vector)).astype(BF)
    put_partial(g_ref, residue, own_new, send, whole)


def last_kernel(s_ref, own, got1, got2, got3, solved, out):
    out[...] = (solved[...].astype(F32) + summed(own, (got1, got2, got3))).astype(BF)


def diagonal_rows_kernel(s_ref, block0, block1, block2, block3, rows_out):
    x = s_ref[1]
    rows = at(x, 64)
    for shift, block in enumerate((block0, block1, block2, block3)):
        cols = at(mod4(x - shift), 256)
        rows_out[0, :, cols] = block[rows, pl.ds(0, 256)]
        rows_out[1, :, cols] = block[rows, pl.ds(256, 256)]


def coupling_rows_kernel(s_ref, pair0, pair1, pair2, pair3, lower_out, upper_out):
    x = s_ref[1]
    rows = at(x, 64)
    for shift, pair in enumerate((pair0, pair1, pair2, pair3)):
        cols = at(mod4(x - shift), 256)
        lower_out[0, :, cols] = pair[rows, pl.ds(0, 256)]
        lower_out[1, :, cols] = pair[rows, pl.ds(256, 256)]
        upper_out[0, :, cols] = pair[rows, pl.ds(512, 256)]
        upper_out[1, :, cols] = pair[rows, pl.ds(768, 256)]


def unpack(solved, vector):
    low, high = halves(solved[...].astype(F32))
    vector[pl.ds(0, 512), :] = low.astype(BF)
    vector[pl.ds(512, 512), :] = high.astype(BF)


def blocks_product(x, blocks, vector):
    real_rows = imag_rows = None
    for shift, block in enumerate(blocks):
        real, imag = block_product(block, vector[at(mod4(x - shift), 256), :])
        real_rows = real if real_rows is None else real_rows + real
        imag_rows = imag if imag_rows is None else imag_rows + imag
    return combine_small(real_rows, imag_rows)


def couple_kernel(s_ref, pair0, pair1, pair2, pair3, source, solved, below, above,
                  out0, out1, out2, out3, held, vector):
    y, x = s_ref[0], s_ref[1]
    pairs = (pair0, pair1, pair2, pair3)
    unpack(below, vector)
    combined = source[...].astype(F32)
    combined = combined - blocks_product(x, [p.at[:, pl.ds(0, 512)] for p in pairs], vector)
    unpack(above, vector)
    combined = combined - blocks_product(x, [p.at[:, pl.ds(512, 512)] for p in pairs], vector)
    rows = pl.ds(pl.multiple_of(lax.rem(y, 2) * 256, 256), 256)
    moved = pltpu.roll(solved[rows, :].astype(F32), jnp.where(y < 2, 64, 0), 1)
    held[...] = jnp.where(lanes_of(256) < 64, combined, moved)
    for shift, out in enumerate((out0, out1, out2, out3)):
        out[...] = held[at(mod4(x + shift), 64), :]


def spread_kernel(s_ref, piece0, piece1, piece2, piece3, combined, solved):
    x = s_ref[1]
    lane = lanes_of(64)
    totals = [jnp.zeros((64, 128), F32) for _ in range(4)]
    for shift, piece in enumerate((piece0, piece1, piece2, piece3)):
        chunk = mod4(x - shift)
        value = piece[...]
        on = (lane >= chunk * 32) & (lane < chunk * 32 + 32)
        for place in range(4):
            turned = pltpu.roll(value, mod4(chunk - place) * 32, 1)
            totals[place] = jnp.where(on, turned, totals[place])
    combined[0] = totals[0]
    combined[1] = totals[1]
    solved[0] = totals[2]
    solved[1] = totals[3]


def moved_x(block, by):
    pairs = [(y * 4 + x, y * 4 + (x + by) % 4) for y in range(4) for x in range(4)]
    return lax.ppermute(block, "row", pairs)


def moved_y(block, by):
    pairs = [(y * 4 + x, ((y + by) % 4) * 4 + x) for y in range(4) for x in range(4)]
    return lax.ppermute(block, "row", pairs)


def gathered_y(block):
    return (block, moved_y(block, 3), moved_y(block, 2), moved_y(block, 1))


def split_kernel(s_ref, block, other, low, high):
    low[...] = block[pl.ds(0, 128), :]
    high[...] = other[pl.ds(128, 128), :]


def ring_gathered_y(scalars, block, beside):
    above, below, *beside = lax.optimization_barrier(
        (moved_y(block, 3), moved_y(block, 1), *beside)
    )
    half = shape((128, block.shape[1]))
    low, high = call(split_kernel, [half, half], 0, scalars, below, above)
    return (block, above, below, moved_y(low, 1), moved_y(high, 3)), beside


def gathered_x(block):
    groups = [[y * 4 + x for x in range(4)] for y in range(4)]
    return lax.all_gather(block, "row", axis_index_groups=groups)


def along_cuts(block, by):
    count = lax.axis_size("cuts")
    pairs = [(i, i + by) for i in range(count) if 0 <= i + by < count]
    return lax.ppermute(block, "cuts", pairs)


def body(diagonal_blocks, diagonal_inverses, lower_blocks, upper_blocks, injection, orbitals):
    cut = lax.axis_index("cuts")
    place = lax.axis_index("row")
    zero = jnp.zeros((1,), jnp.int32)
    window = lax.dynamic_slice_in_dim(jnp.concatenate([zero, orbitals, zero]), 2 * cut, 4)
    scalars = jnp.concatenate([jnp.stack([place // 4, place % 4]).astype(jnp.int32), window])
    turns = (1, 2, 3)
    after = lax.optimization_barrier
    wide_flops = 2 * 512 * 1024 * 512
    solve_flops = 2 * 2048 * 256 * 128

    *pieces, a_even, c_even, g_pieces, g_odd = call(
        prepare_kernel,
        [shape((64, 1664))] * 4 + [shape((2, 64, 1024))] * 2 + [shape((4, 2, 64, 256))]
        + [shape((2, 64, 1024))],
        0,
        scalars, diagonal_blocks, diagonal_inverses, lower_blocks, upper_blocks, injection,
        hbm=5,
        scratch=[pltpu.VMEM((2, 64, 1024), BF)] * 3
        + [pltpu.VMEM((2, 2, 64, 128), BF)]
        + [pltpu.VMEM((2, 64, 1024), BF)] * 3
        + [pltpu.SemaphoreType.DMA((11,))],
    )
    pieces = [pieces[0]] + [moved_x(pieces[by], by) for by in turns]
    g_rows = gathered_x(g_odd)
    a_next = along_cuts(a_even, -1)
    groups = [[y * 4 + x for y in range(4)] for x in range(4)]
    g_columns = lax.all_to_all(
        g_pieces, "row", 0, 0, axis_index_groups=groups, tiled=True
    )
    a_next, g_columns, *pieces = after((a_next, g_columns, *pieces))
    panel, diagonal, couplings = call(
        assemble_kernel,
        [shape((256, 1152)), shape((256, 512)), shape((2, 2, 64, 1024))],
        0, scalars, *pieces, c_even, a_next,
    )
    g_columns = gathered_x(g_columns)
    near = (g_rows, moved_x(couplings, 1), moved_x(couplings, 3))
    panels, near = ring_gathered_y(scalars, panel, near)
    g_rows = near[0]
    ca_blocks = [couplings, near[1], moved_x(couplings, 2), near[2]]
    first, second = call(
        odd_kernel, [shape((256, 640)), shape((304, 512))], wide_flops,
        scalars, g_rows, *panels,
        scratch=[pltpu.VMEM((512, 1024), BF), pltpu.VMEM((256, 1152), BF)],
    )
    firsts = gathered_y(first)
    second, g_columns, *ca_blocks = after((second, g_columns, *ca_blocks))
    seconds = gathered_y(second)
    ship, upper_new, source_part, a_rows, c_rows = call(
        even_kernel,
        [shape((288, 512)), shape((256, 512)), shape((256, 128), F32),
         shape((512, 1024)),
         shape((512, 1024))],
        2 * wide_flops,
        scalars, *ca_blocks, *firsts, panel,
    )
    shipped = along_cuts(ship, 1)
    diagonal_new, ship_lower = call(
        diagonal_kernel, [shape((256, 512))] * 2, 2 * wide_flops,
        scalars, c_rows, a_rows, *seconds, diagonal, shipped,
    )
    diagonals = [diagonal_new] + [moved_x(diagonal_new, by) for by in turns]
    packed_shapes = [shape((512, 128), F32), shape((512, 128))]
    whole = pltpu.VMEM((1024, 128), F32)
    vector = pltpu.VMEM((1024, 128), BF)
    source, own, send = call(
        source_kernel, [shape((256, 128))] + packed_shapes, solve_flops,
        scalars, g_columns, source_part, shipped, scratch=[whole],
    )
    got = gathered_y(send)[1:]
    lower_new = along_cuts(ship_lower, 1)
    (pair,) = call(pair_kernel, [shape((256, 1024))], 0, scalars, lower_new, upper_new)
    pairs = [pair] + [moved_x(pair, by) for by in turns]
    solved = ()
    for turn in range(REFINE):
        *solved, own, send = call(
            functools.partial(turn_kernel, first=turn == 0),
            [shape((512, 128))] + packed_shapes, 2 * solve_flops,
            scalars, own, *got, *solved, *diagonals, source, g_columns,
            scratch=[vector, whole],
        )
        got = gathered_y(send)[1:]
    (solved,) = call(
        last_kernel, [shape((512, 128))], 0,
        scalars, own, *got, *solved,
    )
    below, above = along_cuts(solved, 1), along_cuts(solved, -1)
    (diagonal_rows,) = call(
        diagonal_rows_kernel, [shape((2, 64, 1024))], 0, scalars, *diagonals
    )
    lower_rows, upper_rows = call(
        coupling_rows_kernel, [shape((2, 64, 1024))] * 2, 0, scalars, *pairs
    )
    below, diagonal_rows, lower_rows, upper_rows = after(
        (below, diagonal_rows, lower_rows, upper_rows)
    )
    ends = call(
        couple_kernel, [shape((64, 128), F32)] * 4, solve_flops // 2,
        scalars, *pairs, source, solved, below, above,
        scratch=[pltpu.VMEM((256, 128), F32), vector],
    )
    ends = [ends[0]] + [moved_x(ends[by], by) for by in turns]
    combined, solved_rows = call(
        spread_kernel, [shape((2, 64, 128), F32)] * 2, 0, scalars, *ends
    )
    return (
        diagonal_rows[None],
        lower_rows[None],
        upper_rows[None],
        combined[None],
        solved_rows[None],
    )


def solution(mesh):
    split = P("cuts", None, "row", None)
    return jax.shard_map(
        body,
        mesh=mesh,
        in_specs=(split, split, split, split, split, P()),
        out_specs=(split,) * 5,
        check_vma=False,
    )
```

```python
import functools

import jax
import jax.numpy as jnp
from jax import lax
from jax.experimental import pallas as pl
from jax.experimental.pallas import tpu as pltpu
from jax.sharding import PartitionSpec as P

REFINE = 2
BF = jnp.bfloat16
F32 = jnp.float32
VMEM = pl.BlockSpec(memory_space=pltpu.VMEM)
MIB = 12
SMEM = pl.BlockSpec(memory_space=pltpu.SMEM)


def call(kernel, out_shapes, flops, *args, scratch=(), hbm=0, mib=MIB, hbm_out=False):
    moved = sum(a.size * a.dtype.itemsize for a in args) + sum(
        s.size * s.dtype.itemsize for s in out_shapes
    )
    anywhere = pl.BlockSpec(memory_space=pltpu.HBM)
    args = [
        pltpu.with_memory_space_constraint(a, pltpu.HBM) if 0 < index <= hbm else a
        for index, a in enumerate(args)
    ]
    return pl.pallas_call(
        kernel,
        out_shape=tuple(out_shapes),
        in_specs=[SMEM] + [anywhere] * hbm + [VMEM] * (len(args) - 1 - hbm),
        out_specs=tuple([anywhere if hbm_out else VMEM] * len(out_shapes)),
        scratch_shapes=list(scratch),
        compiler_params=pltpu.CompilerParams(vmem_limit_bytes=mib * 1024 * 1024),
        cost_estimate=pl.CostEstimate(flops=0, bytes_accessed=moved, transcendentals=0),
    )(*args)


def shape(dims, dtype=BF):
    return jax.ShapeDtypeStruct(dims, dtype)


def mod4(v):
    return lax.rem(v + 8, 4)


def at(chunk, size):
    return pl.ds(pl.multiple_of(chunk * size, size), size)


def lanes_of(rows):
    return lax.broadcasted_iota(jnp.int32, (rows, 128), 1)


def combine_small(real_rows, imag_rows):
    lane = lanes_of(real_rows.shape[0])
    turned = jnp.where(lane < 32, -pltpu.roll(imag_rows, 96, 1), pltpu.roll(imag_rows, 32, 1))
    return jnp.where(lane < 64, real_rows + turned, 0.0)


def packed(block):
    half = block.shape[0] // 2
    return jnp.where(lanes_of(half) < 64, block[:half], pltpu.roll(block[half:], 64, 1))


def halves(block):
    return block, pltpu.roll(block, 64, 1)


def masked(block, first_row, rows_on, chunk, cols_on):
    row = first_row + lax.broadcasted_iota(jnp.int32, (64, 256), 0)
    col = chunk * 256 + lax.broadcasted_iota(jnp.int32, (64, 256), 1)
    return jnp.where((row < rows_on) & (col < cols_on), block.astype(F32), 0.0).astype(BF)


def prepare_kernel(s_ref, d_hbm, g_hbm, a_hbm, c_hbm, b_hbm, piece0, piece1, piece2, piece3,
                   a_even, c_even, g_pieces, g_odd,
                   d_ref, a_ref, c_ref, b_ref, a_first, c_first, g_first, sems):
    y, x = s_ref[0], s_ref[1]
    first_row = (y * 4 + x) * 64
    before, own, odd, after = s_ref[2], s_ref[3], s_ref[4], s_ref[5]
    copies = [
        pltpu.make_async_copy(source, target, sems.at[index])
        for index, (source, target) in enumerate(
            (
                (c_hbm.at[1, 0], c_ref.at[0]),
                (c_hbm.at[1, 1], c_ref.at[1]),
                (b_hbm, b_ref),
                (a_hbm.at[1, 0], a_ref.at[0]),
                (a_hbm.at[1, 1], a_ref.at[1]),
                (d_hbm.at[0, 0], d_ref.at[0]),
                (d_hbm.at[0, 1], d_ref.at[1]),
                (a_hbm.at[0], a_first),
                (c_hbm.at[0], c_first),
                (g_hbm.at[0], g_first),
                (g_hbm.at[1], g_odd),
            )
        )
    ]
    for copy in copies:
        copy.start()
    pieces = (piece0, piece1, piece2, piece3)
    row_b = first_row + lax.broadcasted_iota(jnp.int32, (64, 128), 0)
    lane = lanes_of(64)
    copies[0].wait()
    copies[1].wait()
    for shift, piece in enumerate(pieces):
        chunk = mod4(x + shift)
        for part in range(2):
            piece[:, pl.ds(part * 256, 256)] = masked(
                c_ref[part, :, at(chunk, 256)], first_row, odd, chunk, after
            )
    copies[2].wait()
    blocks = [
        jnp.where(row_b < rows_on, b_ref[which, part].astype(F32), 0.0)
        for which, part, rows_on in ((1, 0, odd), (1, 1, odd), (0, 0, own), (0, 1, own))
    ]
    for shift, piece in enumerate(pieces):
        chunk = mod4(x + shift)
        tile = jnp.zeros((64, 128), F32)
        for place, block in enumerate(blocks):
            turned = pltpu.roll(block, mod4(place - chunk) * 32, 1)
            tile = jnp.where((lane >= place * 32) & (lane < place * 32 + 32), turned, tile)
        piece[:, pl.ds(512, 128)] = tile.astype(BF)
    copies[3].wait()
    copies[4].wait()
    for shift, piece in enumerate(pieces):
        chunk = mod4(x + shift)
        for part in range(2):
            piece[:, pl.ds(640 + part * 256, 256)] = masked(
                a_ref[part, :, at(chunk, 256)], first_row, odd, chunk, own
            )
    copies[5].wait()
    copies[6].wait()
    for shift, piece in enumerate(pieces):
        chunk = mod4(x + shift)
        for part in range(2):
            piece[:, pl.ds(1152 + part * 256, 256)] = d_ref[part, :, at(chunk, 256)]
    copies[7].wait()
    copies[8].wait()
    for chunk in range(4):
        cols = pl.ds(chunk * 256, 256)
        for part in range(2):
            a_even[part, :, cols] = masked(a_first[part, :, cols], first_row, own, chunk, before)
            c_even[part, :, cols] = masked(c_first[part, :, cols], first_row, own, chunk, odd)
    copies[9].wait()
    for chunk in range(4):
        for part in range(2):
            g_pieces[chunk, part] = g_first[part, :, pl.ds(chunk * 256, 256)]
    copies[10].wait()


def assemble_kernel(s_ref, piece0, piece1, piece2, piece3, c_even, a_next,
                    panel, diagonal, couplings):
    y, x = s_ref[0], s_ref[1]
    for shift, piece in enumerate((piece0, piece1, piece2, piece3)):
        rows = at(mod4(x - shift), 64)
        panel[rows, :] = piece[:, pl.ds(0, 1152)]
        diagonal[rows, :] = piece[:, pl.ds(1152, 512)]
    couplings[0] = c_even[...]
    couplings[1] = a_next[...]


def stack_rows(x, blocks, held):
    for shift, block in enumerate(blocks):
        held[at(mod4(x - shift), 128), :] = block[...].reshape(128, 1024)


def wide_dot(y, held, panels, start, width):
    total = None
    for place, panel in enumerate(panels):
        term = jnp.dot(
            held[:, at(mod4(y + place), 256)],
            panel[pl.ds(0, 256), pl.ds(start, width)],
            preferred_element_type=F32,
        )
        total = term if total is None else total + term
    parts = total.reshape(4, 2, 64, width)
    return parts[:, 0].reshape(256, width), parts[:, 1].reshape(256, width)


def wide_product(y, held, panels, start=0):
    real_rows, imag_rows = wide_dot(y, held, panels, start, 512)
    real = real_rows[:, :256] - imag_rows[:, 256:]
    imag = real_rows[:, 256:] + imag_rows[:, :256]
    return real, imag


def small_product(y, held, panels):
    return combine_small(*wide_dot(y, held, panels, 512, 128))


def put_pair(out, real, imag):
    out[pl.ds(0, 256), pl.ds(0, 256)] = real.astype(out.dtype)
    out[pl.ds(0, 256), pl.ds(256, 256)] = imag.astype(out.dtype)


def odd_kernel(s_ref, g_ref, panel0, panel1, panel3, low, high, out, out_second, held, panel2):
    y, x = s_ref[0], s_ref[1]
    panel2[pl.ds(0, 128), :] = low[...]
    panel2[pl.ds(128, 128), :] = high[...]
    panels = (panel0, panel1, panel2, panel3)
    held[...] = g_ref[...].reshape(512, 1024)
    put_pair(out, *wide_product(y, held, panels))
    out[:, pl.ds(512, 128)] = small_product(y, held, panels).astype(BF)
    put_pair(out_second, *wide_product(y, held, panels, 640))
    out_second[pl.ds(256, 16), :] = jnp.zeros((16, 512), BF)


def even_kernel(s_ref, ca0, ca1, ca2, ca3, panel0, panel1, panel2, panel3, source,
                ship, ship_source, upper_new, source_part, a_rows, c_rows):
    y, x = s_ref[0], s_ref[1]
    panels = (panel0, panel1, panel2, panel3)
    stack_rows(x, [block.at[1] for block in (ca0, ca1, ca2, ca3)], a_rows)
    stack_rows(x, [block.at[0] for block in (ca0, ca1, ca2, ca3)], c_rows)
    ship_source[...] = small_product(y, a_rows, panels).astype(BF)
    put_pair(ship, *wide_product(y, a_rows, panels))
    own = pltpu.roll(source[:, pl.ds(512, 128)].astype(F32), 64, 1)
    own = jnp.where(lanes_of(256) < 64, own, 0.0)
    source_part[...] = own - small_product(y, c_rows, panels)
    real, imag = wide_product(y, c_rows, panels)
    put_pair(upper_new, -real, -imag)


def diagonal_kernel(s_ref, c_rows, a_rows, panel0, panel1, panel2, panel3, diagonal, shipped,
                    out, lower):
    real, imag = wide_product(s_ref[0], c_rows, (panel0, panel1, panel2, panel3))
    real = diagonal[:, pl.ds(0, 256)].astype(F32) - real - shipped[pl.ds(0, 256), pl.ds(0, 256)].astype(F32)
    imag = diagonal[:, pl.ds(256, 256)].astype(F32) - imag - shipped[pl.ds(0, 256), pl.ds(256, 256)].astype(F32)
    put_pair(out, real, imag)
    real, imag = wide_product(s_ref[0], a_rows, (panel0, panel1, panel2, panel3))
    put_pair(lower, -real, -imag)


def pair_kernel(s_ref, lower, upper, out):
    out[:, pl.ds(0, 512)] = lower[...]
    out[:, pl.ds(512, 512)] = upper[...]


def block_product(block, right):
    real = jnp.dot(block[:, pl.ds(0, 256)], right, preferred_element_type=F32)
    imag = jnp.dot(block[:, pl.ds(256, 256)], right, preferred_element_type=F32)
    return real, imag


def put_partial(g_ref, right, own, send, whole):
    for index in range(4):
        total = jnp.dot(g_ref[index].reshape(512, 256), right, preferred_element_type=F32)
        parts = total.reshape(4, 2, 64, 128)
        value = combine_small(parts[:, 0].reshape(256, 128), parts[:, 1].reshape(256, 128))
        value = value.reshape(4, 64, 128)
        for group in range(4):
            whole[pl.ds(group * 256 + index * 64, 64), :] = value[group]
    total = packed(whole[...])
    own[...] = total
    send[...] = total.astype(BF)


def source_kernel(s_ref, g_ref, source_part, shipped, source_new, own, send, whole):
    source = (source_part[...] - shipped[...].astype(F32)).astype(BF)
    source_new[...] = source
    put_partial(g_ref, source, own, send, whole)


def summed(own, got):
    total = own[...]
    for other in got:
        total = total + other[...].astype(F32)
    return total


def turn_kernel(s_ref, own, got1, got2, got3, *refs, first):
    solved = None if first else refs[0]
    blocks, refs = refs[:4] if first else refs[1:5], refs[4:] if first else refs[5:]
    source, g_ref, out, own_new, send, vector, whole = refs
    x = s_ref[1]
    total = summed(own, (got1, got2, got3))
    if not first:
        total = solved[...].astype(F32) + total
    out[...] = total.astype(BF)
    unpack(out, vector)
    residue = (source[...].astype(F32) - blocks_product(x, blocks, vector)).astype(BF)
    put_partial(g_ref, residue, own_new, send, whole)


def last_kernel(s_ref, own, got1, got2, got3, solved, out):
    out[...] = (solved[...].astype(F32) + summed(own, (got1, got2, got3))).astype(BF)


def diagonal_rows_kernel(s_ref, block0, block1, block2, block3, rows_out):
    x = s_ref[1]
    rows = at(x, 64)
    for shift, block in enumerate((block0, block1, block2, block3)):
        cols = at(mod4(x - shift), 256)
        rows_out[0, :, cols] = block[rows, pl.ds(0, 256)]
        rows_out[1, :, cols] = block[rows, pl.ds(256, 256)]


def coupling_rows_kernel(s_ref, pair0, pair1, pair2, pair3, lower_out, upper_out):
    x = s_ref[1]
    rows = at(x, 64)
    for shift, pair in enumerate((pair0, pair1, pair2, pair3)):
        cols = at(mod4(x - shift), 256)
        lower_out[0, :, cols] = pair[rows, pl.ds(0, 256)]
        lower_out[1, :, cols] = pair[rows, pl.ds(256, 256)]
        upper_out[0, :, cols] = pair[rows, pl.ds(512, 256)]
        upper_out[1, :, cols] = pair[rows, pl.ds(768, 256)]


def unpack(solved, vector):
    low, high = halves(solved[...].astype(F32))
    vector[pl.ds(0, 512), :] = low.astype(BF)
    vector[pl.ds(512, 512), :] = high.astype(BF)


def blocks_product(x, blocks, vector):
    real_rows = imag_rows = None
    for shift, block in enumerate(blocks):
        real, imag = block_product(block, vector[at(mod4(x - shift), 256), :])
        real_rows = real if real_rows is None else real_rows + real
        imag_rows = imag if imag_rows is None else imag_rows + imag
    return combine_small(real_rows, imag_rows)


def couple_kernel(s_ref, pair0, pair1, pair2, pair3, source, solved, below, above,
                  out0, out1, out2, out3, held, vector):
    y, x = s_ref[0], s_ref[1]
    pairs = (pair0, pair1, pair2, pair3)
    unpack(below, vector)
    combined = source[...].astype(F32)
    combined = combined - blocks_product(x, [p.at[:, pl.ds(0, 512)] for p in pairs], vector)
    unpack(above, vector)
    combined = combined - blocks_product(x, [p.at[:, pl.ds(512, 512)] for p in pairs], vector)
    rows = pl.ds(pl.multiple_of(lax.rem(y, 2) * 256, 256), 256)
    moved = pltpu.roll(solved[rows, :].astype(F32), jnp.where(y < 2, 64, 0), 1)
    held[...] = jnp.where(lanes_of(256) < 64, combined, moved)
    for shift, out in enumerate((out0, out1, out2, out3)):
        out[...] = held[at(mod4(x + shift), 64), :]


def spread_kernel(s_ref, piece0, piece1, piece2, piece3, combined, solved):
    x = s_ref[1]
    lane = lanes_of(64)
    totals = [jnp.zeros((64, 128), F32) for _ in range(4)]
    for shift, piece in enumerate((piece0, piece1, piece2, piece3)):
        chunk = mod4(x - shift)
        value = piece[...]
        on = (lane >= chunk * 32) & (lane < chunk * 32 + 32)
        for place in range(4):
            turned = pltpu.roll(value, mod4(chunk - place) * 32, 1)
            totals[place] = jnp.where(on, turned, totals[place])
    combined[0] = totals[0]
    combined[1] = totals[1]
    solved[0] = totals[2]
    solved[1] = totals[3]


def moved_x(block, by):
    pairs = [(y * 4 + x, y * 4 + (x + by) % 4) for y in range(4) for x in range(4)]
    return lax.ppermute(block, "row", pairs)


def moved_y(block, by):
    pairs = [(y * 4 + x, ((y + by) % 4) * 4 + x) for y in range(4) for x in range(4)]
    return lax.ppermute(block, "row", pairs)


def gathered_y(block):
    return (block, moved_y(block, 3), moved_y(block, 2), moved_y(block, 1))


def split_kernel(s_ref, block, other, low, high):
    low[...] = block[pl.ds(0, 128), :]
    high[...] = other[pl.ds(128, 128), :]


def ring_gathered_y(scalars, block, beside):
    above, below, *beside = lax.optimization_barrier(
        (moved_y(block, 3), moved_y(block, 1), *beside)
    )
    half = shape((128, block.shape[1]))
    low, high = call(split_kernel, [half, half], 0, scalars, below, above)
    return (block, above, below, moved_y(low, 1), moved_y(high, 3)), beside


def gathered_x(block):
    groups = [[y * 4 + x for x in range(4)] for y in range(4)]
    return lax.all_gather(block, "row", axis_index_groups=groups)


def along_cuts(block, by):
    count = lax.axis_size("cuts")
    pairs = [(i, i + by) for i in range(count) if 0 <= i + by < count]
    return lax.ppermute(block, "cuts", pairs)


def body(diagonal_blocks, diagonal_inverses, lower_blocks, upper_blocks, injection, orbitals):
    cut = lax.axis_index("cuts")
    place = lax.axis_index("row")
    zero = jnp.zeros((1,), jnp.int32)
    window = lax.dynamic_slice_in_dim(jnp.concatenate([zero, orbitals, zero]), 2 * cut, 4)
    scalars = jnp.concatenate([jnp.stack([place // 4, place % 4]).astype(jnp.int32), window])
    turns = (1, 2, 3)
    after = lax.optimization_barrier
    wide_flops = 2 * 512 * 1024 * 512
    solve_flops = 2 * 2048 * 256 * 128

    *pieces, a_even, c_even, g_pieces, g_odd = call(
        prepare_kernel,
        [shape((64, 1664))] * 4 + [shape((2, 64, 1024))] * 2 + [shape((4, 2, 64, 256))]
        + [shape((2, 64, 1024))],
        0,
        scalars, diagonal_blocks, diagonal_inverses, lower_blocks, upper_blocks, injection,
        hbm=5,
        scratch=[pltpu.VMEM((2, 64, 1024), BF)] * 3
        + [pltpu.VMEM((2, 2, 64, 128), BF)]
        + [pltpu.VMEM((2, 64, 1024), BF)] * 3
        + [pltpu.SemaphoreType.DMA((11,))],
    )
    pieces = [pieces[0]] + [moved_x(pieces[by], by) for by in turns]
    g_rows = gathered_x(g_odd)
    a_next = along_cuts(a_even, -1)
    groups = [[y * 4 + x for y in range(4)] for x in range(4)]
    g_columns = lax.all_to_all(
        g_pieces, "row", 0, 0, axis_index_groups=groups, tiled=True
    )
    a_next, g_columns, *pieces = after((a_next, g_columns, *pieces))
    panel, diagonal, couplings = call(
        assemble_kernel,
        [shape((256, 1152)), shape((256, 512)), shape((2, 2, 64, 1024))],
        0, scalars, *pieces, c_even, a_next,
    )
    g_columns = gathered_x(g_columns)
    panels, (g_rows,) = ring_gathered_y(scalars, panel, (g_rows,))
    ca_blocks = [couplings] + [moved_x(couplings, by) for by in turns]
    first, second = call(
        odd_kernel, [shape((256, 640)), shape((272, 512))], wide_flops,
        scalars, g_rows, *panels,
        scratch=[pltpu.VMEM((512, 1024), BF), pltpu.VMEM((256, 1152), BF)],
    )
    firsts = gathered_y(first)
    second, g_columns, *ca_blocks = after((second, g_columns, *ca_blocks))
    seconds = gathered_y(second)
    ship, ship_source, upper_new, source_part, a_rows, c_rows = call(
        even_kernel,
        [shape((256, 512)), shape((256, 128)), shape((256, 512)), shape((256, 128), F32),
         shape((512, 1024)),
         shape((512, 1024))],
        2 * wide_flops,
        scalars, *ca_blocks, *firsts, panel,
    )
    shipped = along_cuts(ship, 1)
    shipped_source = along_cuts(ship_source, 1)
    diagonal_new, ship_lower = call(
        diagonal_kernel, [shape((256, 512))] * 2, 2 * wide_flops,
        scalars, c_rows, a_rows, *seconds, diagonal, shipped,
    )
    diagonals = [diagonal_new] + [moved_x(diagonal_new, by) for by in turns]
    packed_shapes = [shape((512, 128), F32), shape((512, 128))]
    whole = pltpu.VMEM((1024, 128), F32)
    vector = pltpu.VMEM((1024, 128), BF)
    source, own, send = call(
        source_kernel, [shape((256, 128))] + packed_shapes, solve_flops,
        scalars, g_columns, source_part, shipped_source, scratch=[whole],
    )
    got = gathered_y(send)[1:]
    lower_new = along_cuts(ship_lower, 1)
    (pair,) = call(pair_kernel, [shape((256, 1024))], 0, scalars, lower_new, upper_new)
    pairs = [pair] + [moved_x(pair, by) for by in turns]
    solved = ()
    for turn in range(REFINE):
        *solved, own, send = call(
            functools.partial(turn_kernel, first=turn == 0),
            [shape((512, 128))] + packed_shapes, 2 * solve_flops,
            scalars, own, *got, *solved, *diagonals, source, g_columns,
            scratch=[vector, whole],
        )
        got = gathered_y(send)[1:]
    (solved,) = call(
        last_kernel, [shape((512, 128))], 0,
        scalars, own, *got, *solved,
    )
    below, above = along_cuts(solved, 1), along_cuts(solved, -1)
    (diagonal_rows,) = call(
        diagonal_rows_kernel, [shape((2, 64, 1024))], 0, scalars, *diagonals
    )
    lower_rows, upper_rows = call(
        coupling_rows_kernel, [shape((2, 64, 1024))] * 2, 0, scalars, *pairs
    )
    below, diagonal_rows, lower_rows, upper_rows = after(
        (below, diagonal_rows, lower_rows, upper_rows)
    )
    ends = call(
        couple_kernel, [shape((64, 128), F32)] * 4, solve_flops // 2,
        scalars, *pairs, source, solved, below, above,
        scratch=[pltpu.VMEM((256, 128), F32), vector],
    )
    ends = [ends[0]] + [moved_x(ends[by], by) for by in turns]
    combined, solved_rows = call(
        spread_kernel, [shape((2, 64, 128), F32)] * 2, 0, scalars, *ends
    )
    return (
        diagonal_rows[None],
        lower_rows[None],
        upper_rows[None],
        combined[None],
        solved_rows[None],
    )


def solution(mesh):
    split = P("cuts", None, "row", None)
    return jax.shard_map(
        body,
        mesh=mesh,
        in_specs=(split, split, split, split, split, P()),
        out_specs=(split,) * 5,
        check_vma=False,
    )
```

```python
import functools

import jax
import jax.numpy as jnp
from jax import lax
from jax.experimental import pallas as pl
from jax.experimental.pallas import tpu as pltpu
from jax.sharding import PartitionSpec as P

REFINE = 2
BF = jnp.bfloat16
F32 = jnp.float32
VMEM = pl.BlockSpec(memory_space=pltpu.VMEM)
MIB = 12
SMEM = pl.BlockSpec(memory_space=pltpu.SMEM)


def call(kernel, out_shapes, flops, *args, scratch=(), hbm=0, mib=MIB, hbm_out=False, pinned=()):
    moved = sum(a.size * a.dtype.itemsize for a in args) + sum(
        s.size * s.dtype.itemsize for s in out_shapes
    )
    anywhere = pl.BlockSpec(memory_space=pltpu.HBM)
    args = [
        pltpu.with_memory_space_constraint(a, pltpu.HBM) if 0 < index <= hbm
        else pltpu.with_memory_space_constraint(a, pltpu.VMEM) if index in pinned
        else a
        for index, a in enumerate(args)
    ]
    return pl.pallas_call(
        kernel,
        out_shape=tuple(out_shapes),
        in_specs=[SMEM] + [anywhere] * hbm + [VMEM] * (len(args) - 1 - hbm),
        out_specs=tuple([anywhere if hbm_out else VMEM] * len(out_shapes)),
        scratch_shapes=list(scratch),
        compiler_params=pltpu.CompilerParams(vmem_limit_bytes=mib * 1024 * 1024),
        cost_estimate=pl.CostEstimate(flops=0, bytes_accessed=moved, transcendentals=0),
    )(*args)


def shape(dims, dtype=BF):
    return jax.ShapeDtypeStruct(dims, dtype)


def mod4(v):
    return lax.rem(v + 8, 4)


def at(chunk, size):
    return pl.ds(pl.multiple_of(chunk * size, size), size)


def lanes_of(rows):
    return lax.broadcasted_iota(jnp.int32, (rows, 128), 1)


def combine_small(real_rows, imag_rows):
    lane = lanes_of(real_rows.shape[0])
    turned = jnp.where(lane < 32, -pltpu.roll(imag_rows, 96, 1), pltpu.roll(imag_rows, 32, 1))
    return jnp.where(lane < 64, real_rows + turned, 0.0)


def packed(block):
    half = block.shape[0] // 2
    return jnp.where(lanes_of(half) < 64, block[:half], pltpu.roll(block[half:], 64, 1))


def halves(block):
    return block, pltpu.roll(block, 64, 1)


def masked(block, first_row, rows_on, chunk, cols_on):
    row = first_row + lax.broadcasted_iota(jnp.int32, (64, 256), 0)
    col = chunk * 256 + lax.broadcasted_iota(jnp.int32, (64, 256), 1)
    return jnp.where((row < rows_on) & (col < cols_on), block.astype(F32), 0.0).astype(BF)


def prepare_kernel(s_ref, d_hbm, g_hbm, a_hbm, c_hbm, b_hbm, piece0, piece1, piece2, piece3,
                   a_even, c_even, g_pieces, g_odd,
                   d_ref, a_ref, c_ref, b_ref, a_first, c_first, g_first, sems):
    y, x = s_ref[0], s_ref[1]
    first_row = (y * 4 + x) * 64
    before, own, odd, after = s_ref[2], s_ref[3], s_ref[4], s_ref[5]
    copies = [
        pltpu.make_async_copy(source, target, sems.at[index])
        for index, (source, target) in enumerate(
            (
                (c_hbm.at[1, 0], c_ref.at[0]),
                (c_hbm.at[1, 1], c_ref.at[1]),
                (b_hbm, b_ref),
                (a_hbm.at[1, 0], a_ref.at[0]),
                (a_hbm.at[1, 1], a_ref.at[1]),
                (d_hbm.at[0, 0], d_ref.at[0]),
                (d_hbm.at[0, 1], d_ref.at[1]),
                (a_hbm.at[0], a_first),
                (c_hbm.at[0], c_first),
                (g_hbm.at[0], g_first),
                (g_hbm.at[1], g_odd),
            )
        )
    ]
    for copy in copies:
        copy.start()
    pieces = (piece0, piece1, piece2, piece3)
    row_b = first_row + lax.broadcasted_iota(jnp.int32, (64, 128), 0)
    lane = lanes_of(64)
    copies[0].wait()
    copies[1].wait()
    for shift, piece in enumerate(pieces):
        chunk = mod4(x + shift)
        for part in range(2):
            piece[:, pl.ds(part * 256, 256)] = masked(
                c_ref[part, :, at(chunk, 256)], first_row, odd, chunk, after
            )
    copies[2].wait()
    blocks = [
        jnp.where(row_b < rows_on, b_ref[which, part].astype(F32), 0.0)
        for which, part, rows_on in ((1, 0, odd), (1, 1, odd), (0, 0, own), (0, 1, own))
    ]
    for shift, piece in enumerate(pieces):
        chunk = mod4(x + shift)
        tile = jnp.zeros((64, 128), F32)
        for place, block in enumerate(blocks):
            turned = pltpu.roll(block, mod4(place - chunk) * 32, 1)
            tile = jnp.where((lane >= place * 32) & (lane < place * 32 + 32), turned, tile)
        piece[:, pl.ds(512, 128)] = tile.astype(BF)
    copies[3].wait()
    copies[4].wait()
    for shift, piece in enumerate(pieces):
        chunk = mod4(x + shift)
        for part in range(2):
            piece[:, pl.ds(640 + part * 256, 256)] = masked(
                a_ref[part, :, at(chunk, 256)], first_row, odd, chunk, own
            )
    copies[5].wait()
    copies[6].wait()
    for shift, piece in enumerate(pieces):
        chunk = mod4(x + shift)
        for part in range(2):
            piece[:, pl.ds(1152 + part * 256, 256)] = d_ref[part, :, at(chunk, 256)]
    copies[7].wait()
    copies[8].wait()
    for chunk in range(4):
        cols = pl.ds(chunk * 256, 256)
        for part in range(2):
            a_even[part, :, cols] = masked(a_first[part, :, cols], first_row, own, chunk, before)
            c_even[part, :, cols] = masked(c_first[part, :, cols], first_row, own, chunk, odd)
    copies[9].wait()
    for chunk in range(4):
        for part in range(2):
            g_pieces[chunk, part] = g_first[part, :, pl.ds(chunk * 256, 256)]
    copies[10].wait()


def assemble_kernel(s_ref, piece0, piece1, piece2, piece3, c_even, a_next,
                    panel, diagonal, couplings):
    y, x = s_ref[0], s_ref[1]
    for shift, piece in enumerate((piece0, piece1, piece2, piece3)):
        rows = at(mod4(x - shift), 64)
        panel[rows, :] = piece[:, pl.ds(0, 1152)]
        diagonal[rows, :] = piece[:, pl.ds(1152, 512)]
    couplings[0] = c_even[...]
    couplings[1] = a_next[...]


def stack_rows(x, blocks, held):
    for shift, block in enumerate(blocks):
        held[at(mod4(x - shift), 128), :] = block[...].reshape(128, 1024)


def wide_dot(y, held, panels, start, width):
    total = None
    for place, panel in enumerate(panels):
        term = jnp.dot(
            held[:, at(mod4(y + place), 256)],
            panel[pl.ds(0, 256), pl.ds(start, width)],
            preferred_element_type=F32,
        )
        total = term if total is None else total + term
    parts = total.reshape(4, 2, 64, width)
    return parts[:, 0].reshape(256, width), parts[:, 1].reshape(256, width)


def wide_product(y, held, panels, start=0):
    real_rows, imag_rows = wide_dot(y, held, panels, start, 512)
    real = real_rows[:, :256] - imag_rows[:, 256:]
    imag = real_rows[:, 256:] + imag_rows[:, :256]
    return real, imag


def small_product(y, held, panels):
    return combine_small(*wide_dot(y, held, panels, 512, 128))


def put_pair(out, real, imag):
    out[pl.ds(0, 256), pl.ds(0, 256)] = real.astype(out.dtype)
    out[pl.ds(0, 256), pl.ds(256, 256)] = imag.astype(out.dtype)


def odd_kernel(s_ref, g_ref, panel0, panel1, panel3, low, high, out, out_second, held, panel2):
    y, x = s_ref[0], s_ref[1]
    panel2[pl.ds(0, 128), :] = low[...]
    panel2[pl.ds(128, 128), :] = high[...]
    panels = (panel0, panel1, panel2, panel3)
    held[...] = g_ref[...].reshape(512, 1024)
    put_pair(out, *wide_product(y, held, panels))
    out[:, pl.ds(512, 128)] = small_product(y, held, panels).astype(BF)
    put_pair(out_second, *wide_product(y, held, panels, 640))
    out_second[pl.ds(256, 48), :] = jnp.zeros((48, 512), BF)


def even_kernel(s_ref, ca0, ca1, ca2, ca3, panel0, panel1, panel2, panel3, source,
                ship, upper_new, source_part, a_rows, c_rows):
    y, x = s_ref[0], s_ref[1]
    panels = (panel0, panel1, panel2, panel3)
    stack_rows(x, [block.at[1] for block in (ca0, ca1, ca2, ca3)], a_rows)
    stack_rows(x, [block.at[0] for block in (ca0, ca1, ca2, ca3)], c_rows)
    value = small_product(y, a_rows, panels)
    lane = lanes_of(32)
    for index in range(4):
        low, high = value[index * 64 : index * 64 + 32], value[index * 64 + 32 : index * 64 + 64]
        tile = jnp.where(lane < 64, low, pltpu.roll(high, 64, 1))
        ship[pl.ds(256, 32), pl.ds(index * 128, 128)] = tile.astype(BF)
    put_pair(ship, *wide_product(y, a_rows, panels))
    own = pltpu.roll(source[:, pl.ds(512, 128)].astype(F32), 64, 1)
    own = jnp.where(lanes_of(256) < 64, own, 0.0)
    source_part[...] = own - small_product(y, c_rows, panels)
    real, imag = wide_product(y, c_rows, panels)
    put_pair(upper_new, -real, -imag)


def diagonal_kernel(s_ref, c_rows, a_rows, panel0, panel1, panel2, panel3, diagonal, shipped,
                    out, lower):
    real, imag = wide_product(s_ref[0], c_rows, (panel0, panel1, panel2, panel3))
    real = diagonal[:, pl.ds(0, 256)].astype(F32) - real - shipped[pl.ds(0, 256), pl.ds(0, 256)].astype(F32)
    imag = diagonal[:, pl.ds(256, 256)].astype(F32) - imag - shipped[pl.ds(0, 256), pl.ds(256, 256)].astype(F32)
    put_pair(out, real, imag)
    real, imag = wide_product(s_ref[0], a_rows, (panel0, panel1, panel2, panel3))
    put_pair(lower, -real, -imag)


def pair_kernel(s_ref, lower, upper, out):
    out[:, pl.ds(0, 512)] = lower[...]
    out[:, pl.ds(512, 512)] = upper[...]


def block_product(block, right):
    real = jnp.dot(block[:, pl.ds(0, 256)], right, preferred_element_type=F32)
    imag = jnp.dot(block[:, pl.ds(256, 256)], right, preferred_element_type=F32)
    return real, imag


def put_partial(g_ref, right, own, send, whole):
    for index in range(4):
        total = jnp.dot(g_ref[index].reshape(512, 256), right, preferred_element_type=F32)
        parts = total.reshape(4, 2, 64, 128)
        value = combine_small(parts[:, 0].reshape(256, 128), parts[:, 1].reshape(256, 128))
        value = value.reshape(4, 64, 128)
        for group in range(4):
            whole[pl.ds(group * 256 + index * 64, 64), :] = value[group]
    total = packed(whole[...])
    own[...] = total
    send[...] = total.astype(BF)


def source_kernel(s_ref, g_ref, source_part, shipped, source_new, own, send, whole):
    lane = lanes_of(32)
    for index in range(4):
        tile = shipped[pl.ds(256, 32), pl.ds(index * 128, 128)].astype(F32)
        for half, moved in enumerate(halves(tile)):
            rows = pl.ds(index * 64 + half * 32, 32)
            value = source_part[rows, :] - jnp.where(lane < 64, moved, 0.0)
            source_new[rows, :] = value.astype(BF)
    source = source_new[...]
    put_partial(g_ref, source, own, send, whole)


def summed(own, got):
    total = own[...]
    for other in got:
        total = total + other[...].astype(F32)
    return total


def turn_kernel(s_ref, own, got1, got2, got3, *refs, first):
    solved = None if first else refs[0]
    blocks, refs = refs[:4] if first else refs[1:5], refs[4:] if first else refs[5:]
    source, g_ref, out, own_new, send, vector, whole = refs
    x = s_ref[1]
    total = summed(own, (got1, got2, got3))
    if not first:
        total = solved[...].astype(F32) + total
    out[...] = total.astype(BF)
    unpack(out, vector)
    residue = (source[...].astype(F32) - blocks_product(x, blocks, vector)).astype(BF)
    put_partial(g_ref, residue, own_new, send, whole)


def last_kernel(s_ref, own, got1, got2, got3, solved, out):
    out[...] = (solved[...].astype(F32) + summed(own, (got1, got2, got3))).astype(BF)


def diagonal_rows_kernel(s_ref, block0, block1, block2, block3, rows_out):
    x = s_ref[1]
    rows = at(x, 64)
    for shift, block in enumerate((block0, block1, block2, block3)):
        cols = at(mod4(x - shift), 256)
        rows_out[0, :, cols] = block[rows, pl.ds(0, 256)]
        rows_out[1, :, cols] = block[rows, pl.ds(256, 256)]


def coupling_rows_kernel(s_ref, pair0, pair1, pair2, pair3, lower_out, upper_out):
    x = s_ref[1]
    rows = at(x, 64)
    for shift, pair in enumerate((pair0, pair1, pair2, pair3)):
        cols = at(mod4(x - shift), 256)
        lower_out[0, :, cols] = pair[rows, pl.ds(0, 256)]
        lower_out[1, :, cols] = pair[rows, pl.ds(256, 256)]
        upper_out[0, :, cols] = pair[rows, pl.ds(512, 256)]
        upper_out[1, :, cols] = pair[rows, pl.ds(768, 256)]


def unpack(solved, vector):
    low, high = halves(solved[...].astype(F32))
    vector[pl.ds(0, 512), :] = low.astype(BF)
    vector[pl.ds(512, 512), :] = high.astype(BF)


def blocks_product(x, blocks, vector):
    real_rows = imag_rows = None
    for shift, block in enumerate(blocks):
        real, imag = block_product(block, vector[at(mod4(x - shift), 256), :])
        real_rows = real if real_rows is None else real_rows + real
        imag_rows = imag if imag_rows is None else imag_rows + imag
    return combine_small(real_rows, imag_rows)


def couple_kernel(s_ref, pair0, pair1, pair2, pair3, source, solved, below, above,
                  out0, out1, out2, out3, held, vector):
    y, x = s_ref[0], s_ref[1]
    pairs = (pair0, pair1, pair2, pair3)
    unpack(below, vector)
    combined = source[...].astype(F32)
    combined = combined - blocks_product(x, [p.at[:, pl.ds(0, 512)] for p in pairs], vector)
    unpack(above, vector)
    combined = combined - blocks_product(x, [p.at[:, pl.ds(512, 512)] for p in pairs], vector)
    rows = pl.ds(pl.multiple_of(lax.rem(y, 2) * 256, 256), 256)
    moved = pltpu.roll(solved[rows, :].astype(F32), jnp.where(y < 2, 64, 0), 1)
    held[...] = jnp.where(lanes_of(256) < 64, combined, moved)
    for shift, out in enumerate((out0, out1, out2, out3)):
        out[...] = held[at(mod4(x + shift), 64), :]


def spread_kernel(s_ref, piece0, piece1, piece2, piece3, combined, solved):
    x = s_ref[1]
    lane = lanes_of(64)
    totals = [jnp.zeros((64, 128), F32) for _ in range(4)]
    for shift, piece in enumerate((piece0, piece1, piece2, piece3)):
        chunk = mod4(x - shift)
        value = piece[...]
        on = (lane >= chunk * 32) & (lane < chunk * 32 + 32)
        for place in range(4):
            turned = pltpu.roll(value, mod4(chunk - place) * 32, 1)
            totals[place] = jnp.where(on, turned, totals[place])
    combined[0] = totals[0]
    combined[1] = totals[1]
    solved[0] = totals[2]
    solved[1] = totals[3]


def moved_x(block, by):
    pairs = [(y * 4 + x, y * 4 + (x + by) % 4) for y in range(4) for x in range(4)]
    return lax.ppermute(block, "row", pairs)


def moved_y(block, by):
    pairs = [(y * 4 + x, ((y + by) % 4) * 4 + x) for y in range(4) for x in range(4)]
    return lax.ppermute(block, "row", pairs)


def gathered_y(block):
    return (block, moved_y(block, 3), moved_y(block, 2), moved_y(block, 1))


def split_kernel(s_ref, block, other, low, high):
    low[...] = block[pl.ds(0, 128), :]
    high[...] = other[pl.ds(128, 128), :]


def ring_gathered_y(scalars, block, beside):
    above, below, rows = lax.optimization_barrier(
        (moved_y(block, 3), moved_y(block, 1), beside[0])
    )
    half = shape((128, block.shape[1]))
    low, high = call(split_kernel, [half, half], 0, scalars, below, above)
    low, high, *couplings = lax.optimization_barrier(
        (moved_y(low, 1), moved_y(high, 3), *beside[1:])
    )
    return (block, above, below, low, high), (rows, *couplings)


def gathered_x(block):
    groups = [[y * 4 + x for x in range(4)] for y in range(4)]
    return lax.all_gather(block, "row", axis_index_groups=groups)


def along_cuts(block, by):
    count = lax.axis_size("cuts")
    pairs = [(i, i + by) for i in range(count) if 0 <= i + by < count]
    return lax.ppermute(block, "cuts", pairs)


def body(diagonal_blocks, diagonal_inverses, lower_blocks, upper_blocks, injection, orbitals):
    cut = lax.axis_index("cuts")
    place = lax.axis_index("row")
    zero = jnp.zeros((1,), jnp.int32)
    window = lax.dynamic_slice_in_dim(jnp.concatenate([zero, orbitals, zero]), 2 * cut, 4)
    scalars = jnp.concatenate([jnp.stack([place // 4, place % 4]).astype(jnp.int32), window])
    turns = (1, 2, 3)
    after = lax.optimization_barrier
    wide_flops = 2 * 512 * 1024 * 512
    solve_flops = 2 * 2048 * 256 * 128

    *pieces, a_even, c_even, g_pieces, g_odd = call(
        prepare_kernel,
        [shape((64, 1664))] * 4 + [shape((2, 64, 1024))] * 2 + [shape((4, 2, 64, 256))]
        + [shape((2, 64, 1024))],
        0,
        scalars, diagonal_blocks, diagonal_inverses, lower_blocks, upper_blocks, injection,
        hbm=5,
        scratch=[pltpu.VMEM((2, 64, 1024), BF)] * 3
        + [pltpu.VMEM((2, 2, 64, 128), BF)]
        + [pltpu.VMEM((2, 64, 1024), BF)] * 3
        + [pltpu.SemaphoreType.DMA((11,))],
    )
    pieces = [pieces[0]] + [moved_x(pieces[by], by) for by in turns]
    g_rows = gathered_x(g_odd)
    a_next = along_cuts(a_even, -1)
    groups = [[y * 4 + x for y in range(4)] for x in range(4)]
    g_columns = lax.all_to_all(
        g_pieces, "row", 0, 0, axis_index_groups=groups, tiled=True
    )
    a_next, g_columns, *pieces = after((a_next, g_columns, *pieces))
    panel, diagonal, couplings = call(
        assemble_kernel,
        [shape((256, 1152)), shape((256, 512)), shape((2, 2, 64, 1024))],
        0, scalars, *pieces, c_even, a_next,
    )
    g_columns = gathered_x(g_columns)
    near = (g_rows, moved_x(couplings, 1), moved_x(couplings, 3))
    panels, near = ring_gathered_y(scalars, panel, near)
    g_rows = near[0]
    ca_blocks = [couplings, near[1], moved_x(couplings, 2), near[2]]
    first, second = call(
        odd_kernel, [shape((256, 640)), shape((304, 512))], wide_flops,
        scalars, g_rows, *panels,
        scratch=[pltpu.VMEM((512, 1024), BF), pltpu.VMEM((256, 1152), BF)],
    )
    firsts = gathered_y(first)
    second, g_columns, *ca_blocks = after((second, g_columns, *ca_blocks))
    seconds = gathered_y(second)
    ship, upper_new, source_part, a_rows, c_rows = call(
        even_kernel,
        [shape((288, 512)), shape((256, 512)), shape((256, 128), F32),
         shape((512, 1024)),
         shape((512, 1024))],
        2 * wide_flops,
        scalars, *ca_blocks, *firsts, panel, pinned=(1, 2, 3, 4),
    )
    shipped = along_cuts(ship, 1)
    diagonal_new, ship_lower = call(
        diagonal_kernel, [shape((256, 512))] * 2, 2 * wide_flops,
        scalars, c_rows, a_rows, *seconds, diagonal, shipped, pinned=(3, 7),
    )
    diagonals = [diagonal_new] + [moved_x(diagonal_new, by) for by in turns]
    packed_shapes = [shape((512, 128), F32), shape((512, 128))]
    whole = pltpu.VMEM((1024, 128), F32)
    vector = pltpu.VMEM((1024, 128), BF)
    source, own, send = call(
        source_kernel, [shape((256, 128))] + packed_shapes, solve_flops,
        scalars, g_columns, source_part, shipped, scratch=[whole],
    )
    got = gathered_y(send)[1:]
    lower_new = along_cuts(ship_lower, 1)
    (pair,) = call(pair_kernel, [shape((256, 1024))], 0, scalars, lower_new, upper_new)
    pairs = [pair] + [moved_x(pair, by) for by in turns]
    solved = ()
    for turn in range(REFINE):
        *solved, own, send = call(
            functools.partial(turn_kernel, first=turn == 0),
            [shape((512, 128))] + packed_shapes, 2 * solve_flops,
            scalars, own, *got, *solved, *diagonals, source, g_columns,
            scratch=[vector, whole],
        )
        got = gathered_y(send)[1:]
    (solved,) = call(
        last_kernel, [shape((512, 128))], 0,
        scalars, own, *got, *solved,
    )
    below, above = along_cuts(solved, 1), along_cuts(solved, -1)
    (diagonal_rows,) = call(
        diagonal_rows_kernel, [shape((2, 64, 1024))], 0, scalars, *diagonals
    )
    lower_rows, upper_rows = call(
        coupling_rows_kernel, [shape((2, 64, 1024))] * 2, 0, scalars, *pairs
    )
    below, diagonal_rows, lower_rows, upper_rows = after(
        (below, diagonal_rows, lower_rows, upper_rows)
    )
    ends = call(
        couple_kernel, [shape((64, 128), F32)] * 4, solve_flops // 2,
        scalars, *pairs, source, solved, below, above,
        scratch=[pltpu.VMEM((256, 128), F32), vector],
    )
    ends = [ends[0]] + [moved_x(ends[by], by) for by in turns]
    combined, solved_rows = call(
        spread_kernel, [shape((2, 64, 128), F32)] * 2, 0, scalars, *ends
    )
    return (
        diagonal_rows[None],
        lower_rows[None],
        upper_rows[None],
        combined[None],
        solved_rows[None],
    )


def solution(mesh):
    split = P("cuts", None, "row", None)
    return jax.shard_map(
        body,
        mesh=mesh,
        in_specs=(split, split, split, split, split, P()),
        out_specs=(split,) * 5,
        check_vma=False,
    )
```

```python
import functools

import jax
import jax.numpy as jnp
from jax import lax
from jax.experimental import pallas as pl
from jax.experimental.pallas import tpu as pltpu
from jax.sharding import PartitionSpec as P

REFINE = 2
BF = jnp.bfloat16
F32 = jnp.float32
VMEM = pl.BlockSpec(memory_space=pltpu.VMEM)
MIB = 12
SMEM = pl.BlockSpec(memory_space=pltpu.SMEM)


def call(kernel, out_shapes, flops, *args, scratch=(), hbm=0, mib=MIB, hbm_out=False, pinned=()):
    moved = sum(a.size * a.dtype.itemsize for a in args) + sum(
        s.size * s.dtype.itemsize for s in out_shapes
    )
    anywhere = pl.BlockSpec(memory_space=pltpu.HBM)
    args = [
        pltpu.with_memory_space_constraint(a, pltpu.HBM) if 0 < index <= hbm
        else pltpu.with_memory_space_constraint(a, pltpu.VMEM) if index in pinned
        else a
        for index, a in enumerate(args)
    ]
    return pl.pallas_call(
        kernel,
        out_shape=tuple(out_shapes),
        in_specs=[SMEM] + [anywhere] * hbm + [VMEM] * (len(args) - 1 - hbm),
        out_specs=tuple([anywhere if hbm_out else VMEM] * len(out_shapes)),
        scratch_shapes=list(scratch),
        compiler_params=pltpu.CompilerParams(vmem_limit_bytes=mib * 1024 * 1024),
        cost_estimate=pl.CostEstimate(flops=0, bytes_accessed=moved, transcendentals=0),
    )(*args)


def shape(dims, dtype=BF):
    return jax.ShapeDtypeStruct(dims, dtype)


def mod4(v):
    return lax.rem(v + 8, 4)


def at(chunk, size):
    return pl.ds(pl.multiple_of(chunk * size, size), size)


def lanes_of(rows):
    return lax.broadcasted_iota(jnp.int32, (rows, 128), 1)


def combine_small(real_rows, imag_rows):
    lane = lanes_of(real_rows.shape[0])
    turned = jnp.where(lane < 32, -pltpu.roll(imag_rows, 96, 1), pltpu.roll(imag_rows, 32, 1))
    return jnp.where(lane < 64, real_rows + turned, 0.0)


def packed(block):
    half = block.shape[0] // 2
    return jnp.where(lanes_of(half) < 64, block[:half], pltpu.roll(block[half:], 64, 1))


def halves(block):
    return block, pltpu.roll(block, 64, 1)


def masked(block, first_row, rows_on, chunk, cols_on):
    row = first_row + lax.broadcasted_iota(jnp.int32, (64, 256), 0)
    col = chunk * 256 + lax.broadcasted_iota(jnp.int32, (64, 256), 1)
    return jnp.where((row < rows_on) & (col < cols_on), block.astype(F32), 0.0).astype(BF)


def prepare_kernel(s_ref, d_hbm, g_hbm, a_hbm, c_hbm, b_hbm, piece0, piece1, piece2, piece3,
                   a_even, c_even, g_pieces, g_odd,
                   d_ref, a_ref, c_ref, b_ref, a_first, c_first, g_first, sems):
    y, x = s_ref[0], s_ref[1]
    first_row = (y * 4 + x) * 64
    before, own, odd, after = s_ref[2], s_ref[3], s_ref[4], s_ref[5]
    copies = [
        pltpu.make_async_copy(source, target, sems.at[index])
        for index, (source, target) in enumerate(
            (
                (c_hbm.at[1, 0], c_ref.at[0]),
                (c_hbm.at[1, 1], c_ref.at[1]),
                (b_hbm, b_ref),
                (a_hbm.at[1, 0], a_ref.at[0]),
                (a_hbm.at[1, 1], a_ref.at[1]),
                (d_hbm.at[0, 0], d_ref.at[0]),
                (d_hbm.at[0, 1], d_ref.at[1]),
                (a_hbm.at[0], a_first),
                (c_hbm.at[0], c_first),
                (g_hbm.at[0], g_first),
                (g_hbm.at[1], g_odd),
            )
        )
    ]
    for copy in copies:
        copy.start()
    pieces = (piece0, piece1, piece2, piece3)
    row_b = first_row + lax.broadcasted_iota(jnp.int32, (64, 128), 0)
    lane = lanes_of(64)
    copies[0].wait()
    copies[1].wait()
    for shift, piece in enumerate(pieces):
        chunk = mod4(x + shift)
        for part in range(2):
            piece[:, pl.ds(part * 256, 256)] = masked(
                c_ref[part, :, at(chunk, 256)], first_row, odd, chunk, after
            )
    copies[2].wait()
    blocks = [
        jnp.where(row_b < rows_on, b_ref[which, part].astype(F32), 0.0)
        for which, part, rows_on in ((1, 0, odd), (1, 1, odd), (0, 0, own), (0, 1, own))
    ]
    for shift, piece in enumerate(pieces):
        chunk = mod4(x + shift)
        tile = jnp.zeros((64, 128), F32)
        for place, block in enumerate(blocks):
            turned = pltpu.roll(block, mod4(place - chunk) * 32, 1)
            tile = jnp.where((lane >= place * 32) & (lane < place * 32 + 32), turned, tile)
        piece[:, pl.ds(512, 128)] = tile.astype(BF)
    copies[3].wait()
    copies[4].wait()
    for shift, piece in enumerate(pieces):
        chunk = mod4(x + shift)
        for part in range(2):
            piece[:, pl.ds(640 + part * 256, 256)] = masked(
                a_ref[part, :, at(chunk, 256)], first_row, odd, chunk, own
            )
    copies[5].wait()
    copies[6].wait()
    for shift, piece in enumerate(pieces):
        chunk = mod4(x + shift)
        for part in range(2):
            piece[:, pl.ds(1152 + part * 256, 256)] = d_ref[part, :, at(chunk, 256)]
    copies[7].wait()
    copies[8].wait()
    for chunk in range(4):
        cols = pl.ds(chunk * 256, 256)
        for part in range(2):
            a_even[part, :, cols] = masked(a_first[part, :, cols], first_row, own, chunk, before)
            c_even[part, :, cols] = masked(c_first[part, :, cols], first_row, own, chunk, odd)
    copies[9].wait()
    for chunk in range(4):
        for part in range(2):
            g_pieces[chunk, part] = g_first[part, :, pl.ds(chunk * 256, 256)]
    copies[10].wait()


def assemble_kernel(s_ref, piece0, piece1, piece2, piece3, c_even, a_next,
                    panel, diagonal, couplings):
    y, x = s_ref[0], s_ref[1]
    for shift, piece in enumerate((piece0, piece1, piece2, piece3)):
        rows = at(mod4(x - shift), 64)
        panel[rows, :] = piece[:, pl.ds(0, 1152)]
        diagonal[rows, :] = piece[:, pl.ds(1152, 512)]
    couplings[0] = c_even[...]
    couplings[1] = a_next[...]


def stack_rows(x, blocks, held):
    for shift, block in enumerate(blocks):
        held[at(mod4(x - shift), 128), :] = block[...].reshape(128, 1024)


def wide_dot(y, held, panels, start, width):
    total = None
    for place, panel in enumerate(panels):
        term = jnp.dot(
            held[:, at(mod4(y + place), 256)],
            panel[pl.ds(0, 256), pl.ds(start, width)],
            preferred_element_type=F32,
        )
        total = term if total is None else total + term
    parts = total.reshape(4, 2, 64, width)
    return parts[:, 0].reshape(256, width), parts[:, 1].reshape(256, width)


def wide_product(y, held, panels, start=0):
    real_rows, imag_rows = wide_dot(y, held, panels, start, 512)
    real = real_rows[:, :256] - imag_rows[:, 256:]
    imag = real_rows[:, 256:] + imag_rows[:, :256]
    return real, imag


def small_product(y, held, panels):
    return combine_small(*wide_dot(y, held, panels, 512, 128))


def put_pair(out, real, imag):
    out[pl.ds(0, 256), pl.ds(0, 256)] = real.astype(out.dtype)
    out[pl.ds(0, 256), pl.ds(256, 256)] = imag.astype(out.dtype)


def take_odd(s_ref, g_ref, panel0, panel1, panel3, low, high, held, panel2):
    panel2[pl.ds(0, 128), :] = low[...]
    panel2[pl.ds(128, 128), :] = high[...]
    held[...] = g_ref[...].reshape(512, 1024)
    return s_ref[0], held, (panel0, panel1, panel2, panel3)


def odd_kernel(s_ref, g_ref, panel0, panel1, panel3, low, high, out, held, panel2):
    taken = take_odd(s_ref, g_ref, panel0, panel1, panel3, low, high, held, panel2)
    put_pair(out, *wide_product(*taken))
    out[:, pl.ds(512, 128)] = small_product(*taken).astype(BF)


def odd_second_kernel(s_ref, g_ref, panel0, panel1, panel3, low, high, out, held, panel2):
    taken = take_odd(s_ref, g_ref, panel0, panel1, panel3, low, high, held, panel2)
    put_pair(out, *wide_product(*taken, 640))
    out[pl.ds(256, 48), :] = jnp.zeros((48, 512), BF)


def even_kernel(s_ref, ca0, ca1, ca2, ca3, panel0, panel1, panel2, panel3, ship, a_rows):
    y, x = s_ref[0], s_ref[1]
    panels = (panel0, panel1, panel2, panel3)
    stack_rows(x, [block.at[1] for block in (ca0, ca1, ca2, ca3)], a_rows)
    value = small_product(y, a_rows, panels)
    lane = lanes_of(32)
    for index in range(4):
        low, high = value[index * 64 : index * 64 + 32], value[index * 64 + 32 : index * 64 + 64]
        tile = jnp.where(lane < 64, low, pltpu.roll(high, 64, 1))
        ship[pl.ds(256, 32), pl.ds(index * 128, 128)] = tile.astype(BF)
    put_pair(ship, *wide_product(y, a_rows, panels))


def upper_kernel(s_ref, ca0, ca1, ca2, ca3, panel0, panel1, panel2, panel3, source,
                 upper_new, source_part, c_rows):
    y, x = s_ref[0], s_ref[1]
    panels = (panel0, panel1, panel2, panel3)
    stack_rows(x, [block.at[0] for block in (ca0, ca1, ca2, ca3)], c_rows)
    own = pltpu.roll(source[:, pl.ds(512, 128)].astype(F32), 64, 1)
    own = jnp.where(lanes_of(256) < 64, own, 0.0)
    source_part[...] = own - small_product(y, c_rows, panels)
    real, imag = wide_product(y, c_rows, panels)
    put_pair(upper_new, -real, -imag)


def diagonal_kernel(s_ref, c_rows, panel0, panel1, panel2, panel3, diagonal, shipped,
                    out):
    real, imag = wide_product(s_ref[0], c_rows, (panel0, panel1, panel2, panel3))
    real = diagonal[:, pl.ds(0, 256)].astype(F32) - real - shipped[pl.ds(0, 256), pl.ds(0, 256)].astype(F32)
    imag = diagonal[:, pl.ds(256, 256)].astype(F32) - imag - shipped[pl.ds(0, 256), pl.ds(256, 256)].astype(F32)
    put_pair(out, real, imag)


def lower_kernel(s_ref, a_rows, panel0, panel1, panel2, panel3, lower):
    real, imag = wide_product(s_ref[0], a_rows, (panel0, panel1, panel2, panel3))
    put_pair(lower, -real, -imag)


def pair_kernel(s_ref, lower, upper, out):
    out[:, pl.ds(0, 512)] = lower[...]
    out[:, pl.ds(512, 512)] = upper[...]


def block_product(block, right):
    real = jnp.dot(block[:, pl.ds(0, 256)], right, preferred_element_type=F32)
    imag = jnp.dot(block[:, pl.ds(256, 256)], right, preferred_element_type=F32)
    return real, imag


def put_partial(g_ref, right, own, send, whole):
    for index in range(4):
        total = jnp.dot(g_ref[index].reshape(512, 256), right, preferred_element_type=F32)
        parts = total.reshape(4, 2, 64, 128)
        value = combine_small(parts[:, 0].reshape(256, 128), parts[:, 1].reshape(256, 128))
        value = value.reshape(4, 64, 128)
        for group in range(4):
            whole[pl.ds(group * 256 + index * 64, 64), :] = value[group]
    total = packed(whole[...])
    own[...] = total
    send[...] = total.astype(BF)


def source_kernel(s_ref, g_ref, source_part, shipped, source_new, own, send, whole):
    lane = lanes_of(32)
    for index in range(4):
        tile = shipped[pl.ds(256, 32), pl.ds(index * 128, 128)].astype(F32)
        for half, moved in enumerate(halves(tile)):
            rows = pl.ds(index * 64 + half * 32, 32)
            value = source_part[rows, :] - jnp.where(lane < 64, moved, 0.0)
            source_new[rows, :] = value.astype(BF)
    source = source_new[...]
    put_partial(g_ref, source, own, send, whole)


def summed(own, got):
    total = own[...]
    for other in got:
        total = total + other[...].astype(F32)
    return total


def turn_kernel(s_ref, own, got1, got2, got3, *refs, first):
    solved = None if first else refs[0]
    blocks, refs = refs[:4] if first else refs[1:5], refs[4:] if first else refs[5:]
    source, g_ref, out, own_new, send, vector, whole = refs
    x = s_ref[1]
    total = summed(own, (got1, got2, got3))
    if not first:
        total = solved[...].astype(F32) + total
    out[...] = total.astype(BF)
    unpack(out, vector)
    residue = (source[...].astype(F32) - blocks_product(x, blocks, vector)).astype(BF)
    put_partial(g_ref, residue, own_new, send, whole)


def last_kernel(s_ref, own, got1, got2, got3, solved, out):
    out[...] = (solved[...].astype(F32) + summed(own, (got1, got2, got3))).astype(BF)


def diagonal_rows_kernel(s_ref, block0, block1, block2, block3, rows_out):
    x = s_ref[1]
    rows = at(x, 64)
    for shift, block in enumerate((block0, block1, block2, block3)):
        cols = at(mod4(x - shift), 256)
        rows_out[0, :, cols] = block[rows, pl.ds(0, 256)]
        rows_out[1, :, cols] = block[rows, pl.ds(256, 256)]


def coupling_rows_kernel(s_ref, pair0, pair1, pair2, pair3, lower_out, upper_out):
    x = s_ref[1]
    rows = at(x, 64)
    for shift, pair in enumerate((pair0, pair1, pair2, pair3)):
        cols = at(mod4(x - shift), 256)
        lower_out[0, :, cols] = pair[rows, pl.ds(0, 256)]
        lower_out[1, :, cols] = pair[rows, pl.ds(256, 256)]
        upper_out[0, :, cols] = pair[rows, pl.ds(512, 256)]
        upper_out[1, :, cols] = pair[rows, pl.ds(768, 256)]


def unpack(solved, vector):
    low, high = halves(solved[...].astype(F32))
    vector[pl.ds(0, 512), :] = low.astype(BF)
    vector[pl.ds(512, 512), :] = high.astype(BF)


def blocks_product(x, blocks, vector):
    real_rows = imag_rows = None
    for shift, block in enumerate(blocks):
        real, imag = block_product(block, vector[at(mod4(x - shift), 256), :])
        real_rows = real if real_rows is None else real_rows + real
        imag_rows = imag if imag_rows is None else imag_rows + imag
    return combine_small(real_rows, imag_rows)


def couple_kernel(s_ref, pair0, pair1, pair2, pair3, source, solved, below, above,
                  out0, out1, out2, out3, held, vector):
    y, x = s_ref[0], s_ref[1]
    pairs = (pair0, pair1, pair2, pair3)
    unpack(below, vector)
    combined = source[...].astype(F32)
    combined = combined - blocks_product(x, [p.at[:, pl.ds(0, 512)] for p in pairs], vector)
    unpack(above, vector)
    combined = combined - blocks_product(x, [p.at[:, pl.ds(512, 512)] for p in pairs], vector)
    rows = pl.ds(pl.multiple_of(lax.rem(y, 2) * 256, 256), 256)
    moved = pltpu.roll(solved[rows, :].astype(F32), jnp.where(y < 2, 64, 0), 1)
    held[...] = jnp.where(lanes_of(256) < 64, combined, moved)
    for shift, out in enumerate((out0, out1, out2, out3)):
        out[...] = held[at(mod4(x + shift), 64), :]


def spread_kernel(s_ref, piece0, piece1, piece2, piece3, combined, solved):
    x = s_ref[1]
    lane = lanes_of(64)
    totals = [jnp.zeros((64, 128), F32) for _ in range(4)]
    for shift, piece in enumerate((piece0, piece1, piece2, piece3)):
        chunk = mod4(x - shift)
        value = piece[...]
        on = (lane >= chunk * 32) & (lane < chunk * 32 + 32)
        for place in range(4):
            turned = pltpu.roll(value, mod4(chunk - place) * 32, 1)
            totals[place] = jnp.where(on, turned, totals[place])
    combined[0] = totals[0]
    combined[1] = totals[1]
    solved[0] = totals[2]
    solved[1] = totals[3]


def moved_x(block, by):
    pairs = [(y * 4 + x, y * 4 + (x + by) % 4) for y in range(4) for x in range(4)]
    return lax.ppermute(block, "row", pairs)


def moved_y(block, by):
    pairs = [(y * 4 + x, ((y + by) % 4) * 4 + x) for y in range(4) for x in range(4)]
    return lax.ppermute(block, "row", pairs)


def gathered_y(block):
    return (block, moved_y(block, 3), moved_y(block, 2), moved_y(block, 1))


def split_kernel(s_ref, block, other, low, high):
    low[...] = block[pl.ds(0, 128), :]
    high[...] = other[pl.ds(128, 128), :]


def ring_gathered_y(scalars, block, beside):
    above, below, rows = lax.optimization_barrier(
        (moved_y(block, 3), moved_y(block, 1), beside[0])
    )
    half = shape((128, block.shape[1]))
    low, high = call(split_kernel, [half, half], 0, scalars, below, above)
    low, high, *couplings = lax.optimization_barrier(
        (moved_y(low, 1), moved_y(high, 3), *beside[1:])
    )
    return (block, above, below, low, high), (rows, *couplings)


def gathered_x(block):
    groups = [[y * 4 + x for x in range(4)] for y in range(4)]
    return lax.all_gather(block, "row", axis_index_groups=groups)


def along_cuts(block, by):
    count = lax.axis_size("cuts")
    pairs = [(i, i + by) for i in range(count) if 0 <= i + by < count]
    return lax.ppermute(block, "cuts", pairs)


def body(diagonal_blocks, diagonal_inverses, lower_blocks, upper_blocks, injection, orbitals):
    cut = lax.axis_index("cuts")
    place = lax.axis_index("row")
    zero = jnp.zeros((1,), jnp.int32)
    window = lax.dynamic_slice_in_dim(jnp.concatenate([zero, orbitals, zero]), 2 * cut, 4)
    scalars = jnp.concatenate([jnp.stack([place // 4, place % 4]).astype(jnp.int32), window])
    turns = (1, 2, 3)
    after = lax.optimization_barrier
    wide_flops = 2 * 512 * 1024 * 512
    solve_flops = 2 * 2048 * 256 * 128

    *pieces, a_even, c_even, g_pieces, g_odd = call(
        prepare_kernel,
        [shape((64, 1664))] * 4 + [shape((2, 64, 1024))] * 2 + [shape((4, 2, 64, 256))]
        + [shape((2, 64, 1024))],
        0,
        scalars, diagonal_blocks, diagonal_inverses, lower_blocks, upper_blocks, injection,
        hbm=5,
        scratch=[pltpu.VMEM((2, 64, 1024), BF)] * 3
        + [pltpu.VMEM((2, 2, 64, 128), BF)]
        + [pltpu.VMEM((2, 64, 1024), BF)] * 3
        + [pltpu.SemaphoreType.DMA((11,))],
    )
    pieces = [pieces[0]] + [moved_x(pieces[by], by) for by in turns]
    g_rows = gathered_x(g_odd)
    a_next = along_cuts(a_even, -1)
    groups = [[y * 4 + x for y in range(4)] for x in range(4)]
    g_columns = lax.all_to_all(
        g_pieces, "row", 0, 0, axis_index_groups=groups, tiled=True
    )
    a_next, g_columns, *pieces = after((a_next, g_columns, *pieces))
    panel, diagonal, couplings = call(
        assemble_kernel,
        [shape((256, 1152)), shape((256, 512)), shape((2, 2, 64, 1024))],
        0, scalars, *pieces, c_even, a_next,
    )
    g_columns = gathered_x(g_columns)
    near = (g_rows, moved_x(couplings, 1), moved_x(couplings, 3))
    panels, near = ring_gathered_y(scalars, panel, near)
    g_rows = near[0]
    ca_blocks = [couplings, near[1], moved_x(couplings, 2), near[2]]
    taken = [pltpu.VMEM((512, 1024), BF), pltpu.VMEM((256, 1152), BF)]
    (first,) = call(
        odd_kernel, [shape((256, 640))], wide_flops, scalars, g_rows, *panels, scratch=taken
    )
    (second,) = call(
        odd_second_kernel, [shape((304, 512))], wide_flops,
        scalars, g_rows, *panels, scratch=taken,
    )
    firsts = gathered_y(first)
    second, g_columns, *ca_blocks = after((second, g_columns, *ca_blocks))
    seconds = gathered_y(second)
    ship, a_rows = call(
        even_kernel, [shape((288, 512)), shape((512, 1024))], wide_flops,
        scalars, *ca_blocks, *firsts,
    )
    upper_new, source_part, c_rows = call(
        upper_kernel,
        [shape((256, 512)), shape((256, 128), F32), shape((512, 1024))],
        wide_flops,
        scalars, *ca_blocks, *firsts, panel,
    )
    shipped = along_cuts(ship, 1)
    (diagonal_new,) = call(
        diagonal_kernel, [shape((256, 512))], wide_flops,
        scalars, c_rows, *seconds, diagonal, shipped,
    )
    (ship_lower,) = call(
        lower_kernel, [shape((256, 512))], wide_flops, scalars, a_rows, *seconds
    )
    diagonals = [diagonal_new] + [moved_x(diagonal_new, by) for by in turns]
    packed_shapes = [shape((512, 128), F32), shape((512, 128))]
    whole = pltpu.VMEM((1024, 128), F32)
    vector = pltpu.VMEM((1024, 128), BF)
    source, own, send = call(
        source_kernel, [shape((256, 128))] + packed_shapes, solve_flops,
        scalars, g_columns, source_part, shipped, scratch=[whole],
    )
    got = gathered_y(send)[1:]
    lower_new = along_cuts(ship_lower, 1)
    (pair,) = call(pair_kernel, [shape((256, 1024))], 0, scalars, lower_new, upper_new)
    pairs = [pair] + [moved_x(pair, by) for by in turns]
    solved = ()
    for turn in range(REFINE):
        *solved, own, send = call(
            functools.partial(turn_kernel, first=turn == 0),
            [shape((512, 128))] + packed_shapes, 2 * solve_flops,
            scalars, own, *got, *solved, *diagonals, source, g_columns,
            scratch=[vector, whole],
        )
        got = gathered_y(send)[1:]
    (solved,) = call(
        last_kernel, [shape((512, 128))], 0,
        scalars, own, *got, *solved,
    )
    below, above = along_cuts(solved, 1), along_cuts(solved, -1)
    (diagonal_rows,) = call(
        diagonal_rows_kernel, [shape((2, 64, 1024))], 0, scalars, *diagonals
    )
    lower_rows, upper_rows = call(
        coupling_rows_kernel, [shape((2, 64, 1024))] * 2, 0, scalars, *pairs
    )
    below, diagonal_rows, lower_rows, upper_rows = after(
        (below, diagonal_rows, lower_rows, upper_rows)
    )
    ends = call(
        couple_kernel, [shape((64, 128), F32)] * 4, solve_flops // 2,
        scalars, *pairs, source, solved, below, above,
        scratch=[pltpu.VMEM((256, 128), F32), vector],
    )
    ends = [ends[0]] + [moved_x(ends[by], by) for by in turns]
    combined, solved_rows = call(
        spread_kernel, [shape((2, 64, 128), F32)] * 2, 0, scalars, *ends
    )
    return (
        diagonal_rows[None],
        lower_rows[None],
        upper_rows[None],
        combined[None],
        solved_rows[None],
    )


def solution(mesh):
    split = P("cuts", None, "row", None)
    return jax.shard_map(
        body,
        mesh=mesh,
        in_specs=(split, split, split, split, split, P()),
        out_specs=(split,) * 5,
        check_vma=False,
    )
```

```python
import functools

import jax
import jax.numpy as jnp
from jax import lax
from jax.experimental import pallas as pl
from jax.experimental.pallas import tpu as pltpu
from jax.sharding import PartitionSpec as P

REFINE = 2
BF = jnp.bfloat16
F32 = jnp.float32
VMEM = pl.BlockSpec(memory_space=pltpu.VMEM)
MIB = 8
SMEM = pl.BlockSpec(memory_space=pltpu.SMEM)


def call(kernel, out_shapes, flops, *args, scratch=(), hbm=0, mib=MIB, hbm_out=False, pinned=()):
    moved = sum(a.size * a.dtype.itemsize for a in args) + sum(
        s.size * s.dtype.itemsize for s in out_shapes
    )
    anywhere = pl.BlockSpec(memory_space=pltpu.HBM)
    args = [
        pltpu.with_memory_space_constraint(a, pltpu.HBM) if 0 < index <= hbm
        else pltpu.with_memory_space_constraint(a, pltpu.VMEM) if index in pinned
        else a
        for index, a in enumerate(args)
    ]
    return pl.pallas_call(
        kernel,
        out_shape=tuple(out_shapes),
        in_specs=[SMEM] + [anywhere] * hbm + [VMEM] * (len(args) - 1 - hbm),
        out_specs=tuple([anywhere if hbm_out else VMEM] * len(out_shapes)),
        scratch_shapes=list(scratch),
        compiler_params=pltpu.CompilerParams(vmem_limit_bytes=mib * 1024 * 1024),
        cost_estimate=pl.CostEstimate(flops=0, bytes_accessed=moved, transcendentals=0),
    )(*args)


def shape(dims, dtype=BF):
    return jax.ShapeDtypeStruct(dims, dtype)


def mod4(v):
    return lax.rem(v + 8, 4)


def at(chunk, size):
    return pl.ds(pl.multiple_of(chunk * size, size), size)


def lanes_of(rows):
    return lax.broadcasted_iota(jnp.int32, (rows, 128), 1)


def combine_small(real_rows, imag_rows):
    lane = lanes_of(real_rows.shape[0])
    turned = jnp.where(lane < 32, -pltpu.roll(imag_rows, 96, 1), pltpu.roll(imag_rows, 32, 1))
    return jnp.where(lane < 64, real_rows + turned, 0.0)


def packed(block):
    half = block.shape[0] // 2
    return jnp.where(lanes_of(half) < 64, block[:half], pltpu.roll(block[half:], 64, 1))


def halves(block):
    return block, pltpu.roll(block, 64, 1)


def masked(block, first_row, rows_on, chunk, cols_on):
    row = first_row + lax.broadcasted_iota(jnp.int32, (64, 256), 0)
    col = chunk * 256 + lax.broadcasted_iota(jnp.int32, (64, 256), 1)
    return jnp.where((row < rows_on) & (col < cols_on), block.astype(F32), 0.0).astype(BF)


def prepare_kernel(s_ref, d_hbm, g_hbm, a_hbm, c_hbm, b_hbm, piece0, piece1, piece2, piece3,
                   a_even, c_even, g_pieces, g_odd,
                   d_ref, a_ref, c_ref, b_ref, a_first, c_first, g_first, sems):
    y, x = s_ref[0], s_ref[1]
    first_row = (y * 4 + x) * 64
    before, own, odd, after = s_ref[2], s_ref[3], s_ref[4], s_ref[5]
    copies = [
        pltpu.make_async_copy(source, target, sems.at[index])
        for index, (source, target) in enumerate(
            (
                (c_hbm.at[1, 0], c_ref.at[0]),
                (c_hbm.at[1, 1], c_ref.at[1]),
                (b_hbm, b_ref),
                (a_hbm.at[1, 0], a_ref.at[0]),
                (a_hbm.at[1, 1], a_ref.at[1]),
                (d_hbm.at[0, 0], d_ref.at[0]),
                (d_hbm.at[0, 1], d_ref.at[1]),
                (a_hbm.at[0], a_first),
                (c_hbm.at[0], c_first),
                (g_hbm.at[0], g_first),
                (g_hbm.at[1], g_odd),
            )
        )
    ]
    for copy in copies:
        copy.start()
    pieces = (piece0, piece1, piece2, piece3)
    row_b = first_row + lax.broadcasted_iota(jnp.int32, (64, 128), 0)
    lane = lanes_of(64)
    copies[0].wait()
    copies[1].wait()
    for shift, piece in enumerate(pieces):
        chunk = mod4(x + shift)
        for part in range(2):
            piece[:, pl.ds(part * 256, 256)] = masked(
                c_ref[part, :, at(chunk, 256)], first_row, odd, chunk, after
            )
    copies[2].wait()
    blocks = [
        jnp.where(row_b < rows_on, b_ref[which, part].astype(F32), 0.0)
        for which, part, rows_on in ((1, 0, odd), (1, 1, odd), (0, 0, own), (0, 1, own))
    ]
    for shift, piece in enumerate(pieces):
        chunk = mod4(x + shift)
        tile = jnp.zeros((64, 128), F32)
        for place, block in enumerate(blocks):
            turned = pltpu.roll(block, mod4(place - chunk) * 32, 1)
            tile = jnp.where((lane >= place * 32) & (lane < place * 32 + 32), turned, tile)
        piece[:, pl.ds(512, 128)] = tile.astype(BF)
    copies[3].wait()
    copies[4].wait()
    for shift, piece in enumerate(pieces):
        chunk = mod4(x + shift)
        for part in range(2):
            piece[:, pl.ds(640 + part * 256, 256)] = masked(
                a_ref[part, :, at(chunk, 256)], first_row, odd, chunk, own
            )
    copies[5].wait()
    copies[6].wait()
    for shift, piece in enumerate(pieces):
        chunk = mod4(x + shift)
        for part in range(2):
            piece[:, pl.ds(1152 + part * 256, 256)] = d_ref[part, :, at(chunk, 256)]
    copies[7].wait()
    copies[8].wait()
    for chunk in range(4):
        cols = pl.ds(chunk * 256, 256)
        for part in range(2):
            a_even[part, :, cols] = masked(a_first[part, :, cols], first_row, own, chunk, before)
            c_even[part, :, cols] = masked(c_first[part, :, cols], first_row, own, chunk, odd)
    copies[9].wait()
    for chunk in range(4):
        for part in range(2):
            g_pieces[chunk, part] = g_first[part, :, pl.ds(chunk * 256, 256)]
    copies[10].wait()


def assemble_kernel(s_ref, piece0, piece1, piece2, piece3, c_even, a_next,
                    panel, diagonal, couplings):
    y, x = s_ref[0], s_ref[1]
    for shift, piece in enumerate((piece0, piece1, piece2, piece3)):
        rows = at(mod4(x - shift), 64)
        panel[rows, :] = piece[:, pl.ds(0, 1152)]
        diagonal[rows, :] = piece[:, pl.ds(1152, 512)]
    couplings[0] = c_even[...]
    couplings[1] = a_next[...]


def stack_rows(x, blocks, held):
    for shift, block in enumerate(blocks):
        held[at(mod4(x - shift), 128), :] = block[...].reshape(128, 1024)


def wide_dot(y, held, panels, start, width):
    total = None
    for place, panel in enumerate(panels):
        term = jnp.dot(
            held[:, at(mod4(y + place), 256)],
            panel[pl.ds(0, 256), pl.ds(start, width)],
            preferred_element_type=F32,
        )
        total = term if total is None else total + term
    parts = total.reshape(4, 2, 64, width)
    return parts[:, 0].reshape(256, width), parts[:, 1].reshape(256, width)


def wide_product(y, held, panels, start=0):
    real_rows, imag_rows = wide_dot(y, held, panels, start, 512)
    real = real_rows[:, :256] - imag_rows[:, 256:]
    imag = real_rows[:, 256:] + imag_rows[:, :256]
    return real, imag


def small_product(y, held, panels):
    return combine_small(*wide_dot(y, held, panels, 512, 128))


def put_pair(out, real, imag):
    out[pl.ds(0, 256), pl.ds(0, 256)] = real.astype(out.dtype)
    out[pl.ds(0, 256), pl.ds(256, 256)] = imag.astype(out.dtype)


def take_odd(s_ref, g_ref, panel0, panel1, panel3, low, high, held, panel2):
    panel2[pl.ds(0, 128), :] = low[...]
    panel2[pl.ds(128, 128), :] = high[...]
    held[...] = g_ref[...].reshape(512, 1024)
    return s_ref[0], held, (panel0, panel1, panel2, panel3)


def odd_kernel(s_ref, g_ref, panel0, panel1, panel3, low, high, out, held, panel2):
    taken = take_odd(s_ref, g_ref, panel0, panel1, panel3, low, high, held, panel2)
    put_pair(out, *wide_product(*taken))
    out[:, pl.ds(512, 128)] = small_product(*taken).astype(BF)


def odd_second_kernel(s_ref, g_ref, panel0, panel1, panel3, low, high, out, held, panel2):
    taken = take_odd(s_ref, g_ref, panel0, panel1, panel3, low, high, held, panel2)
    put_pair(out, *wide_product(*taken, 640))
    out[pl.ds(256, 48), :] = jnp.zeros((48, 512), BF)


def even_kernel(s_ref, ca0, ca1, ca2, ca3, panel0, panel1, panel2, panel3, ship, a_rows):
    y, x = s_ref[0], s_ref[1]
    panels = (panel0, panel1, panel2, panel3)
    stack_rows(x, [block.at[1] for block in (ca0, ca1, ca2, ca3)], a_rows)
    value = small_product(y, a_rows, panels)
    lane = lanes_of(32)
    for index in range(4):
        low, high = value[index * 64 : index * 64 + 32], value[index * 64 + 32 : index * 64 + 64]
        tile = jnp.where(lane < 64, low, pltpu.roll(high, 64, 1))
        ship[pl.ds(256, 32), pl.ds(index * 128, 128)] = tile.astype(BF)
    put_pair(ship, *wide_product(y, a_rows, panels))


def upper_kernel(s_ref, ca0, ca1, ca2, ca3, panel0, panel1, panel2, panel3, source,
                 upper_new, source_part, c_rows):
    y, x = s_ref[0], s_ref[1]
    panels = (panel0, panel1, panel2, panel3)
    stack_rows(x, [block.at[0] for block in (ca0, ca1, ca2, ca3)], c_rows)
    own = pltpu.roll(source[:, pl.ds(512, 128)].astype(F32), 64, 1)
    own = jnp.where(lanes_of(256) < 64, own, 0.0)
    source_part[...] = own - small_product(y, c_rows, panels)
    real, imag = wide_product(y, c_rows, panels)
    put_pair(upper_new, -real, -imag)


def diagonal_kernel(s_ref, c_rows, panel0, panel1, panel2, panel3, diagonal, shipped,
                    out):
    real, imag = wide_product(s_ref[0], c_rows, (panel0, panel1, panel2, panel3))
    real = diagonal[:, pl.ds(0, 256)].astype(F32) - real - shipped[pl.ds(0, 256), pl.ds(0, 256)].astype(F32)
    imag = diagonal[:, pl.ds(256, 256)].astype(F32) - imag - shipped[pl.ds(0, 256), pl.ds(256, 256)].astype(F32)
    put_pair(out, real, imag)


def lower_kernel(s_ref, a_rows, panel0, panel1, panel2, panel3, lower):
    real, imag = wide_product(s_ref[0], a_rows, (panel0, panel1, panel2, panel3))
    put_pair(lower, -real, -imag)


def pair_kernel(s_ref, lower, upper, out):
    out[:, pl.ds(0, 512)] = lower[...]
    out[:, pl.ds(512, 512)] = upper[...]


def block_product(block, right):
    real = jnp.dot(block[:, pl.ds(0, 256)], right, preferred_element_type=F32)
    imag = jnp.dot(block[:, pl.ds(256, 256)], right, preferred_element_type=F32)
    return real, imag


def put_partial(g_ref, right, own, send, whole):
    for index in range(4):
        total = jnp.dot(g_ref[index].reshape(512, 256), right, preferred_element_type=F32)
        parts = total.reshape(4, 2, 64, 128)
        value = combine_small(parts[:, 0].reshape(256, 128), parts[:, 1].reshape(256, 128))
        value = value.reshape(4, 64, 128)
        for group in range(4):
            whole[pl.ds(group * 256 + index * 64, 64), :] = value[group]
    total = packed(whole[...])
    own[...] = total
    send[...] = total.astype(BF)


def source_kernel(s_ref, g_ref, source_part, shipped, source_new, own, send, whole):
    lane = lanes_of(32)
    for index in range(4):
        tile = shipped[pl.ds(256, 32), pl.ds(index * 128, 128)].astype(F32)
        for half, moved in enumerate(halves(tile)):
            rows = pl.ds(index * 64 + half * 32, 32)
            value = source_part[rows, :] - jnp.where(lane < 64, moved, 0.0)
            source_new[rows, :] = value.astype(BF)
    source = source_new[...]
    put_partial(g_ref, source, own, send, whole)


def summed(own, got):
    total = own[...]
    for other in got:
        total = total + other[...].astype(F32)
    return total


def turn_kernel(s_ref, own, got1, got2, got3, *refs, first):
    solved = None if first else refs[0]
    blocks, refs = refs[:4] if first else refs[1:5], refs[4:] if first else refs[5:]
    source, g_ref, out, own_new, send, vector, whole = refs
    x = s_ref[1]
    total = summed(own, (got1, got2, got3))
    if not first:
        total = solved[...].astype(F32) + total
    out[...] = total.astype(BF)
    unpack(out, vector)
    residue = (source[...].astype(F32) - blocks_product(x, blocks, vector)).astype(BF)
    put_partial(g_ref, residue, own_new, send, whole)


def last_kernel(s_ref, own, got1, got2, got3, solved, out):
    out[...] = (solved[...].astype(F32) + summed(own, (got1, got2, got3))).astype(BF)


def diagonal_rows_kernel(s_ref, block0, block1, block2, block3, rows_out):
    x = s_ref[1]
    rows = at(x, 64)
    for shift, block in enumerate((block0, block1, block2, block3)):
        cols = at(mod4(x - shift), 256)
        rows_out[0, :, cols] = block[rows, pl.ds(0, 256)]
        rows_out[1, :, cols] = block[rows, pl.ds(256, 256)]


def coupling_rows_kernel(s_ref, pair0, pair1, pair2, pair3, lower_out, upper_out):
    x = s_ref[1]
    rows = at(x, 64)
    for shift, pair in enumerate((pair0, pair1, pair2, pair3)):
        cols = at(mod4(x - shift), 256)
        lower_out[0, :, cols] = pair[rows, pl.ds(0, 256)]
        lower_out[1, :, cols] = pair[rows, pl.ds(256, 256)]
        upper_out[0, :, cols] = pair[rows, pl.ds(512, 256)]
        upper_out[1, :, cols] = pair[rows, pl.ds(768, 256)]


def unpack(solved, vector):
    low, high = halves(solved[...].astype(F32))
    vector[pl.ds(0, 512), :] = low.astype(BF)
    vector[pl.ds(512, 512), :] = high.astype(BF)


def blocks_product(x, blocks, vector):
    real_rows = imag_rows = None
    for shift, block in enumerate(blocks):
        real, imag = block_product(block, vector[at(mod4(x - shift), 256), :])
        real_rows = real if real_rows is None else real_rows + real
        imag_rows = imag if imag_rows is None else imag_rows + imag
    return combine_small(real_rows, imag_rows)


def couple_kernel(s_ref, pair0, pair1, pair2, pair3, source, solved, below, above,
                  out0, out1, out2, out3, held, vector):
    y, x = s_ref[0], s_ref[1]
    pairs = (pair0, pair1, pair2, pair3)
    unpack(below, vector)
    combined = source[...].astype(F32)
    combined = combined - blocks_product(x, [p.at[:, pl.ds(0, 512)] for p in pairs], vector)
    unpack(above, vector)
    combined = combined - blocks_product(x, [p.at[:, pl.ds(512, 512)] for p in pairs], vector)
    rows = pl.ds(pl.multiple_of(lax.rem(y, 2) * 256, 256), 256)
    moved = pltpu.roll(solved[rows, :].astype(F32), jnp.where(y < 2, 64, 0), 1)
    held[...] = jnp.where(lanes_of(256) < 64, combined, moved)
    for shift, out in enumerate((out0, out1, out2, out3)):
        out[...] = held[at(mod4(x + shift), 64), :]


def spread_kernel(s_ref, piece0, piece1, piece2, piece3, combined, solved):
    x = s_ref[1]
    lane = lanes_of(64)
    totals = [jnp.zeros((64, 128), F32) for _ in range(4)]
    for shift, piece in enumerate((piece0, piece1, piece2, piece3)):
        chunk = mod4(x - shift)
        value = piece[...]
        on = (lane >= chunk * 32) & (lane < chunk * 32 + 32)
        for place in range(4):
            turned = pltpu.roll(value, mod4(chunk - place) * 32, 1)
            totals[place] = jnp.where(on, turned, totals[place])
    combined[0] = totals[0]
    combined[1] = totals[1]
    solved[0] = totals[2]
    solved[1] = totals[3]


def moved_x(block, by):
    pairs = [(y * 4 + x, y * 4 + (x + by) % 4) for y in range(4) for x in range(4)]
    return lax.ppermute(block, "row", pairs)


def moved_y(block, by):
    pairs = [(y * 4 + x, ((y + by) % 4) * 4 + x) for y in range(4) for x in range(4)]
    return lax.ppermute(block, "row", pairs)


def gathered_y(block):
    return (block, moved_y(block, 3), moved_y(block, 2), moved_y(block, 1))


def split_kernel(s_ref, block, other, low, high):
    low[...] = block[pl.ds(0, 128), :]
    high[...] = other[pl.ds(128, 128), :]


def ring_gathered_y(scalars, block, beside):
    above, below, rows = lax.optimization_barrier(
        (moved_y(block, 3), moved_y(block, 1), beside[0])
    )
    half = shape((128, block.shape[1]))
    low, high = call(split_kernel, [half, half], 0, scalars, below, above)
    low, high, *couplings = lax.optimization_barrier(
        (moved_y(low, 1), moved_y(high, 3), *beside[1:])
    )
    return (block, above, below, low, high), (rows, *couplings)


def gathered_x(block):
    groups = [[y * 4 + x for x in range(4)] for y in range(4)]
    return lax.all_gather(block, "row", axis_index_groups=groups)


def along_cuts(block, by):
    count = lax.axis_size("cuts")
    pairs = [(i, i + by) for i in range(count) if 0 <= i + by < count]
    return lax.ppermute(block, "cuts", pairs)


def body(diagonal_blocks, diagonal_inverses, lower_blocks, upper_blocks, injection, orbitals):
    cut = lax.axis_index("cuts")
    place = lax.axis_index("row")
    zero = jnp.zeros((1,), jnp.int32)
    window = lax.dynamic_slice_in_dim(jnp.concatenate([zero, orbitals, zero]), 2 * cut, 4)
    scalars = jnp.concatenate([jnp.stack([place // 4, place % 4]).astype(jnp.int32), window])
    turns = (1, 2, 3)
    after = lax.optimization_barrier
    wide_flops = 2 * 512 * 1024 * 512
    solve_flops = 2 * 2048 * 256 * 128

    *pieces, a_even, c_even, g_pieces, g_odd = call(
        prepare_kernel,
        [shape((64, 1664))] * 4 + [shape((2, 64, 1024))] * 2 + [shape((4, 2, 64, 256))]
        + [shape((2, 64, 1024))],
        0,
        scalars, diagonal_blocks, diagonal_inverses, lower_blocks, upper_blocks, injection,
        hbm=5,
        scratch=[pltpu.VMEM((2, 64, 1024), BF)] * 3
        + [pltpu.VMEM((2, 2, 64, 128), BF)]
        + [pltpu.VMEM((2, 64, 1024), BF)] * 3
        + [pltpu.SemaphoreType.DMA((11,))],
    )
    pieces = [pieces[0]] + [moved_x(pieces[by], by) for by in turns]
    g_rows = gathered_x(g_odd)
    a_next = along_cuts(a_even, -1)
    groups = [[y * 4 + x for y in range(4)] for x in range(4)]
    g_columns = lax.all_to_all(
        g_pieces, "row", 0, 0, axis_index_groups=groups, tiled=True
    )
    a_next, g_columns, *pieces = after((a_next, g_columns, *pieces))
    panel, diagonal, couplings = call(
        assemble_kernel,
        [shape((256, 1152)), shape((256, 512)), shape((2, 2, 64, 1024))],
        0, scalars, *pieces, c_even, a_next,
    )
    g_columns = gathered_x(g_columns)
    near = (g_rows, moved_x(couplings, 1), moved_x(couplings, 3))
    panels, near = ring_gathered_y(scalars, panel, near)
    g_rows = near[0]
    ca_blocks = [couplings, near[1], moved_x(couplings, 2), near[2]]
    taken = [pltpu.VMEM((512, 1024), BF), pltpu.VMEM((256, 1152), BF)]
    (first,) = call(
        odd_kernel, [shape((256, 640))], wide_flops, scalars, g_rows, *panels, scratch=taken
    )
    (second,) = call(
        odd_second_kernel, [shape((304, 512))], wide_flops,
        scalars, g_rows, *panels, scratch=taken,
    )
    firsts = gathered_y(first)
    second, g_columns, *ca_blocks = after((second, g_columns, *ca_blocks))
    seconds = gathered_y(second)
    ship, a_rows = call(
        even_kernel, [shape((288, 512)), shape((512, 1024))], wide_flops,
        scalars, *ca_blocks, *firsts,
    )
    upper_new, source_part, c_rows = call(
        upper_kernel,
        [shape((256, 512)), shape((256, 128), F32), shape((512, 1024))],
        wide_flops,
        scalars, *ca_blocks, *firsts, panel,
    )
    shipped = along_cuts(ship, 1)
    (diagonal_new,) = call(
        diagonal_kernel, [shape((256, 512))], wide_flops,
        scalars, c_rows, *seconds, diagonal, shipped,
    )
    (ship_lower,) = call(
        lower_kernel, [shape((256, 512))], wide_flops, scalars, a_rows, *seconds
    )
    diagonals = [diagonal_new] + [moved_x(diagonal_new, by) for by in turns]
    packed_shapes = [shape((512, 128), F32), shape((512, 128))]
    whole = pltpu.VMEM((1024, 128), F32)
    vector = pltpu.VMEM((1024, 128), BF)
    source, own, send = call(
        source_kernel, [shape((256, 128))] + packed_shapes, solve_flops,
        scalars, g_columns, source_part, shipped, scratch=[whole],
    )
    got = gathered_y(send)[1:]
    lower_new = along_cuts(ship_lower, 1)
    (pair,) = call(pair_kernel, [shape((256, 1024))], 0, scalars, lower_new, upper_new)
    pairs = [pair] + [moved_x(pair, by) for by in turns]
    solved = ()
    for turn in range(REFINE):
        *solved, own, send = call(
            functools.partial(turn_kernel, first=turn == 0),
            [shape((512, 128))] + packed_shapes, 2 * solve_flops,
            scalars, own, *got, *solved, *diagonals, source, g_columns,
            scratch=[vector, whole],
        )
        got = gathered_y(send)[1:]
    (solved,) = call(
        last_kernel, [shape((512, 128))], 0,
        scalars, own, *got, *solved,
    )
    below, above = along_cuts(solved, 1), along_cuts(solved, -1)
    (diagonal_rows,) = call(
        diagonal_rows_kernel, [shape((2, 64, 1024))], 0, scalars, *diagonals
    )
    lower_rows, upper_rows = call(
        coupling_rows_kernel, [shape((2, 64, 1024))] * 2, 0, scalars, *pairs
    )
    below, diagonal_rows, lower_rows, upper_rows = after(
        (below, diagonal_rows, lower_rows, upper_rows)
    )
    ends = call(
        couple_kernel, [shape((64, 128), F32)] * 4, solve_flops // 2,
        scalars, *pairs, source, solved, below, above,
        scratch=[pltpu.VMEM((256, 128), F32), vector],
    )
    ends = [ends[0]] + [moved_x(ends[by], by) for by in turns]
    combined, solved_rows = call(
        spread_kernel, [shape((2, 64, 128), F32)] * 2, 0, scalars, *ends
    )
    return (
        diagonal_rows[None],
        lower_rows[None],
        upper_rows[None],
        combined[None],
        solved_rows[None],
    )


def solution(mesh):
    split = P("cuts", None, "row", None)
    return jax.shard_map(
        body,
        mesh=mesh,
        in_specs=(split, split, split, split, split, P()),
        out_specs=(split,) * 5,
        check_vma=False,
    )
```
